32 devices in a mesh: section: 4 (over y, x), frame: 2 (over core), patch: 4 (over z).
Axes of the slice: x: 2, y: 2, z: 4, core: 2. Of those that a mesh axis runs over, the one named last changes fastest.
Arguments:
- exposure: bfloat16 [2, 2, 896, 4096], P('frame', None, ('section', 'patch')), may hold values from -6 to 6, as said below
- row_prof: bfloat16 [2, 320, 50, 64], P('frame', ('section', 'patch')), may hold values from -0.875 to 0.875
- col_prof: bfloat16 [2, 320, 25, 256], P('frame', ('section', 'patch')), may hold values from -1.25 to 1.25
- row_off: int32 [2, 320], P('frame', ('section', 'patch')), may hold values from 0 to 8, as said below
- col_off: int32 [2, 320], P('frame', ('section', 'patch')), may hold values from 0 to 3840, as said below
- dest: int32 [2, 320], P('frame', ('section', 'patch')), may hold values from 0 to 3, as said below
- fibre_weight: float32 [2, 320, 25], P('frame', ('section', 'patch')), may hold values from 0.2 to 5
Outputs:
- spectra_ext: float32 [2, 320, 50, 25], P('frame', ('section', 'patch'))
- coadd: float32 [320, 50, 25], P(('section', 'patch'))
The draws below stay inside these ranges and needn't reach their ends.
Inputs may be any that keep to these rules, and one draw needn't show every extreme that they name: `exposure`: channel 0 holds pixel values, channel 1 inverse variances between 0.25 and 4. `row_off`: offsets of patches within their band extended by 8 rows on each side. `col_off`: patches of neighbouring fibre blocks share columns. `dest`: of the 20 patches of one band (p // 20 equal) in one frame, each patch index receives 20 // 4 or (23) // 4 of them, so at most 5, and some index exactly 5.
All inputs are finite; a program needn't handle non-finite values.
Results may differ from the reference program's by a relative error of at most 0.0003.
Values may be sent and summed in bfloat16 or wider, within the bound.
No kernel may reach another device: no remote copies, remote signals or barrier semaphores. Data moves between devices by JAX's collectives and lax.ppermute only.
A program may use at most 64 MiB of HBM per device.

```python
import math
import jax
import jax.numpy as jnp
from jax import lax

NCOL = 4096
BAND = 56
HALO = 8
FB = 20
FPB = 25
WPB = 50
PC = 256
ITERS = 6
PR = 64
OWNERS = 16
NROW = 896
FRAMES = 2
NPATCH = 320
CAP = 5
N_PATCH = 4


def draw_exposure(key, part):
    first_key, second_key = jax.random.split(jax.random.fold_in(key, 11))
    shape = (FRAMES, NROW, NCOL)
    values = jnp.clip(jax.random.normal(first_key, shape, jnp.float32), -6.0, 6.0)
    inverse = jnp.exp(jax.random.uniform(second_key, shape, jnp.float32, math.log(0.25), math.log(4.0)))
    return jnp.stack([values, inverse], axis=1).astype(jnp.bfloat16)


def draw_row_off(key, part):
    first_key, second_key = jax.random.split(jax.random.fold_in(key, 23))
    keys = jax.random.split(first_key, FRAMES * OWNERS)
    orders = jax.vmap(lambda one_key: jax.random.permutation(one_key, FB))(keys)
    offset = jax.random.randint(second_key, (FRAMES * OWNERS, 1), 0, HALO + 1)
    return ((orders + offset) % (HALO + 1)).reshape(FRAMES, NPATCH).astype(jnp.int32)


def draw_col_off(key, part):
    spacing = (NCOL - PC) // (FB - 1)
    starts = jnp.arange(FB, dtype=jnp.int32) * spacing
    jitter = jax.random.randint(jax.random.fold_in(key, 37), (FRAMES, OWNERS, FB), -8, 9)
    placed = jnp.clip(starts[None, None, :] + jitter, 0, NCOL - PC)
    return placed.reshape(FRAMES, NPATCH).astype(jnp.int32)


def draw_dest(key, part):
    keys = jax.random.split(jax.random.fold_in(key, 41), FRAMES * OWNERS)
    orders = jax.vmap(lambda one_key: jax.random.permutation(one_key, N_PATCH))(keys)
    wanted = jnp.arange(FB, dtype=jnp.int32) % N_PATCH
    chosen = jnp.take(orders, wanted, axis=1)
    return chosen.reshape(FRAMES, NPATCH).astype(jnp.int32)


def shard_levels(rng, dims, pieces, smallest, top_value):
    loudness = 1.0
    for dim, shards_of in pieces:
        heights = jax.random.uniform(jax.random.fold_in(jax.random.fold_in(rng, 6), dim), (shards_of,), jnp.float32, smallest / len(pieces), top_value / len(pieces))
        loudness = loudness * jnp.repeat(jnp.exp(heights), dims[dim] // shards_of).reshape((-1,) + (1,) * (len(dims) - 1 - dim))
    return loudness


def centred(own_key, dims, scale, most, pieces=(), held_as=jnp.bfloat16):
    array = scale * jax.random.normal(own_key, dims, jnp.float32)
    if pieces:
        array = array * shard_levels(own_key, dims, pieces, -0.22, 0.18)
    return jnp.clip(array, -most, most).astype(held_as)


def setup_inputs(seed: int = 0) -> dict:
    splits = jax.random.split(jax.random.key(seed), 8)
    exposure = draw_exposure(jax.random.fold_in(splits[7], 71), 0)
    row_prof = centred(splits[1], (FRAMES, NPATCH, WPB, PR), WPB ** -0.5, 0.875, ((0, 2), (1, 16)))
    col_prof = centred(splits[2], (FRAMES, NPATCH, FPB, PC), FPB ** -0.5, 1.25, ((0, 2), (1, 16)))
    row_off = draw_row_off(jax.random.fold_in(splits[7], 71), 0)
    col_off = draw_col_off(jax.random.fold_in(splits[7], 71), 0)
    dest = draw_dest(jax.random.fold_in(splits[7], 71), 0)
    fibre_weight = jnp.clip(jnp.exp(math.log(5.0) - 3.218876 * jax.random.uniform(splits[6], (FRAMES, NPATCH, FPB), jnp.float32) ** shard_levels(splits[6], (FRAMES, NPATCH, FPB), ((0, 2), (1, 16)), -0.2, 0.2)), 0.2, 5.0)
    return dict(exposure=exposure, row_prof=row_prof, col_prof=col_prof, row_off=row_off, col_off=col_off, dest=dest, fibre_weight=fibre_weight)


def extract(pixels, row_psf, col_psf):
    highest = lax.Precision.HIGHEST
    values = pixels[..., 0, :, :].astype(jnp.float32)
    inverse = pixels[..., 1, :, :].astype(jnp.float32)
    row_float = row_psf.astype(jnp.float32)
    col_float = col_psf.astype(jnp.float32)

    def normal(spectrum):
        across = jnp.einsum('...wf,...fc->...wc', spectrum, col_float, precision=highest)
        modeled = jnp.einsum('...wr,...wc->...rc', row_float, across, precision=highest)
        folded = jnp.einsum('...wr,...rc->...wc', row_float, inverse * modeled, precision=highest)
        return jnp.einsum('...wc,...fc->...wf', folded, col_float, precision=highest)

    folded = jnp.einsum('...wr,...rc->...wc', row_float, inverse * values, precision=highest)
    rhs_side = jnp.einsum('...wc,...fc->...wf', folded, col_float, precision=highest)
    estimate = jnp.zeros_like(rhs_side)
    residual = rhs_side
    direction = rhs_side
    norm_now = jnp.sum(residual * residual, axis=(-2, -1), keepdims=True)
    for sweep in range(ITERS):
        imaged = normal(direction)
        curvature = jnp.sum(direction * imaged, axis=(-2, -1), keepdims=True)
        step_size = norm_now / curvature
        estimate = estimate + step_size * direction
        residual = residual - step_size * imaged
        norm_next = jnp.sum(residual * residual, axis=(-2, -1), keepdims=True)
        direction = residual + (norm_next / norm_now) * direction
        norm_now = norm_next
    return estimate


def reference(exposure, row_prof, col_prof, row_off, col_off, dest, fibre_weight):
    bands = jnp.pad(exposure, ((0, 0), (0, 0), (HALO, HALO), (0, 0)))
    owners = (jnp.arange(NPATCH) // FB).astype(jnp.int32)
    first_rows = (owners[None, :] * BAND + row_off).astype(jnp.int32)

    def cut_patch(frame_rows, first_row, first_col):
        zero_index = jnp.zeros((), jnp.int32)
        return lax.dynamic_slice(frame_rows, (zero_index, first_row, first_col), (2, PR, PC))

    def per_frame(inputs):
        frame_rows, row_starts, col_starts, row_psf, col_psf = inputs
        blocks = jax.vmap(cut_patch, (None, 0, 0))(frame_rows, row_starts, col_starts)
        return extract(blocks, row_psf, col_psf)

    spectra = lax.map(per_frame, (bands, first_rows, col_off.astype(jnp.int32), row_prof, col_prof))
    grouped = dest.reshape(FRAMES, OWNERS, FB)
    same = grouped[:, :, :, None] == grouped[:, :, None, :]
    earlier = jnp.arange(FB)[None, :] < jnp.arange(FB)[:, None]
    slot_index = jnp.sum((same & earlier[None, None]).astype(jnp.int32), axis=-1).reshape(FRAMES, NPATCH)
    position = (((owners // N_PATCH) * N_PATCH)[None, :] + dest) * (N_PATCH * CAP)
    position = (position + ((owners % N_PATCH) * CAP)[None, :] + slot_index).astype(jnp.int32)
    frame_ids = jnp.broadcast_to(jnp.arange(FRAMES).astype(jnp.int32)[:, None], (FRAMES, NPATCH))
    spectra_ext = jnp.zeros((FRAMES, OWNERS * N_PATCH * CAP, WPB, FPB), jnp.float32)
    spectra_ext = spectra_ext.at[frame_ids, position].set(spectra)
    numerator = jnp.sum(fibre_weight[:, :, None, :] * spectra, axis=0)
    denominator = jnp.sum(fibre_weight, axis=0)
    coadd = numerator / denominator[:, None, :]
    return spectra_ext, coadd
```

```python
import functools

import jax
import jax.numpy as jnp
from jax import lax
from jax.experimental import pallas as pl
from jax.experimental.pallas import tpu as pltpu
from jax.sharding import PartitionSpec as P

HALO = 8
PC = 256
ITERS = 6
PR = 64
LANES = 128
SUB = 8
HALF = LANES // 2
F32 = jnp.float32
BF16 = jnp.bfloat16


def up(count, multiple):
    return -(-count // multiple) * multiple


def dot_nt(lhs, rhs):
    return lax.dot_general(lhs, rhs, (((1,), (1,)), ((), ())), preferred_element_type=F32)


def dot_nn(lhs, rhs):
    return lax.dot_general(lhs, rhs, (((1,), (0,)), ((), ())), preferred_element_type=F32)


def two_parts(value):
    high = value.astype(BF16)
    return high, (value - high.astype(F32)).astype(BF16)


def two_pass(dot, value, weights):
    rows = value.shape[0]
    both = dot(jnp.concatenate(two_parts(value), axis=0), weights)
    return both[:rows] + both[rows:]


def block_tiles(fibres):
    blocks = fibres // SUB
    tiles = [(f, t) for f in range(blocks * SUB) for t in range(f // SUB, blocks)]
    for f in range(blocks * SUB, fibres):
        tiles += [(f, t) for t in range(up(fibres, SUB) // SUB)]
    return tiles


def solve_kernel(
    capacity,
    row_off,
    col_off,
    dest,
    exposure,
    low,
    high,
    row_prof,
    col_prof,
    weight,
    send,
    numer,
    band_w,
    band_wx,
    prof,
    cut_row,
    row_block,
    weights_w,
    weights_wx,
    fibre_rows,
    products,
    fibre_bf,
    matrix,
    tails,
    estimate,
    residual,
    direction,
    imaged,
    partial,
    norm,
    collected,
    counts,
):
    patches, waves, _ = row_prof.shape
    fibres = col_prof.shape[0]
    band = exposure.shape[1]
    columns = exposure.shape[2]
    pairs = patches // 2
    blocks = fibres // SUB
    main = blocks * SUB
    padded_f = up(fibres, SUB)
    padded_p = up(patches, SUB)
    tiles = block_tiles(fibres)
    lane = lax.broadcasted_iota(jnp.int32, (SUB, LANES), 1)

    for start, rows, source in ((0, HALO, low), (HALO, band, exposure), (HALO + band, HALO, high)):
        inverse = source[1].astype(F32)
        scaled = inverse * source[0].astype(F32)
        for piece in range(columns // LANES):
            at = piece * LANES
            band_w[piece, start : start + rows, :] = inverse[:, at : at + LANES]
            band_wx[piece, start : start + rows, :] = scaled[:, at : at + LANES]
    for f in range(fibres):
        both = col_prof[f].astype(F32)
        for half in range(PC // LANES):
            prof[half, f * padded_p : f * padded_p + patches, :] = both[
                :, half * LANES : (half + 1) * LANES
            ]
    cut_row[...] = jnp.zeros_like(cut_row)
    weights_w[...] = jnp.zeros_like(weights_w)
    weights_wx[...] = jnp.zeros_like(weights_wx)
    fibre_rows[...] = jnp.zeros_like(fibre_rows)
    row_block[...] = jnp.zeros_like(row_block)
    partial[...] = jnp.zeros_like(partial)

    def window(source, first_row, base, shift):
        pieces = []
        for piece in range(PC // LANES + 1):
            value = source[base + piece, pl.ds(first_row, PR), :]
            pieces.append(pltpu.roll(value, LANES - shift, 1))
        inside = lax.broadcasted_iota(jnp.int32, (PR, LANES), 1) < LANES - shift
        return [
            jnp.where(inside, pieces[piece], pieces[piece + 1]) for piece in range(PC // LANES)
        ]

    def prepare(pair, carry):
        for half in range(2):
            patch = 2 * pair + half
            first_row = row_off[patch]
            first_col = col_off[patch]
            base = first_col // LANES
            shift = first_col - base * LANES
            rows = slice(half * HALF, half * HALF + PR)
            left = half * 2 * PC
            for piece, value in enumerate(window(band_w, first_row, base, shift)):
                inverse = value.astype(BF16)
                at = left + piece * LANES
                weights_w[rows, at : at + LANES] = inverse
                weights_w[rows, at + PC : at + PC + LANES] = inverse
            for piece, value in enumerate(window(band_wx, first_row, base, shift)):
                upper, lower = two_parts(value)
                at = left + piece * LANES
                weights_wx[rows, at : at + LANES] = upper
                weights_wx[rows, at + PC : at + PC + LANES] = lower
            for piece in range(PC // LANES):
                at = piece * LANES
                fibre_rows[0:fibres, at : at + LANES] = prof[
                    piece, pl.ds(patch, fibres, stride=padded_p), :
                ]
            both = fibre_rows[...].astype(BF16)
            fibre_bf[:, left : left + PC] = both
            fibre_bf[:, left + PC : left + 2 * PC] = both
            for at in range(0, len(tiles), 2):
                value = jnp.concatenate(
                    [
                        fibre_rows[f : f + 1, :] * fibre_rows[t * SUB : (t + 1) * SUB, :]
                        for f, t in tiles[at : at + 2]
                    ],
                    axis=0,
                )
                upper, lower = two_parts(value)
                products[at * SUB : (at + 2) * SUB, left : left + PC] = upper
                products[at * SUB : (at + 2) * SUB, left + PC : left + 2 * PC] = lower
            cut_row[0:waves, 0:PR] = row_prof[patch].astype(F32)
            profile = cut_row[...]
            if half:
                profile = pltpu.roll(profile, HALF, 1)
            row_block[pair, rows, :] = profile.astype(BF16)
        blended = dot_nt(products[...], weights_w[...])
        for index, (f, t) in enumerate(tiles):
            value = blended[index * SUB : (index + 1) * SUB]
            if f < main:
                matrix[pair, f * main + t * SUB : f * main + (t + 1) * SUB, :] = value
                if t > f // SUB:
                    matrix[pair, pl.ds(t * SUB * main + f, SUB, stride=main), :] = value
            else:
                if t < blocks:
                    matrix[pair, f * main + t * SUB : f * main + (t + 1) * SUB, :] = value
                tails[pair, f - main, t * SUB : (t + 1) * SUB, :] = value
        folded = dot_nt(fibre_bf[...], weights_wx[...])
        rhs = two_pass(dot_nt, folded, row_block[pair])
        residual[pair] = rhs
        direction[pair] = rhs
        estimate[pair] = jnp.zeros_like(rhs)
        partial[pl.ds(pair, 1), :] = jnp.sum(rhs * rhs, axis=0, keepdims=True)
        return carry

    lax.fori_loop(0, pairs, prepare, 0)

    lane_all = lax.broadcasted_iota(jnp.int32, partial.shape, 1)
    lower_half = lane_all < HALF

    def patch_sums(value):
        first = jnp.sum(jnp.where(lower_half, value, 0.0), axis=1, keepdims=True)
        second = jnp.sum(jnp.where(lower_half, 0.0, value), axis=1, keepdims=True)
        return jnp.where(lower_half, first, second)

    norm[...] = patch_sums(partial[...])

    def sweep(step, carry):
        for pair in range(pairs):
            now = direction[pair]
            across = two_pass(dot_nn, now, row_block[pair])
            total = jnp.zeros((main, LANES), F32)
            for f in range(fibres):
                total = total + matrix[pair, f * main : (f + 1) * main, :] * across[f : f + 1]
            pieces = [total]
            if fibres > main:
                rest = jnp.zeros((padded_f - main, LANES), F32)
                row = lax.broadcasted_iota(jnp.int32, rest.shape, 0)
                for f in range(main, fibres):
                    one = jnp.sum(tails[pair, f - main] * across, axis=0, keepdims=True)
                    rest = jnp.where(row == f - main, one, rest)
                pieces.append(rest)
            value = two_pass(dot_nt, jnp.concatenate(pieces, axis=0), row_block[pair])
            imaged[pair] = value
            partial[pair : pair + 1, :] = jnp.sum(now * value, axis=0, keepdims=True)
        norm_now = norm[...]
        curvature = patch_sums(partial[...])
        step_size = norm_now / jnp.where(curvature > 0.0, curvature, 1.0)
        for pair in range(pairs):
            size = step_size[pair : pair + 1]
            estimate[pair] = estimate[pair] + size * direction[pair]
            rest = residual[pair] - size * imaged[pair]
            residual[pair] = rest
            partial[pair : pair + 1, :] = jnp.sum(rest * rest, axis=0, keepdims=True)
        norm_next = patch_sums(partial[...])
        ratio = norm_next / jnp.where(norm_now > 0.0, norm_now, 1.0)
        for pair in range(pairs):
            direction[pair] = residual[pair] + ratio[pair : pair + 1] * direction[pair]
        norm[...] = norm_next
        return carry

    lax.fori_loop(0, ITERS, sweep, 0)

    slots = send.shape[0]
    for index in range(slots):
        counts[index] = 0
    if slots * capacity > patches:
        send[...] = jnp.zeros_like(send)
    upper_rows = (fibres + 1) // 2
    slot_rows = send.shape[1] // capacity
    eye = lax.broadcasted_iota(jnp.int32, (padded_f, LANES), 0) == lax.broadcasted_iota(
        jnp.int32, (padded_f, LANES), 1
    )
    lane_f = lax.broadcasted_iota(jnp.int32, (padded_f, LANES), 1)
    for pair in range(pairs):
        spectra = estimate[pair]
        turned = pltpu.roll(spectra, HALF, 1)
        for half in range(2):
            patch = 2 * pair + half
            here = turned if half else spectra
            away = spectra if half else turned
            target = dest[patch]
            slot = counts[target]
            counts[target] = slot + 1
            compact = jnp.where(
                lane_f[:upper_rows] < HALF,
                here[:upper_rows],
                jnp.concatenate(
                    [away[upper_rows:fibres], away[: 2 * upper_rows - fibres]], axis=0
                ),
            )
            first = pl.multiple_of(slot * slot_rows, slot_rows)
            send[target, pl.ds(first, upper_rows), :] = compact
            own = jnp.broadcast_to(weight[patch], (padded_f, fibres))
            own = jnp.sum(jnp.where(eye[:, :fibres], own, 0.0), axis=1, keepdims=True)
            value = jnp.where(lane_f == waves, 1.0, here) * own
            collected[pl.ds(patch, fibres, stride=padded_p), :] = value[:fibres]
    for f in range(fibres):
        numer[f] = collected[f * padded_p : f * padded_p + patches, : waves + 1]


def finish_kernel(capacity, received, numer, others, spectra_ext, coadd):
    fibres, patches, _ = coadd.shape
    waves = coadd.shape[2]
    upper_rows = (fibres + 1) // 2
    group = received.shape[0]
    slot_rows = received.shape[1] // capacity
    for source in range(group):
        for slot in range(capacity):
            value = received[source, slot * slot_rows : (slot + 1) * slot_rows, :]
            turned = pltpu.roll(value, HALF, 1)
            entry = source * capacity + slot
            for f in range(fibres):
                row = value[f : f + 1] if f < upper_rows else turned[f - upper_rows : f - upper_rows + 1]
                spectra_ext[entry, f] = row[:, :waves]
    for f in range(fibres):
        total = numer[f]
        for index in range(others.shape[0]):
            total = total + others[index, f]
        coadd[f] = total[:, :waves] / total[:, waves : waves + 1]


def vmem(count=1):
    return [pl.BlockSpec(memory_space=pltpu.VMEM)] * count


def solve(exposure, low, high, row_prof, col_prof, row_off, col_off, dest, weight, group):
    patches, waves, _ = row_prof.shape
    fibres = col_prof.shape[0]
    band = exposure.shape[1]
    columns = exposure.shape[2]
    capacity = (patches + group - 1) // group
    pairs = patches // 2
    main = fibres // SUB * SUB
    padded_f = up(fibres, SUB)
    padded_p = up(patches, SUB)
    slot_rows = up((fibres + 1) // 2, SUB)
    rows = SUB * len(block_tiles(fibres))
    wide = 4 * PC
    vectors = pltpu.VMEM((pairs, padded_f, LANES), F32)
    sums = pltpu.VMEM((up(pairs, SUB), LANES), F32)
    return pl.pallas_call(
        functools.partial(solve_kernel, capacity),
        out_shape=(
            jax.ShapeDtypeStruct((group, capacity * slot_rows, LANES), F32),
            jax.ShapeDtypeStruct((fibres, patches, waves + 1), F32),
        ),
        in_specs=[pl.BlockSpec(memory_space=pltpu.SMEM)] * 3 + vmem(6),
        out_specs=tuple(vmem(2)),
        scratch_shapes=[
            pltpu.VMEM((columns // LANES + 1, band + 2 * HALO, LANES), F32),
            pltpu.VMEM((columns // LANES + 1, band + 2 * HALO, LANES), F32),
            pltpu.VMEM((PC // LANES, fibres * padded_p, LANES), F32),
            pltpu.VMEM((HALF, LANES), F32),
            pltpu.VMEM((pairs, LANES, LANES), BF16),
            pltpu.VMEM((LANES, wide), BF16),
            pltpu.VMEM((LANES, wide), BF16),
            pltpu.VMEM((padded_f, PC), F32),
            pltpu.VMEM((rows, wide), BF16),
            pltpu.VMEM((padded_f, wide), BF16),
            pltpu.VMEM((pairs, fibres * main, LANES), F32),
            pltpu.VMEM((pairs, max(fibres - main, 1), padded_f, LANES), F32),
            vectors,
            vectors,
            vectors,
            vectors,
            sums,
            sums,
            pltpu.VMEM((fibres * padded_p, LANES), F32),
            pltpu.SMEM((group,), jnp.int32),
        ],
        compiler_params=pltpu.CompilerParams(vmem_limit_bytes=40 * 1024 * 1024),
    )(row_off, col_off, dest, exposure, low, high, row_prof, col_prof, weight)


def finish(received, numer, others, capacity):
    fibres, patches, wide = numer.shape
    entries = received.shape[0] * capacity
    return pl.pallas_call(
        functools.partial(finish_kernel, capacity),
        out_shape=(
            jax.ShapeDtypeStruct((entries, fibres, 1, wide - 1), F32),
            jax.ShapeDtypeStruct((fibres, patches, wide - 1), F32),
        ),
        in_specs=vmem(3),
        out_specs=tuple(vmem(2)),
        compiler_params=pltpu.CompilerParams(vmem_limit_bytes=16 * 1024 * 1024),
    )(received, numer, others)


def neighbours(block):
    axes = ("section", "patch")
    count = lax.axis_size(axes)
    forward = [(i, i + 1) for i in range(count - 1)]
    backward = [(target, source) for source, target in forward]
    low = lax.ppermute(block[:, -HALO:], axes, forward)
    high = lax.ppermute(block[:, :HALO], axes, backward)
    return low, high


def local(exposure, row_prof, col_prof, row_off, col_off, dest, fibre_weight):
    group = lax.axis_size("patch")
    frames = lax.axis_size("frame")
    patches = dest.shape[1]
    capacity = (patches + group - 1) // group
    exposure = exposure[0]
    low, high = neighbours(exposure)
    send, numer = solve(
        exposure,
        low,
        high,
        row_prof[0],
        col_prof[0].transpose(1, 0, 2),
        row_off[0],
        col_off[0],
        dest[0],
        fibre_weight[0][:, None, :],
        group,
    )
    received = lax.all_to_all(send, "patch", split_axis=0, concat_axis=0, tiled=True)
    others = jnp.stack(
        [
            lax.ppermute(numer, "frame", [(i, (i + hop) % frames) for i in range(frames)])
            for hop in range(1, frames)
        ]
    )
    spectra_ext, coadd = finish(received, numer, others, capacity)
    return spectra_ext.transpose(2, 0, 3, 1), coadd.transpose(1, 2, 0)


def solution(mesh):
    in_specs = (
        P("frame", None, ("section", "patch"), None),
        P("frame", ("section", "patch"), None, None),
        P("frame", ("section", "patch"), None, None),
        P("frame", ("section", "patch")),
        P("frame", ("section", "patch")),
        P("frame", ("section", "patch")),
        P("frame", ("section", "patch"), None),
    )
    out_specs = (P("frame", ("section", "patch"), None, None), P(("section", "patch"), None, None))
    return jax.shard_map(local, mesh=mesh, in_specs=in_specs, out_specs=out_specs, check_vma=False)
```

```python
import functools

import jax
import jax.numpy as jnp
from jax import lax
from jax.experimental import pallas as pl
from jax.experimental.pallas import tpu as pltpu
from jax.sharding import PartitionSpec as P

HALO = 8
PC = 256
ITERS = 6
PR = 64
LANES = 128
SUB = 8
HALF = LANES // 2
F32 = jnp.float32
BF16 = jnp.bfloat16


def up(count, multiple):
    return -(-count // multiple) * multiple


def dot_nt(lhs, rhs):
    return lax.dot_general(lhs, rhs, (((1,), (1,)), ((), ())), preferred_element_type=F32)


def dot_nn(lhs, rhs):
    return lax.dot_general(lhs, rhs, (((1,), (0,)), ((), ())), preferred_element_type=F32)


def two_parts(value):
    high = value.astype(BF16)
    return high, (value - high.astype(F32)).astype(BF16)


def two_pass(dot, value, weights):
    rows = value.shape[0]
    both = dot(jnp.concatenate(two_parts(value), axis=0), weights)
    return both[:rows] + both[rows:]


def block_tiles(fibres):
    blocks = fibres // SUB
    tiles = [(f, t) for f in range(blocks * SUB) for t in range(f // SUB, blocks)]
    for f in range(blocks * SUB, fibres):
        tiles += [(f, t) for t in range(up(fibres, SUB) // SUB)]
    return tiles


def split_lanes(value):
    return [value[:, at : at + LANES] for at in range(0, value.shape[1], LANES)]


def shifted(pieces, shift):
    rows = pieces[0].shape[0]
    turned = [pltpu.roll(piece, LANES - shift, 1) for piece in pieces]
    inside = lax.broadcasted_iota(jnp.int32, (rows, LANES), 1) < LANES - shift
    return [jnp.where(inside, turned[i], turned[i + 1]) for i in range(len(pieces) - 1)]


def prepare_kernel(
    row_off,
    col_off,
    exposure,
    row_prof,
    col_prof,
    products,
    weights_w,
    upper_wx,
    lower_wx,
    fibre,
    row_block,
    band_w,
    band_wx,
    prof,
    fibre_rows,
    cut_row,
):
    patches, waves, _ = row_prof.shape
    fibres = col_prof.shape[0]
    columns = exposure.shape[2]
    padded_p = up(patches, SUB)
    tiles = block_tiles(fibres)
    inverse = exposure[1].astype(F32)
    scaled = inverse * exposure[0].astype(F32)
    for piece, value in enumerate(split_lanes(inverse)):
        band_w[piece] = value
    for piece, value in enumerate(split_lanes(scaled)):
        band_wx[piece] = value
    for f in range(fibres):
        for piece, value in enumerate(split_lanes(col_prof[f].astype(F32))):
            prof[piece, f * padded_p : f * padded_p + patches, :] = value
    cut_row[...] = jnp.zeros_like(cut_row)
    fibre_rows[...] = jnp.zeros_like(fibre_rows)
    halo = jnp.zeros((HALO, LANES), F32)
    lower_half = lax.broadcasted_iota(jnp.int32, (HALF, LANES), 1) < HALF

    def prepare(patch, carry):
        first_row = row_off[patch]
        first_col = col_off[patch]
        base = first_col // LANES
        shift = first_col - base * LANES
        count = PC // LANES
        window = shifted([band_w[base + piece] for piece in range(count + 1)], shift)
        for piece, value in enumerate(window):
            lanes = slice(piece * LANES, (piece + 1) * LANES)
            weights_w[patch, :, lanes] = jnp.concatenate([halo, value], axis=0).astype(BF16)
        window = shifted([band_wx[base + piece] for piece in range(count + 1)], shift)
        for piece, value in enumerate(window):
            lanes = slice(piece * LANES, (piece + 1) * LANES)
            upper, lower = two_parts(jnp.concatenate([halo, value], axis=0))
            upper_wx[patch, :, lanes] = upper
            lower_wx[patch, :, lanes] = lower
        for piece in range(count):
            lanes = slice(piece * LANES, (piece + 1) * LANES)
            fibre_rows[0:fibres, lanes] = prof[piece, pl.ds(patch, fibres, stride=padded_p), :]
        fibre[patch] = fibre_rows[...].astype(BF16)
        for at in range(0, len(tiles), 2):
            value = jnp.concatenate(
                [
                    fibre_rows[f : f + 1, :] * fibre_rows[t * SUB : (t + 1) * SUB, :]
                    for f, t in tiles[at : at + 2]
                ],
                axis=0,
            )
            upper, lower = two_parts(value)
            products[patch, at * SUB : (at + 2) * SUB, 0:PC] = upper
            products[patch, at * SUB : (at + 2) * SUB, PC : 2 * PC] = lower
        cut_row[0:waves, 0:PR] = row_prof[patch].astype(F32)
        profile = cut_row[...]
        turned = pltpu.roll(profile + pltpu.roll(profile, HALF, 1), first_row, 1)
        keep = lower_half == (lax.rem(patch, 2) == 0)
        row_block[patch] = jnp.where(keep, turned, 0.0).astype(BF16)
        return carry

    lax.fori_loop(0, patches, prepare, 0)


def solve_kernel(
    capacity,
    waves,
    row_off,
    col_off,
    dest,
    halo_one,
    halo_two,
    products,
    weights_w,
    upper_wx,
    lower_wx,
    fibre,
    blocks_in,
    weight,
    send,
    numer,
    halo_w,
    halo_wx,
    row_block,
    matrix,
    tails,
    estimate,
    residual,
    direction,
    imaged,
    partial,
    norm,
    collected,
    counts,
):
    patches = weight.shape[0]
    fibres = weight.shape[2]
    pairs = patches // 2
    blocks = fibres // SUB
    main = blocks * SUB
    padded_f = up(fibres, SUB)
    padded_p = up(patches, SUB)
    tiles = block_tiles(fibres)
    rank = lax.axis_index("section") * lax.axis_size("patch") + lax.axis_index("patch")
    odd = lax.rem(rank, 2) == 1

    for slot, source in enumerate((halo_one, halo_two)):
        rows = slice(slot * HALO, (slot + 1) * HALO)
        inverse = source[1].astype(F32)
        for piece, value in enumerate(split_lanes(inverse)):
            halo_w[piece, rows, :] = value
        for piece, value in enumerate(split_lanes(inverse * source[0].astype(F32))):
            halo_wx[piece, rows, :] = value
    partial[...] = jnp.zeros_like(partial)
    halo_row = lax.broadcasted_iota(jnp.int32, (HALO, LANES), 0)
    empty = jnp.zeros((PR, PC), BF16)

    def with_halo(own, edge):
        top = jnp.concatenate([edge, own[: 2 * HALO].astype(F32)[HALO:]], axis=0)
        return jnp.concatenate([top.astype(BF16), own[2 * HALO :]], axis=0)

    def assemble(pair, carry):
        inverse, upper, lower = [], [], []
        for half in range(2):
            patch = 2 * pair + half
            first_row = row_off[patch]
            first_col = col_off[patch]
            base = first_col // LANES
            shift = first_col - base * LANES
            take_one = (halo_row >= first_row) == odd
            edges = []
            for source in (halo_w, halo_wx):
                pieces = [
                    jnp.where(
                        take_one,
                        source[base + piece, 0:HALO, :],
                        source[base + piece, HALO : 2 * HALO, :],
                    )
                    for piece in range(PC // LANES + 1)
                ]
                edges.append(jnp.concatenate(shifted(pieces, shift), axis=1))
            inverse.append(with_halo(weights_w[patch], edges[0]))
            above = edges[1].astype(BF16).astype(F32)
            upper.append(with_halo(upper_wx[patch], above))
            lower.append(with_halo(lower_wx[patch], edges[1] - above))
        one, two = 2 * pair, 2 * pair + 1

        def diagonal(first, second):
            return jnp.concatenate(
                [
                    jnp.concatenate(first + [empty] * len(second), axis=1),
                    jnp.concatenate([empty] * len(first) + second, axis=1),
                ],
                axis=0,
            )

        blended = dot_nt(
            jnp.concatenate([products[one], products[two]], axis=1),
            diagonal([inverse[0]] * 2, [inverse[1]] * 2),
        )
        for index, (f, t) in enumerate(tiles):
            value = blended[index * SUB : (index + 1) * SUB]
            if f < main:
                matrix[pair, f * main + t * SUB : f * main + (t + 1) * SUB, :] = value
                if t > f // SUB:
                    matrix[pair, pl.ds(t * SUB * main + f, SUB, stride=main), :] = value
            else:
                if t < blocks:
                    matrix[pair, f * main + t * SUB : f * main + (t + 1) * SUB, :] = value
                tails[pair, f - main, t * SUB : (t + 1) * SUB, :] = value
        folded = dot_nt(
            jnp.concatenate([fibre[one], fibre[one], fibre[two], fibre[two]], axis=1),
            diagonal([upper[0], lower[0]], [upper[1], lower[1]]),
        )
        row_block[pair] = jnp.concatenate([blocks_in[one], blocks_in[two]], axis=0)
        rhs = two_pass(dot_nt, folded, row_block[pair])
        residual[pair] = rhs
        direction[pair] = rhs
        estimate[pair] = jnp.zeros_like(rhs)
        partial[pl.ds(pair, 1), :] = jnp.sum(rhs * rhs, axis=0, keepdims=True)
        return carry

    lax.fori_loop(0, pairs, assemble, 0)

    lane_all = lax.broadcasted_iota(jnp.int32, partial.shape, 1)
    lower_half = lane_all < HALF

    def patch_sums(value):
        first = jnp.sum(jnp.where(lower_half, value, 0.0), axis=1, keepdims=True)
        second = jnp.sum(jnp.where(lower_half, 0.0, value), axis=1, keepdims=True)
        return jnp.where(lower_half, first, second)

    norm[...] = patch_sums(partial[...])

    def sweep(step, carry):
        for pair in range(pairs):
            now = direction[pair]
            across = two_pass(dot_nn, now, row_block[pair])
            total = jnp.zeros((main, LANES), F32)
            for f in range(fibres):
                total = total + matrix[pair, f * main : (f + 1) * main, :] * across[f : f + 1]
            pieces = [total]
            if fibres > main:
                rest = jnp.zeros((padded_f - main, LANES), F32)
                row = lax.broadcasted_iota(jnp.int32, rest.shape, 0)
                for f in range(main, fibres):
                    one = jnp.sum(tails[pair, f - main] * across, axis=0, keepdims=True)
                    rest = jnp.where(row == f - main, one, rest)
                pieces.append(rest)
            value = two_pass(dot_nt, jnp.concatenate(pieces, axis=0), row_block[pair])
            imaged[pair] = value
            partial[pair : pair + 1, :] = jnp.sum(now * value, axis=0, keepdims=True)
        norm_now = norm[...]
        curvature = patch_sums(partial[...])
        step_size = norm_now / jnp.where(curvature > 0.0, curvature, 1.0)
        for pair in range(pairs):
            size = step_size[pair : pair + 1]
            estimate[pair] = estimate[pair] + size * direction[pair]
            rest = residual[pair] - size * imaged[pair]
            residual[pair] = rest
            partial[pair : pair + 1, :] = jnp.sum(rest * rest, axis=0, keepdims=True)
        norm_next = patch_sums(partial[...])
        ratio = norm_next / jnp.where(norm_now > 0.0, norm_now, 1.0)
        for pair in range(pairs):
            direction[pair] = residual[pair] + ratio[pair : pair + 1] * direction[pair]
        norm[...] = norm_next
        return carry

    lax.fori_loop(0, ITERS, sweep, 0)

    slots = send.shape[0]
    for index in range(slots):
        counts[index] = 0
    if slots * capacity > patches:
        send[...] = jnp.zeros_like(send)
    upper_rows = (fibres + 1) // 2
    slot_rows = upper_rows
    eye = lax.broadcasted_iota(jnp.int32, (padded_f, LANES), 0) == lax.broadcasted_iota(
        jnp.int32, (padded_f, LANES), 1
    )
    lane_f = lax.broadcasted_iota(jnp.int32, (padded_f, LANES), 1)
    for pair in range(pairs):
        spectra = estimate[pair]
        turned = pltpu.roll(spectra, HALF, 1)
        for half in range(2):
            patch = 2 * pair + half
            here = turned if half else spectra
            away = spectra if half else turned
            target = dest[patch]
            slot = counts[target]
            counts[target] = slot + 1
            compact = jnp.where(
                lane_f[:upper_rows] < HALF,
                here[:upper_rows],
                jnp.concatenate(
                    [away[upper_rows:fibres], away[: 2 * upper_rows - fibres]], axis=0
                ),
            )
            send[target, pl.ds(slot * slot_rows, slot_rows), :] = compact
            own = jnp.broadcast_to(weight[patch], (padded_f, fibres))
            own = jnp.sum(jnp.where(eye[:, :fibres], own, 0.0), axis=1, keepdims=True)
            value = jnp.where(lane_f == waves, 1.0, here) * own
            collected[pl.ds(patch, fibres, stride=padded_p), :] = value[:fibres]
    for f in range(fibres):
        numer[f] = collected[f * padded_p : f * padded_p + patches, : waves + 1]


def finish_kernel(capacity, received, numer, others, spectra_ext, coadd):
    fibres, patches, _ = coadd.shape
    waves = coadd.shape[2]
    upper_rows = (fibres + 1) // 2
    group = received.shape[0]
    slot_rows = upper_rows
    for source in range(group):
        for slot in range(capacity):
            value = received[source, slot * slot_rows : (slot + 1) * slot_rows, :]
            turned = pltpu.roll(value, HALF, 1)
            entry = source * capacity + slot
            for f in range(fibres):
                row = value[f : f + 1] if f < upper_rows else turned[f - upper_rows : f - upper_rows + 1]
                spectra_ext[entry, f] = row[:, :waves]
    for f in range(fibres):
        total = numer[f]
        for index in range(others.shape[0]):
            total = total + others[index, f]
        coadd[f] = total[:, :waves] / total[:, waves : waves + 1]


def vmem(count=1):
    return [pl.BlockSpec(memory_space=pltpu.VMEM)] * count


def prepare(exposure, row_prof, col_prof, row_off, col_off):
    patches = row_prof.shape[0]
    fibres = col_prof.shape[0]
    _, band, columns = exposure.shape
    padded_f = up(fibres, SUB)
    padded_p = up(patches, SUB)
    rows = SUB * len(block_tiles(fibres))

    def made(*shape):
        return jax.ShapeDtypeStruct((patches,) + shape, BF16)

    return pl.pallas_call(
        prepare_kernel,
        out_shape=(
            made(rows, 2 * PC),
            made(PR, PC),
            made(PR, PC),
            made(PR, PC),
            made(padded_f, PC),
            made(HALF, LANES),
        ),
        in_specs=[pl.BlockSpec(memory_space=pltpu.SMEM)] * 2 + vmem(3),
        out_specs=tuple(vmem(6)),
        scratch_shapes=[
            pltpu.VMEM((columns // LANES + 1, band, LANES), F32),
            pltpu.VMEM((columns // LANES + 1, band, LANES), F32),
            pltpu.VMEM((PC // LANES, fibres * padded_p, LANES), F32),
            pltpu.VMEM((padded_f, PC), F32),
            pltpu.VMEM((HALF, LANES), F32),
        ],
        cost_estimate=pl.CostEstimate(
            flops=patches * rows * PC * 8, bytes_accessed=16 * 1024 * 1024, transcendentals=0
        ),
        compiler_params=pltpu.CompilerParams(vmem_limit_bytes=24 * 1024 * 1024),
    )(row_off, col_off, exposure, row_prof, col_prof)


def solve(halos, prepared, waves, row_off, col_off, dest, weight, group):
    patches, _, fibres = weight.shape
    columns = halos[0].shape[2]
    capacity = (patches + group - 1) // group
    pairs = patches // 2
    main = fibres // SUB * SUB
    padded_f = up(fibres, SUB)
    padded_p = up(patches, SUB)
    vectors = pltpu.VMEM((pairs, padded_f, LANES), F32)
    sums = pltpu.VMEM((up(pairs, SUB), LANES), F32)
    return pl.pallas_call(
        functools.partial(solve_kernel, capacity, waves),
        out_shape=(
            jax.ShapeDtypeStruct((group, up(capacity * ((fibres + 1) // 2), SUB), LANES), F32),
            jax.ShapeDtypeStruct((fibres, patches, waves + 1), F32),
        ),
        in_specs=[pl.BlockSpec(memory_space=pltpu.SMEM)] * 3 + vmem(9),
        out_specs=tuple(vmem(2)),
        scratch_shapes=[
            pltpu.VMEM((columns // LANES + 1, 2 * HALO, LANES), F32),
            pltpu.VMEM((columns // LANES + 1, 2 * HALO, LANES), F32),
            pltpu.VMEM((pairs, LANES, LANES), BF16),
            pltpu.VMEM((pairs, fibres * main, LANES), F32),
            pltpu.VMEM((pairs, max(fibres - main, 1), padded_f, LANES), F32),
            vectors,
            vectors,
            vectors,
            vectors,
            sums,
            sums,
            pltpu.VMEM((fibres * padded_p, LANES), F32),
            pltpu.SMEM((group,), jnp.int32),
        ],
        compiler_params=pltpu.CompilerParams(vmem_limit_bytes=24 * 1024 * 1024),
    )(row_off, col_off, dest, *halos, *prepared, weight)


def finish(received, numer, others, capacity):
    fibres, patches, wide = numer.shape
    entries = received.shape[0] * capacity
    return pl.pallas_call(
        functools.partial(finish_kernel, capacity),
        out_shape=(
            jax.ShapeDtypeStruct((entries, fibres, 1, wide - 1), F32),
            jax.ShapeDtypeStruct((fibres, patches, wide - 1), F32),
        ),
        in_specs=vmem(3),
        out_specs=tuple(vmem(2)),
        compiler_params=pltpu.CompilerParams(vmem_limit_bytes=16 * 1024 * 1024),
    )(received, numer, others)


def neighbours(block):
    axes = ("section", "patch")
    count = lax.axis_size(axes)
    rank = lax.axis_index(axes)
    even = lax.rem(rank, 2) == 0
    top = block[:, :HALO]
    bottom = block[:, -HALO:]
    received = []
    for first, value in ((1, jnp.where(even, top, bottom)), (0, jnp.where(even, bottom, top))):
        pairs = [(i, i + 1) for i in range(first, count - 1, 2)]
        received.append(lax.ppermute(value, axes, pairs + [(b, a) for a, b in pairs]))
    return received[1], received[0]


def local(exposure, row_prof, col_prof, row_off, col_off, dest, fibre_weight):
    group = lax.axis_size("patch")
    frames = lax.axis_size("frame")
    patches = dest.shape[1]
    waves = row_prof.shape[2]
    capacity = (patches + group - 1) // group
    halos = neighbours(exposure[0])
    prepared = prepare(
        exposure[0], row_prof[0], col_prof[0].transpose(1, 0, 2), row_off[0], col_off[0]
    )
    send, numer = solve(
        halos,
        prepared,
        waves,
        row_off[0],
        col_off[0],
        dest[0],
        fibre_weight[0][:, None, :],
        group,
    )
    received = lax.all_to_all(send, "patch", split_axis=0, concat_axis=0, tiled=True)
    others = jnp.stack(
        [
            lax.ppermute(numer, "frame", [(i, (i + hop) % frames) for i in range(frames)])
            for hop in range(1, frames)
        ]
    )
    spectra_ext, coadd = finish(received, numer, others, capacity)
    return spectra_ext.transpose(2, 0, 3, 1), coadd.transpose(1, 2, 0)


def solution(mesh):
    in_specs = (
        P("frame", None, ("section", "patch"), None),
        P("frame", ("section", "patch"), None, None),
        P("frame", ("section", "patch"), None, None),
        P("frame", ("section", "patch")),
        P("frame", ("section", "patch")),
        P("frame", ("section", "patch")),
        P("frame", ("section", "patch"), None),
    )
    out_specs = (P("frame", ("section", "patch"), None, None), P(("section", "patch"), None, None))
    return jax.shard_map(local, mesh=mesh, in_specs=in_specs, out_specs=out_specs, check_vma=False)
```

```python
import functools

import jax
import jax.numpy as jnp
from jax import lax
from jax.experimental import pallas as pl
from jax.experimental.pallas import tpu as pltpu
from jax.sharding import PartitionSpec as P

HALO = 8
PC = 256
ITERS = 6
PR = 64
LANES = 128
SUB = 8
HALF = LANES // 2
EDGE_FLOPS = 1 << 34
EDGE_BYTES = 1 << 27
F32 = jnp.float32
BF16 = jnp.bfloat16


def up(count, multiple):
    return -(-count // multiple) * multiple


def dot_nt(lhs, rhs):
    return lax.dot_general(lhs, rhs, (((1,), (1,)), ((), ())), preferred_element_type=F32)


def dot_nn(lhs, rhs):
    return lax.dot_general(lhs, rhs, (((1,), (0,)), ((), ())), preferred_element_type=F32)


def two_parts(value):
    high = value.astype(BF16)
    return high, (value - high.astype(F32)).astype(BF16)


def two_pass(dot, value, weights):
    rows = value.shape[0]
    both = dot(jnp.concatenate(two_parts(value), axis=0), weights)
    return both[:rows] + both[rows:]


def block_tiles(fibres):
    blocks = fibres // SUB
    tiles = [(f, t) for f in range(blocks * SUB) for t in range(f // SUB, blocks)]
    for f in range(blocks * SUB, fibres):
        tiles += [(f, t) for t in range(up(fibres, SUB) // SUB)]
    return tiles


def split_lanes(value):
    return [value[:, at : at + LANES] for at in range(0, value.shape[1], LANES)]


def shifted(pieces, shift):
    rows = pieces[0].shape[0]
    turned = [pltpu.roll(piece, LANES - shift, 1) for piece in pieces]
    inside = lax.broadcasted_iota(jnp.int32, (rows, LANES), 1) < LANES - shift
    return [jnp.where(inside, turned[i], turned[i + 1]) for i in range(len(pieces) - 1)]


def start_copies(sources, targets, arrived):
    copies = [
        pltpu.make_async_copy(source, target, arrived.at[index])
        for index, (source, target) in enumerate(zip(sources, targets))
    ]
    for copy in copies:
        copy.start()
    return copies


def prepare_kernel(
    row_off_in,
    col_off_in,
    exposure_in,
    row_prof_in,
    col_prof_in,
    products,
    weights_w,
    upper_wx,
    lower_wx,
    fibre,
    row_block,
    row_off,
    col_off,
    exposure,
    row_prof,
    col_prof,
    band_w,
    band_wx,
    prof,
    fibre_rows,
    cut_row,
    arrived,
):
    copies = start_copies(
        (exposure_in, col_prof_in, row_prof_in, row_off_in, col_off_in),
        (exposure, col_prof, row_prof, row_off, col_off),
        arrived,
    )
    patches, waves, _ = row_prof.shape
    fibres = col_prof.shape[0]
    columns = exposure.shape[2]
    padded_p = up(patches, SUB)
    tiles = block_tiles(fibres)
    copies[0].wait()
    inverse = exposure[1].astype(F32)
    scaled = inverse * exposure[0].astype(F32)
    for piece, value in enumerate(split_lanes(inverse)):
        band_w[piece] = value
    for piece, value in enumerate(split_lanes(scaled)):
        band_wx[piece] = value
    copies[1].wait()
    for f in range(fibres):
        for piece, value in enumerate(split_lanes(col_prof[f].astype(F32))):
            prof[piece, f * padded_p : f * padded_p + patches, :] = value
    for copy in copies[2:]:
        copy.wait()
    cut_row[...] = jnp.zeros_like(cut_row)
    fibre_rows[...] = jnp.zeros_like(fibre_rows)
    halo = jnp.zeros((HALO, LANES), F32)
    lower_half = lax.broadcasted_iota(jnp.int32, (HALF, LANES), 1) < HALF

    def prepare(patch, carry):
        first_row = row_off[patch]
        first_col = col_off[patch]
        base = first_col // LANES
        shift = first_col - base * LANES
        count = PC // LANES
        window = shifted([band_w[base + piece] for piece in range(count + 1)], shift)
        for piece, value in enumerate(window):
            lanes = slice(piece * LANES, (piece + 1) * LANES)
            weights_w[patch, :, lanes] = jnp.concatenate([halo, value], axis=0).astype(BF16)
        window = shifted([band_wx[base + piece] for piece in range(count + 1)], shift)
        for piece, value in enumerate(window):
            lanes = slice(piece * LANES, (piece + 1) * LANES)
            upper, lower = two_parts(jnp.concatenate([halo, value], axis=0))
            upper_wx[patch, :, lanes] = upper
            lower_wx[patch, :, lanes] = lower
        for piece in range(count):
            lanes = slice(piece * LANES, (piece + 1) * LANES)
            fibre_rows[0:fibres, lanes] = prof[piece, pl.ds(patch, fibres, stride=padded_p), :]
        fibre[patch] = fibre_rows[...].astype(BF16)
        for at in range(0, len(tiles), 2):
            value = jnp.concatenate(
                [
                    fibre_rows[f : f + 1, :] * fibre_rows[t * SUB : (t + 1) * SUB, :]
                    for f, t in tiles[at : at + 2]
                ],
                axis=0,
            )
            upper, lower = two_parts(value)
            products[patch, at * SUB : (at + 2) * SUB, 0:PC] = upper
            products[patch, at * SUB : (at + 2) * SUB, PC : 2 * PC] = lower
        cut_row[0:waves, 0:PR] = row_prof[patch].astype(F32)
        profile = cut_row[...]
        turned = pltpu.roll(profile + pltpu.roll(profile, HALF, 1), first_row, 1)
        keep = lower_half == (lax.rem(patch, 2) == 0)
        row_block[patch] = jnp.where(keep, turned, 0.0).astype(BF16)
        return carry

    lax.fori_loop(0, patches, prepare, 0)


def solve_kernel(
    capacity,
    waves,
    row_off_in,
    col_off_in,
    dest_in,
    weight_in,
    halo_one,
    halo_two,
    products,
    weights_w,
    upper_wx,
    lower_wx,
    fibre,
    blocks_in,
    send,
    numer,
    row_off,
    col_off,
    dest,
    weight,
    halo_w,
    halo_wx,
    top_w,
    top_upper,
    top_lower,
    row_block,
    matrix,
    tails,
    estimate,
    residual,
    direction,
    imaged,
    across,
    partial,
    norm,
    collected,
    counts,
    arrived,
):
    copies = start_copies(
        (row_off_in, col_off_in, dest_in, weight_in), (row_off, col_off, dest, weight), arrived
    )
    patches = weight.shape[0]
    fibres = weight.shape[2]
    pairs = patches // 2
    blocks = fibres // SUB
    main = blocks * SUB
    padded_f = up(fibres, SUB)
    padded_p = up(patches, SUB)
    tiles = block_tiles(fibres)
    rank = lax.axis_index("section") * lax.axis_size("patch") + lax.axis_index("patch")
    odd = lax.rem(rank, 2) == 1

    for slot, source in enumerate((halo_one, halo_two)):
        rows = slice(slot * HALO, (slot + 1) * HALO)
        inverse = source[1].astype(F32)
        for piece, value in enumerate(split_lanes(inverse)):
            halo_w[piece, rows, :] = value
        for piece, value in enumerate(split_lanes(inverse * source[0].astype(F32))):
            halo_wx[piece, rows, :] = value
    partial[...] = jnp.zeros_like(partial)
    for pair in range(pairs):
        for half in range(2):
            row_block[pair, half * HALF : (half + 1) * HALF, :] = blocks_in[2 * pair + half]
    halo_row = lax.broadcasted_iota(jnp.int32, (HALO, LANES), 0)
    empty = jnp.zeros((PR, PC), BF16)
    copies[0].wait()
    copies[1].wait()

    def beside_own(edge, own):
        return jnp.concatenate([edge, own.astype(F32)[HALO:]], axis=0).astype(BF16)

    for patch in range(patches):
        first_row = row_off[patch]
        first_col = col_off[patch]
        base = first_col // LANES
        shift = first_col - base * LANES
        take_one = (halo_row >= first_row) == odd
        edges = []
        for source in (halo_w, halo_wx):
            pieces = [
                jnp.where(
                    take_one,
                    source[base + piece, 0:HALO, :],
                    source[base + piece, HALO : 2 * HALO, :],
                )
                for piece in range(PC // LANES + 1)
            ]
            edges.append(jnp.concatenate(shifted(pieces, shift), axis=1))
        above = edges[1].astype(BF16).astype(F32)
        top_w[patch] = beside_own(edges[0], weights_w[patch, : 2 * HALO, :])
        top_upper[patch] = beside_own(above, upper_wx[patch, : 2 * HALO, :])
        top_lower[patch] = beside_own(edges[1] - above, lower_wx[patch, : 2 * HALO, :])

    def whole(top, own, patch):
        return jnp.concatenate([top[patch], own[patch, 2 * HALO :, :]], axis=0)

    def diagonal(first, second):
        return jnp.concatenate(
            [
                jnp.concatenate(first + [empty] * len(second), axis=1),
                jnp.concatenate([empty] * len(first) + second, axis=1),
            ],
            axis=0,
        )

    for pair in range(pairs):
        one, two = 2 * pair, 2 * pair + 1
        folded = dot_nt(
            jnp.concatenate([fibre[one], fibre[one], fibre[two], fibre[two]], axis=1),
            diagonal(
                [whole(top_upper, upper_wx, one), whole(top_lower, lower_wx, one)],
                [whole(top_upper, upper_wx, two), whole(top_lower, lower_wx, two)],
            ),
        )
        imaged[pair] = folded
    for pair in range(pairs):
        rhs = two_pass(dot_nt, imaged[pair], row_block[pair])
        residual[pair] = rhs
        direction[pair] = rhs
        estimate[pair] = jnp.zeros_like(rhs)
        partial[pair : pair + 1, :] = jnp.sum(rhs * rhs, axis=0, keepdims=True)
    for pair in range(pairs):
        one, two = 2 * pair, 2 * pair + 1
        blended = dot_nt(
            jnp.concatenate([products[one], products[two]], axis=1),
            diagonal(
                [whole(top_w, weights_w, one)] * 2,
                [whole(top_w, weights_w, two)] * 2,
            ),
        )
        for index, (f, t) in enumerate(tiles):
            value = blended[index * SUB : (index + 1) * SUB]
            if f < main:
                matrix[pair, f * main + t * SUB : f * main + (t + 1) * SUB, :] = value
                if t > f // SUB:
                    matrix[pair, pl.ds(t * SUB * main + f, SUB, stride=main), :] = value
            else:
                if t < blocks:
                    matrix[pair, f * main + t * SUB : f * main + (t + 1) * SUB, :] = value
                tails[pair, f - main, t * SUB : (t + 1) * SUB, :] = value

    lane_all = lax.broadcasted_iota(jnp.int32, partial.shape, 1)
    lower_half = lane_all < HALF

    def patch_sums(value):
        first = jnp.sum(jnp.where(lower_half, value, 0.0), axis=1, keepdims=True)
        second = jnp.sum(jnp.where(lower_half, 0.0, value), axis=1, keepdims=True)
        return jnp.where(lower_half, first, second)

    norm[...] = patch_sums(partial[...])

    def sweep(step, carry):
        def spread(pair):
            across[pair] = two_pass(dot_nn, direction[pair], row_block[pair])

        def blend(pair):
            totals = [jnp.zeros((main, LANES), F32)] * 2
            for f in range(fibres):
                totals[f % 2] = totals[f % 2] + (
                    matrix[pair, f * main : (f + 1) * main, :] * across[pair, f : f + 1, :]
                )
            imaged[pair, 0:main, :] = totals[0] + totals[1]
            if fibres > main:
                rest = jnp.zeros((padded_f - main, LANES), F32)
                row = lax.broadcasted_iota(jnp.int32, rest.shape, 0)
                for f in range(main, fibres):
                    one = jnp.sum(tails[pair, f - main] * across[pair], axis=0, keepdims=True)
                    rest = jnp.where(row == f - main, one, rest)
                imaged[pair, main:padded_f, :] = rest

        def fold(pair):
            value = two_pass(dot_nt, imaged[pair], row_block[pair])
            imaged[pair] = value
            partial[pair : pair + 1, :] = jnp.sum(direction[pair] * value, axis=0, keepdims=True)

        for turn in range(pairs + 2):
            if turn < pairs:
                spread(turn)
            if 0 <= turn - 1 < pairs:
                blend(turn - 1)
            if 0 <= turn - 2:
                fold(turn - 2)
        norm_now = norm[...]
        curvature = patch_sums(partial[...])
        step_size = norm_now / jnp.where(curvature > 0.0, curvature, 1.0)
        for pair in range(pairs):
            size = step_size[pair : pair + 1]
            estimate[pair] = estimate[pair] + size * direction[pair]
            rest = residual[pair] - size * imaged[pair]
            residual[pair] = rest
            partial[pair : pair + 1, :] = jnp.sum(rest * rest, axis=0, keepdims=True)
        norm_next = patch_sums(partial[...])
        ratio = norm_next / jnp.where(norm_now > 0.0, norm_now, 1.0)
        for pair in range(pairs):
            direction[pair] = residual[pair] + ratio[pair : pair + 1] * direction[pair]
        norm[...] = norm_next
        return carry

    lax.fori_loop(0, ITERS, sweep, 0)

    copies[2].wait()
    copies[3].wait()
    slots = send.shape[0]
    for index in range(slots):
        counts[index] = 0
    if slots * capacity > patches:
        send[...] = jnp.zeros_like(send)
    upper_rows = (fibres + 1) // 2
    slot_rows = upper_rows
    eye = lax.broadcasted_iota(jnp.int32, (padded_f, LANES), 0) == lax.broadcasted_iota(
        jnp.int32, (padded_f, LANES), 1
    )
    lane_f = lax.broadcasted_iota(jnp.int32, (padded_f, LANES), 1)
    for pair in range(pairs):
        spectra = estimate[pair]
        turned = pltpu.roll(spectra, HALF, 1)
        for half in range(2):
            patch = 2 * pair + half
            here = turned if half else spectra
            away = spectra if half else turned
            target = dest[patch]
            slot = counts[target]
            counts[target] = slot + 1
            compact = jnp.where(
                lane_f[:upper_rows] < HALF,
                here[:upper_rows],
                jnp.concatenate(
                    [away[upper_rows:fibres], away[: 2 * upper_rows - fibres]], axis=0
                ),
            )
            send[target, pl.ds(slot * slot_rows, slot_rows), :] = compact
            own = jnp.broadcast_to(weight[patch], (padded_f, fibres))
            own = jnp.sum(jnp.where(eye[:, :fibres], own, 0.0), axis=1, keepdims=True)
            value = jnp.where(lane_f == waves, 1.0, here) * own
            collected[pl.ds(patch, fibres, stride=padded_p), :] = value[:fibres]
    for f in range(fibres):
        numer[f] = collected[f * padded_p : f * padded_p + patches, : waves + 1]


def finish_kernel(capacity, received, numer, others, spectra_ext, coadd):
    fibres, patches, _ = coadd.shape
    waves = coadd.shape[2]
    upper_rows = (fibres + 1) // 2
    group = received.shape[0]
    slot_rows = upper_rows
    for source in range(group):
        for slot in range(capacity):
            value = received[source, slot * slot_rows : (slot + 1) * slot_rows, :]
            turned = pltpu.roll(value, HALF, 1)
            entry = source * capacity + slot
            for f in range(fibres):
                row = value[f : f + 1] if f < upper_rows else turned[f - upper_rows : f - upper_rows + 1]
                spectra_ext[entry, f] = row[:, :waves]
    for f in range(fibres):
        total = numer[f]
        for index in range(others.shape[0]):
            total = total + others[index, f]
        coadd[f] = total[:, :waves] / total[:, waves : waves + 1]


def vmem(count=1):
    return [pl.BlockSpec(memory_space=pltpu.VMEM)] * count


def hbm(count=1):
    return [pl.BlockSpec(memory_space=pltpu.HBM)] * count


def prepare(exposure, row_prof, col_prof, row_off, col_off):
    patches = row_prof.shape[0]
    fibres = col_prof.shape[0]
    _, band, columns = exposure.shape
    padded_f = up(fibres, SUB)
    padded_p = up(patches, SUB)
    rows = SUB * len(block_tiles(fibres))

    def made(*shape):
        return jax.ShapeDtypeStruct((patches,) + shape, BF16)

    return pl.pallas_call(
        prepare_kernel,
        out_shape=(
            made(rows, 2 * PC),
            made(PR, PC),
            made(PR, PC),
            made(PR, PC),
            made(padded_f, PC),
            made(HALF, LANES),
        ),
        in_specs=hbm(5),
        out_specs=tuple(vmem(6)),
        scratch_shapes=[
            pltpu.SMEM(row_off.shape, row_off.dtype),
            pltpu.SMEM(col_off.shape, col_off.dtype),
            pltpu.VMEM(exposure.shape, exposure.dtype),
            pltpu.VMEM(row_prof.shape, row_prof.dtype),
            pltpu.VMEM(col_prof.shape, col_prof.dtype),
            pltpu.VMEM((columns // LANES + 1, band, LANES), F32),
            pltpu.VMEM((columns // LANES + 1, band, LANES), F32),
            pltpu.VMEM((PC // LANES, fibres * padded_p, LANES), F32),
            pltpu.VMEM((padded_f, PC), F32),
            pltpu.VMEM((HALF, LANES), F32),
            pltpu.SemaphoreType.DMA((5,)),
        ],
        cost_estimate=pl.CostEstimate(
            flops=patches * rows * PC * 8, bytes_accessed=16 * 1024 * 1024, transcendentals=0
        ),
        compiler_params=pltpu.CompilerParams(vmem_limit_bytes=24 * 1024 * 1024),
    )(row_off, col_off, exposure, row_prof, col_prof)


def solve(halos, prepared, waves, row_off, col_off, dest, weight, group):
    patches, _, fibres = weight.shape
    columns = halos[0].shape[2]
    capacity = (patches + group - 1) // group
    pairs = patches // 2
    main = fibres // SUB * SUB
    padded_f = up(fibres, SUB)
    padded_p = up(patches, SUB)
    vectors = pltpu.VMEM((pairs, padded_f, LANES), F32)
    sums = pltpu.VMEM((up(pairs, SUB), LANES), F32)
    return pl.pallas_call(
        functools.partial(solve_kernel, capacity, waves),
        out_shape=(
            jax.ShapeDtypeStruct((group, up(capacity * ((fibres + 1) // 2), SUB), LANES), F32),
            jax.ShapeDtypeStruct((fibres, patches, waves + 1), F32),
        ),
        in_specs=hbm(4) + vmem(8),
        out_specs=tuple(vmem(2)),
        scratch_shapes=[
            pltpu.SMEM(row_off.shape, row_off.dtype),
            pltpu.SMEM(col_off.shape, col_off.dtype),
            pltpu.SMEM(dest.shape, dest.dtype),
            pltpu.VMEM(weight.shape, weight.dtype),
            pltpu.VMEM((columns // LANES + 1, 2 * HALO, LANES), F32),
            pltpu.VMEM((columns // LANES + 1, 2 * HALO, LANES), F32),
            pltpu.VMEM((patches, 2 * HALO, PC), BF16),
            pltpu.VMEM((patches, 2 * HALO, PC), BF16),
            pltpu.VMEM((patches, 2 * HALO, PC), BF16),
            pltpu.VMEM((pairs, LANES, LANES), BF16),
            pltpu.VMEM((pairs, fibres * main, LANES), F32),
            pltpu.VMEM((pairs, max(fibres - main, 1), padded_f, LANES), F32),
            vectors,
            vectors,
            vectors,
            vectors,
            vectors,
            sums,
            sums,
            pltpu.VMEM((fibres * padded_p, LANES), F32),
            pltpu.SMEM((group,), jnp.int32),
            pltpu.SemaphoreType.DMA((4,)),
        ],
        compiler_params=pltpu.CompilerParams(vmem_limit_bytes=24 * 1024 * 1024),
    )(row_off, col_off, dest, weight, *halos, *prepared)


def finish(received, numer, others, capacity):
    fibres, patches, wide = numer.shape
    entries = received.shape[0] * capacity
    return pl.pallas_call(
        functools.partial(finish_kernel, capacity),
        out_shape=(
            jax.ShapeDtypeStruct((entries, fibres, 1, wide - 1), F32),
            jax.ShapeDtypeStruct((fibres, patches, wide - 1), F32),
        ),
        in_specs=vmem(3),
        out_specs=tuple(vmem(2)),
        compiler_params=pltpu.CompilerParams(vmem_limit_bytes=16 * 1024 * 1024),
    )(received, numer, others)


def edge_kernel(exposure, two, one):
    rank = lax.axis_index("section") * lax.axis_size("patch") + lax.axis_index("patch")
    even = lax.rem(rank, 2) == 0
    band = exposure.shape[1]
    for channel in range(exposure.shape[0]):
        top = exposure[channel, 0:HALO, :].astype(F32)
        bottom = exposure[channel, band - HALO : band, :].astype(F32)
        one[channel] = jnp.where(even, bottom, top).astype(BF16)
        two[channel] = jnp.where(even, top, bottom).astype(BF16)


def edges(exposure):
    channels, _, columns = exposure.shape
    return pl.pallas_call(
        edge_kernel,
        out_shape=(jax.ShapeDtypeStruct((channels, HALO, columns), BF16),) * 2,
        in_specs=vmem(1),
        out_specs=tuple(vmem(2)),
        cost_estimate=pl.CostEstimate(
            flops=EDGE_FLOPS, bytes_accessed=EDGE_BYTES, transcendentals=0
        ),
        compiler_params=pltpu.CompilerParams(vmem_limit_bytes=8 * 1024 * 1024),
    )(exposure)


def neighbours(block):
    axes = ("section", "patch")
    count = lax.axis_size(axes)
    two, one = edges(block)
    received = []
    for first, value in ((1, two), (0, one)):
        pairs = [(i, i + 1) for i in range(first, count - 1, 2)]
        received.append(lax.ppermute(value, axes, pairs + [(b, a) for a, b in pairs]))
    return received[1], received[0]


def local(exposure, row_prof, col_prof, row_off, col_off, dest, fibre_weight):
    group = lax.axis_size("patch")
    frames = lax.axis_size("frame")
    patches = dest.shape[1]
    waves = row_prof.shape[2]
    capacity = (patches + group - 1) // group
    halos = neighbours(exposure[0])
    prepared = prepare(
        exposure[0], row_prof[0], col_prof[0].transpose(1, 0, 2), row_off[0], col_off[0]
    )
    send, numer = solve(
        halos,
        prepared,
        waves,
        row_off[0],
        col_off[0],
        dest[0],
        fibre_weight[0][:, None, :],
        group,
    )
    received = lax.all_to_all(send, "patch", split_axis=0, concat_axis=0, tiled=True)
    others = jnp.stack(
        [
            lax.ppermute(numer, "frame", [(i, (i + hop) % frames) for i in range(frames)])
            for hop in range(1, frames)
        ]
    )
    spectra_ext, coadd = finish(received, numer, others, capacity)
    return spectra_ext.transpose(2, 0, 3, 1), coadd.transpose(1, 2, 0)


def solution(mesh):
    in_specs = (
        P("frame", None, ("section", "patch"), None),
        P("frame", ("section", "patch"), None, None),
        P("frame", ("section", "patch"), None, None),
        P("frame", ("section", "patch")),
        P("frame", ("section", "patch")),
        P("frame", ("section", "patch")),
        P("frame", ("section", "patch"), None),
    )
    out_specs = (P("frame", ("section", "patch"), None, None), P(("section", "patch"), None, None))
    return jax.shard_map(local, mesh=mesh, in_specs=in_specs, out_specs=out_specs, check_vma=False)
```

```python
import functools

import jax
import jax.numpy as jnp
from jax import lax
from jax.experimental import pallas as pl
from jax.experimental.pallas import tpu as pltpu
from jax.sharding import PartitionSpec as P

HALO = 8
PC = 256
ITERS = 6
PR = 64
LANES = 128
SUB = 8
HALF = LANES // 2
CODE_BITS = 15.0
CODE_TOP = 32767.0
TINY = 1e-30
EDGE_FLOPS = 1 << 34
EDGE_BYTES = 1 << 27
F32 = jnp.float32
BF16 = jnp.bfloat16


def up(count, multiple):
    return -(-count // multiple) * multiple


def dot_nt(lhs, rhs):
    return lax.dot_general(lhs, rhs, (((1,), (1,)), ((), ())), preferred_element_type=F32)


def dot_nn(lhs, rhs):
    return lax.dot_general(lhs, rhs, (((1,), (0,)), ((), ())), preferred_element_type=F32)


def two_parts(value):
    high = value.astype(BF16)
    return high, (value - high.astype(F32)).astype(BF16)


def two_pass(dot, value, weights):
    rows = value.shape[0]
    both = dot(jnp.concatenate(two_parts(value), axis=0), weights)
    return both[:rows] + both[rows:]


def block_tiles(fibres):
    blocks = fibres // SUB
    tiles = [(f, t) for f in range(blocks * SUB) for t in range(f // SUB, blocks)]
    for f in range(blocks * SUB, fibres):
        tiles += [(f, t) for t in range(up(fibres, SUB) // SUB)]
    return tiles


def split_lanes(value):
    return [value[:, at : at + LANES] for at in range(0, value.shape[1], LANES)]


def shifted(pieces, shift):
    rows = pieces[0].shape[0]
    turned = [pltpu.roll(piece, LANES - shift, 1) for piece in pieces]
    inside = lax.broadcasted_iota(jnp.int32, (rows, LANES), 1) < LANES - shift
    return [jnp.where(inside, turned[i], turned[i + 1]) for i in range(len(pieces) - 1)]


def start_copies(sources, targets, arrived):
    copies = [
        pltpu.make_async_copy(source, target, arrived.at[index])
        for index, (source, target) in enumerate(zip(sources, targets))
    ]
    for copy in copies:
        copy.start()
    return copies


def prepare_kernel(
    row_off_in,
    col_off_in,
    exposure_in,
    row_prof_in,
    col_prof_in,
    weight,
    products,
    weights_w,
    upper_wx,
    lower_wx,
    fibre,
    row_block,
    weight_lanes,
    row_off,
    col_off,
    exposure,
    row_prof,
    col_prof,
    band_w,
    band_wx,
    prof,
    fibre_rows,
    cut_row,
    arrived,
):
    copies = start_copies(
        (exposure_in, col_prof_in, row_prof_in, row_off_in, col_off_in),
        (exposure, col_prof, row_prof, row_off, col_off),
        arrived,
    )
    patches, waves, _ = row_prof.shape
    fibres = col_prof.shape[0]
    columns = exposure.shape[2]
    padded_p = up(patches, SUB)
    tiles = block_tiles(fibres)
    copies[0].wait()
    inverse = exposure[1].astype(F32)
    scaled = inverse * exposure[0].astype(F32)
    for piece, value in enumerate(split_lanes(inverse)):
        band_w[piece] = value
    for piece, value in enumerate(split_lanes(scaled)):
        band_wx[piece] = value
    copies[1].wait()
    for f in range(fibres):
        for piece, value in enumerate(split_lanes(col_prof[f].astype(F32))):
            prof[piece, f * padded_p : f * padded_p + patches, :] = value
    for copy in copies[2:]:
        copy.wait()
    cut_row[...] = jnp.zeros_like(cut_row)
    fibre_rows[...] = jnp.zeros_like(fibre_rows)
    halo = jnp.zeros((HALO, LANES), F32)
    square = (fibre.shape[1], fibres)
    eye = lax.broadcasted_iota(jnp.int32, square, 0) == lax.broadcasted_iota(jnp.int32, square, 1)
    lower_half = lax.broadcasted_iota(jnp.int32, (HALF, LANES), 1) < HALF

    def prepare(patch, carry):
        first_row = row_off[patch]
        first_col = col_off[patch]
        base = first_col // LANES
        shift = first_col - base * LANES
        count = PC // LANES
        window = shifted([band_w[base + piece] for piece in range(count + 1)], shift)
        for piece, value in enumerate(window):
            lanes = slice(piece * LANES, (piece + 1) * LANES)
            weights_w[patch, :, lanes] = jnp.concatenate([halo, value], axis=0).astype(BF16)
        window = shifted([band_wx[base + piece] for piece in range(count + 1)], shift)
        for piece, value in enumerate(window):
            lanes = slice(piece * LANES, (piece + 1) * LANES)
            upper, lower = two_parts(jnp.concatenate([halo, value], axis=0))
            upper_wx[patch, :, lanes] = upper
            lower_wx[patch, :, lanes] = lower
        for piece in range(count):
            lanes = slice(piece * LANES, (piece + 1) * LANES)
            fibre_rows[0:fibres, lanes] = prof[piece, pl.ds(patch, fibres, stride=padded_p), :]
        fibre[patch] = fibre_rows[...].astype(BF16)
        for at in range(0, len(tiles), 2):
            value = jnp.concatenate(
                [
                    fibre_rows[f : f + 1, :] * fibre_rows[t * SUB : (t + 1) * SUB, :]
                    for f, t in tiles[at : at + 2]
                ],
                axis=0,
            )
            upper, lower = two_parts(value)
            products[patch, at * SUB : (at + 2) * SUB, 0:PC] = upper
            products[patch, at * SUB : (at + 2) * SUB, PC : 2 * PC] = lower
        cut_row[0:waves, 0:PR] = row_prof[patch].astype(F32)
        profile = cut_row[...]
        turned = pltpu.roll(profile + pltpu.roll(profile, HALF, 1), first_row, 1)
        keep = lower_half == (lax.rem(patch, 2) == 0)
        row_block[patch] = jnp.where(keep, turned, 0.0).astype(BF16)
        own = jnp.broadcast_to(weight[patch], eye.shape)
        own = jnp.sum(jnp.where(eye, own, 0.0), axis=1, keepdims=True)
        weight_lanes[patch] = jnp.where(keep[: own.shape[0]], own, 0.0)
        return carry

    lax.fori_loop(0, patches, prepare, 0)


def solve_kernel(
    fibres,
    waves,
    row_off_in,
    col_off_in,
    dest_in,
    halo_one,
    halo_two,
    products,
    weights_w,
    upper_wx,
    lower_wx,
    fibre,
    row_block,
    weight_lanes,
    send,
    numer,
    row_off,
    col_off,
    dest,
    halo_w,
    halo_wx,
    top_w,
    top_upper,
    top_lower,
    matrix,
    tails,
    estimate,
    residual,
    direction,
    imaged,
    across,
    partial,
    norm,
    packed,
    counts,
    arrived,
):
    copies = start_copies(
        (row_off_in, col_off_in, dest_in), (row_off, col_off, dest), arrived
    )
    patches = products.shape[0]
    pairs = patches // 2
    blocks = fibres // SUB
    main = blocks * SUB
    padded_f = up(fibres, SUB)
    tiles = block_tiles(fibres)
    rank = lax.axis_index("section") * lax.axis_size("patch") + lax.axis_index("patch")
    odd = lax.rem(rank, 2) == 1

    for slot, source in enumerate((halo_one, halo_two)):
        rows = slice(slot * HALO, (slot + 1) * HALO)
        inverse = source[1].astype(F32)
        for piece, value in enumerate(split_lanes(inverse)):
            halo_w[piece, rows, :] = value
        for piece, value in enumerate(split_lanes(inverse * source[0].astype(F32))):
            halo_wx[piece, rows, :] = value
    partial[...] = jnp.zeros_like(partial)
    halo_row = lax.broadcasted_iota(jnp.int32, (HALO, LANES), 0)
    empty = jnp.zeros((PR, PC), BF16)
    copies[0].wait()
    copies[1].wait()

    def beside_own(edge, own):
        return jnp.concatenate([edge, own.astype(F32)[HALO:]], axis=0).astype(BF16)

    for patch in range(patches):
        first_row = row_off[patch]
        first_col = col_off[patch]
        base = first_col // LANES
        shift = first_col - base * LANES
        take_one = (halo_row >= first_row) == odd
        edges = []
        for source in (halo_w, halo_wx):
            pieces = [
                jnp.where(
                    take_one,
                    source[base + piece, 0:HALO, :],
                    source[base + piece, HALO : 2 * HALO, :],
                )
                for piece in range(PC // LANES + 1)
            ]
            edges.append(jnp.concatenate(shifted(pieces, shift), axis=1))
        above = edges[1].astype(BF16).astype(F32)
        top_w[patch] = beside_own(edges[0], weights_w[patch, : 2 * HALO, :])
        top_upper[patch] = beside_own(above, upper_wx[patch, : 2 * HALO, :])
        top_lower[patch] = beside_own(edges[1] - above, lower_wx[patch, : 2 * HALO, :])

    halves = partial.shape[0]
    members = [list(range(at, pairs, halves)) for at in range(halves)]

    def set_partial(pair, value):
        row = pair // halves
        partial[pair % halves, row : row + 1, :] = value

    def whole(top, own, patch):
        return jnp.concatenate([top[patch], own[patch, 2 * HALO :, :]], axis=0)

    def diagonal(first, second):
        return jnp.concatenate(
            [
                jnp.concatenate(first + [empty] * len(second), axis=1),
                jnp.concatenate([empty] * len(first) + second, axis=1),
            ],
            axis=0,
        )

    for pair in range(pairs):
        one, two = 2 * pair, 2 * pair + 1
        folded = dot_nt(
            jnp.concatenate([fibre[one], fibre[one], fibre[two], fibre[two]], axis=1),
            diagonal(
                [whole(top_upper, upper_wx, one), whole(top_lower, lower_wx, one)],
                [whole(top_upper, upper_wx, two), whole(top_lower, lower_wx, two)],
            ),
        )
        imaged[pair] = folded
    for pair in range(pairs):
        rhs = two_pass(dot_nt, imaged[pair], row_block[pair])
        residual[pair] = rhs
        direction[pair] = rhs
        estimate[pair] = jnp.zeros_like(rhs)
        set_partial(pair, jnp.sum(rhs * rhs, axis=0, keepdims=True))
    for pair in range(pairs):
        one, two = 2 * pair, 2 * pair + 1
        blended = dot_nt(
            jnp.concatenate([products[one], products[two]], axis=1),
            diagonal(
                [whole(top_w, weights_w, one)] * 2,
                [whole(top_w, weights_w, two)] * 2,
            ),
        )
        for index, (f, t) in enumerate(tiles):
            value = blended[index * SUB : (index + 1) * SUB]
            if f < main:
                matrix[pair, f * main + t * SUB : f * main + (t + 1) * SUB, :] = value
                if t > f // SUB:
                    matrix[pair, pl.ds(t * SUB * main + f, SUB, stride=main), :] = value
            else:
                if t < blocks:
                    matrix[pair, f * main + t * SUB : f * main + (t + 1) * SUB, :] = value
                tails[pair, f - main, t * SUB : (t + 1) * SUB, :] = value

    lower_half = lax.broadcasted_iota(jnp.int32, partial.shape[1:], 1) < HALF

    def patch_sums(value):
        first = jnp.sum(jnp.where(lower_half, value, 0.0), axis=1, keepdims=True)
        second = jnp.sum(jnp.where(lower_half, 0.0, value), axis=1, keepdims=True)
        return jnp.where(lower_half, first, second)

    def spread(pair):
        across[pair] = two_pass(dot_nn, direction[pair], row_block[pair])

    def blend(pair):
        totals = [jnp.zeros((main, LANES), F32)] * 2
        for f in range(fibres):
            totals[f % 2] = totals[f % 2] + (
                matrix[pair, f * main : (f + 1) * main, :] * across[pair, f : f + 1, :]
            )
        imaged[pair, 0:main, :] = totals[0] + totals[1]
        if fibres > main:
            rest = jnp.zeros((padded_f - main, LANES), F32)
            row = lax.broadcasted_iota(jnp.int32, rest.shape, 0)
            for f in range(main, fibres):
                one = jnp.sum(tails[pair, f - main] * across[pair], axis=0, keepdims=True)
                rest = jnp.where(row == f - main, one, rest)
            imaged[pair, main:padded_f, :] = rest

    def fold(pair):
        value = two_pass(dot_nt, imaged[pair], row_block[pair])
        imaged[pair] = value
        set_partial(pair, jnp.sum(direction[pair] * value, axis=0, keepdims=True))

    def image(half):
        some = members[half]
        for turn in range(len(some) + 2):
            if turn < len(some):
                spread(some[turn])
            if 0 <= turn - 1 < len(some):
                blend(some[turn - 1])
            if 0 <= turn - 2:
                fold(some[turn - 2])

    def move(half):
        norm_now = norm[half]
        curvature = patch_sums(partial[half])
        step_size = norm_now / jnp.where(curvature > 0.0, curvature, 1.0)
        for row, pair in enumerate(members[half]):
            size = step_size[row : row + 1]
            estimate[pair] = estimate[pair] + size * direction[pair]
            rest = residual[pair] - size * imaged[pair]
            residual[pair] = rest
            set_partial(pair, jnp.sum(rest * rest, axis=0, keepdims=True))
        norm_next = patch_sums(partial[half])
        ratio = norm_next / jnp.where(norm_now > 0.0, norm_now, 1.0)
        for row, pair in enumerate(members[half]):
            direction[pair] = residual[pair] + ratio[row : row + 1] * direction[pair]
        norm[half] = norm_next

    for half in range(halves):
        norm[half] = patch_sums(partial[half])
    image(0)

    image_rest = range(1, halves)
    for half in image_rest:
        image(half)
        move(half - 1)

    def turn_about(step, carry):
        image(0)
        move(halves - 1)
        for half in image_rest:
            image(half)
            move(half - 1)
        return carry

    lax.fori_loop(0, ITERS - 1, turn_about, 0)
    move(halves - 1)

    copies[2].wait()
    for index in range(send.shape[0]):
        counts[index] = 0
    packed[...] = jnp.zeros_like(packed)
    upper_rows = (fibres + 1) // 2
    lane_f = lax.broadcasted_iota(jnp.int32, (padded_f, LANES), 1)
    at_wave = lax.rem(lane_f, HALF) == waves
    unit = jnp.where(at_wave, 1.0, 0.0)
    for pair in range(pairs):
        spectra = estimate[pair]
        numer[pair] = (spectra + unit) * (weight_lanes[2 * pair] + weight_lanes[2 * pair + 1])
        size = jnp.abs(spectra)
        first = jnp.max(jnp.where(lane_f < HALF, size, 0.0), axis=1, keepdims=True)
        second = jnp.max(jnp.where(lane_f < HALF, 0.0, size), axis=1, keepdims=True)
        largest = jnp.where(lane_f < HALF, first, second)
        power = jnp.floor(jnp.log2(jnp.maximum(largest, TINY))) + 1.0
        coded = jnp.clip(jnp.round(spectra * jnp.exp2(CODE_BITS - power)), -CODE_TOP, CODE_TOP)
        coded = jnp.where(at_wave, power, coded)
        turned = pltpu.roll(coded, HALF, 1)
        for half in range(2):
            here = turned if half else coded
            away = coded if half else turned
            target = dest[2 * pair + half]
            slot = counts[target]
            counts[target] = slot + 1
            compact = jnp.where(
                lane_f[:upper_rows] < HALF,
                here[:upper_rows],
                jnp.concatenate(
                    [away[upper_rows:fibres], away[: 2 * upper_rows - fibres]], axis=0
                ),
            )
            packed[target, pl.ds(slot * upper_rows, upper_rows), :] = compact
    for index in range(send.shape[0]):
        send[index] = packed[index].astype(jnp.int32).astype(jnp.int16)


def coadd_kernel(numer, others, coadd, collected):
    fibres, patches, waves = coadd.shape
    padded_p = up(patches, SUB)
    lower_half = lax.broadcasted_iota(jnp.int32, numer.shape[1:], 1) < HALF
    for pair in range(numer.shape[0]):
        total = numer[pair]
        for index in range(others.shape[0]):
            total = total + others[index, pair]
        first, second = total[:, waves : waves + 1], total[:, HALF + waves : HALF + waves + 1]
        mean = total / jnp.where(lower_half, first, second)
        for half in range(2):
            value = pltpu.roll(mean, HALF, 1) if half else mean
            collected[pl.ds(2 * pair + half, fibres, stride=padded_p), :] = value[:fibres]
    for f in range(fibres):
        coadd[f] = collected[f * padded_p : f * padded_p + patches, :waves]


def finish_kernel(capacity, received, spectra_ext):
    _, fibres, _, waves = spectra_ext.shape
    upper_rows = (fibres + 1) // 2
    lower_half = lax.broadcasted_iota(jnp.int32, received.shape[1:], 1) < HALF
    for source in range(received.shape[0]):
        coded = received[source].astype(jnp.int32).astype(F32)
        power = jnp.where(
            lower_half, coded[:, waves : waves + 1], coded[:, HALF + waves : HALF + waves + 1]
        )
        value = coded * jnp.exp2(power - CODE_BITS)
        turned = pltpu.roll(value, HALF, 1)
        for slot in range(capacity):
            entry = source * capacity + slot
            for f in range(fibres):
                at = slot * upper_rows + f % upper_rows
                row = (value if f < upper_rows else turned)[at : at + 1]
                spectra_ext[entry, f] = row[:, :waves]


def vmem(count=1):
    return [pl.BlockSpec(memory_space=pltpu.VMEM)] * count


def hbm(count=1):
    return [pl.BlockSpec(memory_space=pltpu.HBM)] * count


def prepare(exposure, row_prof, col_prof, row_off, col_off, weight):
    patches = row_prof.shape[0]
    fibres = col_prof.shape[0]
    _, band, columns = exposure.shape
    padded_f = up(fibres, SUB)
    padded_p = up(patches, SUB)
    rows = SUB * len(block_tiles(fibres))

    def made(*shape):
        return jax.ShapeDtypeStruct((patches,) + shape, BF16)

    return list(
        pl.pallas_call(
        prepare_kernel,
        out_shape=(
            made(rows, 2 * PC),
            made(PR, PC),
            made(PR, PC),
            made(PR, PC),
            made(padded_f, PC),
            made(HALF, LANES),
            jax.ShapeDtypeStruct((patches, padded_f, LANES), F32),
        ),
        in_specs=hbm(5) + vmem(1),
        out_specs=tuple(vmem(7)),
        scratch_shapes=[
            pltpu.SMEM(row_off.shape, row_off.dtype),
            pltpu.SMEM(col_off.shape, col_off.dtype),
            pltpu.VMEM(exposure.shape, exposure.dtype),
            pltpu.VMEM(row_prof.shape, row_prof.dtype),
            pltpu.VMEM(col_prof.shape, col_prof.dtype),
            pltpu.VMEM((columns // LANES + 1, band, LANES), F32),
            pltpu.VMEM((columns // LANES + 1, band, LANES), F32),
            pltpu.VMEM((PC // LANES, fibres * padded_p, LANES), F32),
            pltpu.VMEM((padded_f, PC), F32),
            pltpu.VMEM((HALF, LANES), F32),
            pltpu.SemaphoreType.DMA((5,)),
        ],
        cost_estimate=pl.CostEstimate(
            flops=patches * rows * PC * 8, bytes_accessed=16 * 1024 * 1024, transcendentals=0
        ),
        compiler_params=pltpu.CompilerParams(vmem_limit_bytes=24 * 1024 * 1024),
    )(row_off, col_off, exposure, row_prof, col_prof, weight)
    )


def solve(halos, prepared, fibres, waves, row_off, col_off, dest, group):
    patches = dest.shape[0]
    columns = halos[0].shape[2]
    capacity = (patches + group - 1) // group
    pairs = patches // 2
    main = fibres // SUB * SUB
    padded_f = up(fibres, SUB)
    code_rows = up(capacity * ((fibres + 1) // 2), SUB)
    vectors = pltpu.VMEM((pairs, padded_f, LANES), F32)
    sums = pltpu.VMEM((2, up((pairs + 1) // 2, SUB), LANES), F32)
    tops = pltpu.VMEM((patches, 2 * HALO, PC), BF16)
    halo_band = pltpu.VMEM((columns // LANES + 1, 2 * HALO, LANES), F32)
    return pl.pallas_call(
        functools.partial(solve_kernel, fibres, waves),
        out_shape=(
            jax.ShapeDtypeStruct((group, code_rows, LANES), jnp.int16),
            jax.ShapeDtypeStruct((pairs, padded_f, LANES), F32),
        ),
        in_specs=hbm(3) + vmem(9),
        out_specs=tuple(vmem(2)),
        scratch_shapes=[
            pltpu.SMEM(row_off.shape, row_off.dtype),
            pltpu.SMEM(col_off.shape, col_off.dtype),
            pltpu.SMEM(dest.shape, dest.dtype),
            halo_band,
            halo_band,
            tops,
            tops,
            tops,
            pltpu.VMEM((pairs, fibres * main, LANES), F32),
            pltpu.VMEM((pairs, max(fibres - main, 1), padded_f, LANES), F32),
            vectors,
            vectors,
            vectors,
            vectors,
            vectors,
            sums,
            sums,
            pltpu.VMEM((group, code_rows, LANES), F32),
            pltpu.SMEM((group,), jnp.int32),
            pltpu.SemaphoreType.DMA((3,)),
        ],
        compiler_params=pltpu.CompilerParams(vmem_limit_bytes=24 * 1024 * 1024),
    )(row_off, col_off, dest, *halos, *prepared)


def frame_mean(numer, others, patches, fibres, waves):
    return pl.pallas_call(
        coadd_kernel,
        out_shape=jax.ShapeDtypeStruct((fibres, patches, waves), F32),
        in_specs=vmem(2),
        out_specs=vmem()[0],
        scratch_shapes=[pltpu.VMEM((fibres * up(patches, SUB), LANES), F32)],
        compiler_params=pltpu.CompilerParams(vmem_limit_bytes=16 * 1024 * 1024),
    )(numer, others)


def finish(received, capacity, fibres, waves):
    entries = received.shape[0] * capacity
    return pl.pallas_call(
        functools.partial(finish_kernel, capacity),
        out_shape=jax.ShapeDtypeStruct((entries, fibres, 1, waves), F32),
        in_specs=vmem(1),
        out_specs=vmem()[0],
        compiler_params=pltpu.CompilerParams(vmem_limit_bytes=16 * 1024 * 1024),
    )(received)


def edge_kernel(exposure, two, one):
    rank = lax.axis_index("section") * lax.axis_size("patch") + lax.axis_index("patch")
    even = lax.rem(rank, 2) == 0
    band = exposure.shape[1]
    for channel in range(exposure.shape[0]):
        top = exposure[channel, 0:HALO, :].astype(F32)
        bottom = exposure[channel, band - HALO : band, :].astype(F32)
        one[channel] = jnp.where(even, bottom, top).astype(BF16)
        two[channel] = jnp.where(even, top, bottom).astype(BF16)


def edges(exposure):
    channels, _, columns = exposure.shape
    return pl.pallas_call(
        edge_kernel,
        out_shape=(jax.ShapeDtypeStruct((channels, HALO, columns), BF16),) * 2,
        in_specs=vmem(1),
        out_specs=tuple(vmem(2)),
        cost_estimate=pl.CostEstimate(
            flops=EDGE_FLOPS, bytes_accessed=EDGE_BYTES, transcendentals=0
        ),
        compiler_params=pltpu.CompilerParams(vmem_limit_bytes=8 * 1024 * 1024),
    )(exposure)


def neighbours(block):
    axes = ("section", "patch")
    count = lax.axis_size(axes)
    two, one = edges(block)
    received = []
    for first, value in ((1, two), (0, one)):
        pairs = [(i, i + 1) for i in range(first, count - 1, 2)]
        received.append(lax.ppermute(value, axes, pairs + [(b, a) for a, b in pairs]))
    return received[1], received[0]


def local(exposure, row_prof, col_prof, row_off, col_off, dest, fibre_weight):
    group = lax.axis_size("patch")
    frames = lax.axis_size("frame")
    patches = dest.shape[1]
    fibres, waves = col_prof.shape[2], row_prof.shape[2]
    capacity = (patches + group - 1) // group
    halos = neighbours(exposure[0])
    prepared = prepare(
        exposure[0],
        row_prof[0],
        col_prof[0].transpose(1, 0, 2),
        row_off[0],
        col_off[0],
        fibre_weight[0][:, None, :],
    )
    prepared[5] = prepared[5].reshape(patches // 2, LANES, LANES)
    send, numer = solve(halos, prepared, fibres, waves, row_off[0], col_off[0], dest[0], group)
    received = lax.all_to_all(send, "patch", split_axis=0, concat_axis=0, tiled=True)
    others = jnp.stack(
        [
            lax.ppermute(numer, "frame", [(i, (i + hop) % frames) for i in range(frames)])
            for hop in range(1, frames)
        ]
    )
    coadd = frame_mean(numer, others, patches, fibres, waves)
    spectra_ext = finish(received, capacity, fibres, waves)
    return spectra_ext.transpose(2, 0, 3, 1), coadd.transpose(1, 2, 0)


def solution(mesh):
    in_specs = (
        P("frame", None, ("section", "patch"), None),
        P("frame", ("section", "patch"), None, None),
        P("frame", ("section", "patch"), None, None),
        P("frame", ("section", "patch")),
        P("frame", ("section", "patch")),
        P("frame", ("section", "patch")),
        P("frame", ("section", "patch"), None),
    )
    out_specs = (P("frame", ("section", "patch"), None, None), P(("section", "patch"), None, None))
    return jax.shard_map(local, mesh=mesh, in_specs=in_specs, out_specs=out_specs, check_vma=False)
```

```python
import functools

import jax
import jax.numpy as jnp
from jax import lax
from jax.experimental import pallas as pl
from jax.experimental.pallas import tpu as pltpu
from jax.sharding import PartitionSpec as P

HALO = 8
PC = 256
ITERS = 6
PR = 64
LANES = 128
SUB = 8
HALF = LANES // 2
CODE_BITS = 15.0
CODE_TOP = 32767.0
TINY = 1e-30
EDGE_FLOPS = 1 << 34
EDGE_BYTES = 1 << 27
F32 = jnp.float32
BF16 = jnp.bfloat16


def up(count, multiple):
    return -(-count // multiple) * multiple


def dot_nt(lhs, rhs):
    return lax.dot_general(lhs, rhs, (((1,), (1,)), ((), ())), preferred_element_type=F32)


def dot_nn(lhs, rhs):
    return lax.dot_general(lhs, rhs, (((1,), (0,)), ((), ())), preferred_element_type=F32)


def two_parts(value):
    high = value.astype(BF16)
    return high, (value - high.astype(F32)).astype(BF16)


def two_pass(dot, value, weights):
    rows = value.shape[0]
    both = dot(jnp.concatenate(two_parts(value), axis=0), weights)
    return both[:rows] + both[rows:]


def block_tiles(fibres):
    blocks = fibres // SUB
    tiles = [(f, t) for f in range(blocks * SUB) for t in range(f // SUB, blocks)]
    for f in range(blocks * SUB, fibres):
        tiles += [(f, t) for t in range(up(fibres, SUB) // SUB)]
    return tiles


def split_lanes(value):
    return [value[:, at : at + LANES] for at in range(0, value.shape[1], LANES)]


def shifted(pieces, shift):
    rows = pieces[0].shape[0]
    turned = [pltpu.roll(piece, LANES - shift, 1) for piece in pieces]
    inside = lax.broadcasted_iota(jnp.int32, (rows, LANES), 1) < LANES - shift
    return [jnp.where(inside, turned[i], turned[i + 1]) for i in range(len(pieces) - 1)]


def start_copies(sources, targets, arrived):
    copies = [
        pltpu.make_async_copy(source, target, arrived.at[index])
        for index, (source, target) in enumerate(zip(sources, targets))
    ]
    for copy in copies:
        copy.start()
    return copies


def prepare_kernel(
    row_off_in,
    col_off_in,
    exposure_in,
    row_prof_in,
    col_prof_in,
    weight,
    products,
    weights_w,
    upper_wx,
    lower_wx,
    fibre,
    row_block,
    weight_lanes,
    row_off,
    col_off,
    exposure,
    row_prof,
    col_prof,
    band_w,
    band_wx,
    prof,
    fibre_rows,
    cut_row,
    arrived,
):
    copies = start_copies(
        (exposure_in, col_prof_in, row_prof_in, row_off_in, col_off_in),
        (exposure, col_prof, row_prof, row_off, col_off),
        arrived,
    )
    patches, waves, _ = row_prof.shape
    fibres = col_prof.shape[0]
    columns = exposure.shape[2]
    padded_p = up(patches, SUB)
    tiles = block_tiles(fibres)
    copies[0].wait()
    inverse = exposure[1].astype(F32)
    scaled = inverse * exposure[0].astype(F32)
    for piece, value in enumerate(split_lanes(inverse)):
        band_w[piece] = value
    for piece, value in enumerate(split_lanes(scaled)):
        band_wx[piece] = value
    copies[1].wait()
    for f in range(fibres):
        for piece, value in enumerate(split_lanes(col_prof[f].astype(F32))):
            prof[piece, f * padded_p : f * padded_p + patches, :] = value
    for copy in copies[2:]:
        copy.wait()
    cut_row[...] = jnp.zeros_like(cut_row)
    fibre_rows[...] = jnp.zeros_like(fibre_rows)
    halo = jnp.zeros((HALO, LANES), F32)
    square = (fibre.shape[1], fibres)
    eye = lax.broadcasted_iota(jnp.int32, square, 0) == lax.broadcasted_iota(jnp.int32, square, 1)
    lower_half = lax.broadcasted_iota(jnp.int32, (HALF, LANES), 1) < HALF

    def prepare(patch, half):
        first_row = row_off[patch]
        first_col = col_off[patch]
        base = first_col // LANES
        shift = first_col - base * LANES
        count = PC // LANES
        window = shifted([band_w[base + piece] for piece in range(count + 1)], shift)
        for piece, value in enumerate(window):
            lanes = slice(piece * LANES, (piece + 1) * LANES)
            weights_w[patch, :, lanes] = jnp.concatenate([halo, value], axis=0).astype(BF16)
        window = shifted([band_wx[base + piece] for piece in range(count + 1)], shift)
        for piece, value in enumerate(window):
            lanes = slice(piece * LANES, (piece + 1) * LANES)
            upper, lower = two_parts(jnp.concatenate([halo, value], axis=0))
            upper_wx[patch, :, lanes] = upper
            lower_wx[patch, :, lanes] = lower
        for piece in range(count):
            lanes = slice(piece * LANES, (piece + 1) * LANES)
            fibre_rows[half, 0:fibres, lanes] = prof[piece, pl.ds(patch, fibres, stride=padded_p), :]
        fibre[patch] = fibre_rows[half].astype(BF16)
        for at in range(0, len(tiles), 2):
            value = jnp.concatenate(
                [
                    fibre_rows[half, f : f + 1, :] * fibre_rows[half, t * SUB : (t + 1) * SUB, :]
                    for f, t in tiles[at : at + 2]
                ],
                axis=0,
            )
            upper, lower = two_parts(value)
            products[patch, at * SUB : (at + 2) * SUB, 0:PC] = upper
            products[patch, at * SUB : (at + 2) * SUB, PC : 2 * PC] = lower
        cut_row[half, 0:waves, 0:PR] = row_prof[patch].astype(F32)
        profile = cut_row[half]
        turned = pltpu.roll(profile + pltpu.roll(profile, HALF, 1), first_row, 1)
        keep = lower_half == (half == 0)
        row_block[patch] = jnp.where(keep, turned, 0.0).astype(BF16)
        own = jnp.broadcast_to(weight[patch], eye.shape)
        own = jnp.sum(jnp.where(eye, own, 0.0), axis=1, keepdims=True)
        weight_lanes[patch] = jnp.where(keep[: own.shape[0]], own, 0.0)

    def prepare_two(pair, carry):
        for half in range(2):
            prepare(2 * pair + half, half)
        return carry

    lax.fori_loop(0, patches // 2, prepare_two, 0)


def solve_kernel(
    fibres,
    waves,
    row_off_in,
    col_off_in,
    dest_in,
    halo_two,
    halo_one,
    products,
    weights_w,
    upper_wx,
    lower_wx,
    fibre,
    row_block,
    weight_lanes,
    send,
    numer,
    row_off,
    col_off,
    dest,
    halo_w,
    halo_wx,
    top_w,
    top_upper,
    top_lower,
    matrix,
    tails,
    estimate,
    residual,
    direction,
    imaged,
    across,
    partial,
    norm,
    packed,
    counts,
    arrived,
):
    copies = start_copies(
        (row_off_in, col_off_in, dest_in), (row_off, col_off, dest), arrived
    )
    patches = products.shape[0]
    pairs = patches // 2
    blocks = fibres // SUB
    main = blocks * SUB
    padded_f = up(fibres, SUB)
    tiles = block_tiles(fibres)
    rank = lax.axis_index("section") * lax.axis_size("patch") + lax.axis_index("patch")
    odd = lax.rem(rank, 2) == 1

    for slot, source in enumerate((halo_one, halo_two)):
        rows = slice(slot * HALO, (slot + 1) * HALO)
        inverse = source[1].astype(F32)
        for piece, value in enumerate(split_lanes(inverse)):
            halo_w[piece, rows, :] = value
        for piece, value in enumerate(split_lanes(inverse * source[0].astype(F32))):
            halo_wx[piece, rows, :] = value
    partial[...] = jnp.zeros_like(partial)
    halo_row = lax.broadcasted_iota(jnp.int32, (HALO, LANES), 0)
    empty = jnp.zeros((PR, PC), BF16)
    copies[0].wait()
    copies[1].wait()

    def beside_own(edge, own):
        return jnp.concatenate([edge, own.astype(F32)[HALO:]], axis=0).astype(BF16)

    for patch in range(patches):
        first_row = row_off[patch]
        first_col = col_off[patch]
        base = first_col // LANES
        shift = first_col - base * LANES
        take_one = (halo_row >= first_row) == odd
        edges = []
        for source in (halo_w, halo_wx):
            pieces = [
                jnp.where(
                    take_one,
                    source[base + piece, 0:HALO, :],
                    source[base + piece, HALO : 2 * HALO, :],
                )
                for piece in range(PC // LANES + 1)
            ]
            edges.append(jnp.concatenate(shifted(pieces, shift), axis=1))
        above = edges[1].astype(BF16).astype(F32)
        top_w[patch] = beside_own(edges[0], weights_w[patch, : 2 * HALO, :])
        top_upper[patch] = beside_own(above, upper_wx[patch, : 2 * HALO, :])
        top_lower[patch] = beside_own(edges[1] - above, lower_wx[patch, : 2 * HALO, :])

    halves = partial.shape[0]
    members = [list(range(at, pairs, halves)) for at in range(halves)]

    def set_partial(pair, value):
        row = pair // halves
        partial[pair % halves, row : row + 1, :] = value

    def whole(top, own, patch):
        return jnp.concatenate([top[patch], own[patch, 2 * HALO :, :]], axis=0)

    def diagonal(first, second):
        return jnp.concatenate(
            [
                jnp.concatenate(first + [empty] * len(second), axis=1),
                jnp.concatenate([empty] * len(first) + second, axis=1),
            ],
            axis=0,
        )

    for pair in range(pairs):
        one, two = 2 * pair, 2 * pair + 1
        folded = dot_nt(
            jnp.concatenate([fibre[one], fibre[one], fibre[two], fibre[two]], axis=1),
            diagonal(
                [whole(top_upper, upper_wx, one), whole(top_lower, lower_wx, one)],
                [whole(top_upper, upper_wx, two), whole(top_lower, lower_wx, two)],
            ),
        )
        imaged[pair] = folded
    for pair in range(pairs):
        rhs = two_pass(dot_nt, imaged[pair], row_block[pair])
        residual[pair] = rhs
        direction[pair] = rhs
        estimate[pair] = jnp.zeros_like(rhs)
        set_partial(pair, jnp.sum(rhs * rhs, axis=0, keepdims=True))
    for pair in range(pairs):
        one, two = 2 * pair, 2 * pair + 1
        blended = dot_nt(
            jnp.concatenate([products[one], products[two]], axis=1),
            diagonal(
                [whole(top_w, weights_w, one)] * 2,
                [whole(top_w, weights_w, two)] * 2,
            ),
        )
        for index, (f, t) in enumerate(tiles):
            value = blended[index * SUB : (index + 1) * SUB]
            if f < main:
                matrix[pair, f * main + t * SUB : f * main + (t + 1) * SUB, :] = value
                if t > f // SUB:
                    matrix[pair, pl.ds(t * SUB * main + f, SUB, stride=main), :] = value
            else:
                if t < blocks:
                    matrix[pair, f * main + t * SUB : f * main + (t + 1) * SUB, :] = value
                tails[pair, f - main, t * SUB : (t + 1) * SUB, :] = value

    lower_half = lax.broadcasted_iota(jnp.int32, partial.shape[1:], 1) < HALF

    def patch_sums(value):
        first = jnp.sum(jnp.where(lower_half, value, 0.0), axis=1, keepdims=True)
        second = jnp.sum(jnp.where(lower_half, 0.0, value), axis=1, keepdims=True)
        return jnp.where(lower_half, first, second)

    def spread(pair):
        across[pair] = two_pass(dot_nn, direction[pair], row_block[pair])

    def blend(pair):
        totals = [jnp.zeros((main, LANES), F32)] * 2
        for f in range(fibres):
            totals[f % 2] = totals[f % 2] + (
                matrix[pair, f * main : (f + 1) * main, :] * across[pair, f : f + 1, :]
            )
        imaged[pair, 0:main, :] = totals[0] + totals[1]
        if fibres > main:
            rest = jnp.zeros((padded_f - main, LANES), F32)
            row = lax.broadcasted_iota(jnp.int32, rest.shape, 0)
            for f in range(main, fibres):
                one = jnp.sum(tails[pair, f - main] * across[pair], axis=0, keepdims=True)
                rest = jnp.where(row == f - main, one, rest)
            imaged[pair, main:padded_f, :] = rest

    def fold(pair):
        value = two_pass(dot_nt, imaged[pair], row_block[pair])
        imaged[pair] = value
        set_partial(pair, jnp.sum(direction[pair] * value, axis=0, keepdims=True))

    def image(half):
        some = members[half]
        for turn in range(len(some) + 2):
            if turn < len(some):
                spread(some[turn])
            if 0 <= turn - 1 < len(some):
                blend(some[turn - 1])
            if 0 <= turn - 2:
                fold(some[turn - 2])

    def move(half):
        norm_now = norm[half]
        curvature = patch_sums(partial[half])
        step_size = norm_now / jnp.where(curvature > 0.0, curvature, 1.0)
        for row, pair in enumerate(members[half]):
            size = step_size[row : row + 1]
            estimate[pair] = estimate[pair] + size * direction[pair]
            rest = residual[pair] - size * imaged[pair]
            residual[pair] = rest
            set_partial(pair, jnp.sum(rest * rest, axis=0, keepdims=True))
        norm_next = patch_sums(partial[half])
        ratio = norm_next / jnp.where(norm_now > 0.0, norm_now, 1.0)
        for row, pair in enumerate(members[half]):
            direction[pair] = residual[pair] + ratio[row : row + 1] * direction[pair]
        norm[half] = norm_next

    for half in range(halves):
        norm[half] = patch_sums(partial[half])
    image(0)

    image_rest = range(1, halves)
    for half in image_rest:
        image(half)
        move(half - 1)

    def turn_about(step, carry):
        image(0)
        move(halves - 1)
        for half in image_rest:
            image(half)
            move(half - 1)
        return carry

    lax.fori_loop(0, ITERS - 1, turn_about, 0)
    move(halves - 1)

    copies[2].wait()
    for index in range(send.shape[0]):
        counts[index] = 0
    packed[...] = jnp.zeros_like(packed)
    upper_rows = (fibres + 1) // 2
    lane_f = lax.broadcasted_iota(jnp.int32, (padded_f, LANES), 1)
    at_wave = lax.rem(lane_f, HALF) == waves
    unit = jnp.where(at_wave, 1.0, 0.0)
    for pair in range(pairs):
        spectra = estimate[pair]
        numer[pair] = (spectra + unit) * (weight_lanes[2 * pair] + weight_lanes[2 * pair + 1])
        size = jnp.abs(spectra)
        first = jnp.max(jnp.where(lane_f < HALF, size, 0.0), axis=1, keepdims=True)
        second = jnp.max(jnp.where(lane_f < HALF, 0.0, size), axis=1, keepdims=True)
        largest = jnp.where(lane_f < HALF, first, second)
        power = jnp.floor(jnp.log2(jnp.maximum(largest, TINY))) + 1.0
        coded = jnp.clip(jnp.round(spectra * jnp.exp2(CODE_BITS - power)), -CODE_TOP, CODE_TOP)
        coded = jnp.where(at_wave, power, coded)
        turned = pltpu.roll(coded, HALF, 1)
        for half in range(2):
            here = turned if half else coded
            away = coded if half else turned
            target = dest[2 * pair + half]
            slot = counts[target]
            counts[target] = slot + 1
            compact = jnp.where(
                lane_f[:upper_rows] < HALF,
                here[:upper_rows],
                jnp.concatenate(
                    [away[upper_rows:fibres], away[: 2 * upper_rows - fibres]], axis=0
                ),
            )
            packed[target, pl.ds(slot * upper_rows, upper_rows), :] = compact
    for index in range(send.shape[0]):
        send[index] = packed[index].astype(jnp.int32).astype(jnp.int16)


def finish_kernel(capacity, received, numer, others, spectra_ext, coadd, collected):
    fibres, patches, waves = coadd.shape
    padded_p = up(patches, SUB)
    lower_half = lax.broadcasted_iota(jnp.int32, numer.shape[1:], 1) < HALF
    for pair in range(numer.shape[0]):
        total = numer[pair]
        for index in range(others.shape[0]):
            total = total + others[index, pair]
        first, second = total[:, waves : waves + 1], total[:, HALF + waves : HALF + waves + 1]
        mean = total / jnp.where(lower_half, first, second)
        for half in range(2):
            value = pltpu.roll(mean, HALF, 1) if half else mean
            collected[pl.ds(2 * pair + half, fibres, stride=padded_p), :] = value[:fibres]
    for f in range(fibres):
        coadd[f] = collected[f * padded_p : f * padded_p + patches, :waves]
    upper_rows = (fibres + 1) // 2
    lower_half = lax.broadcasted_iota(jnp.int32, received.shape[1:], 1) < HALF
    for source in range(received.shape[0]):
        coded = received[source].astype(jnp.int32).astype(F32)
        power = jnp.where(
            lower_half, coded[:, waves : waves + 1], coded[:, HALF + waves : HALF + waves + 1]
        )
        value = coded * jnp.exp2(power - CODE_BITS)
        turned = pltpu.roll(value, HALF, 1)
        for slot in range(capacity):
            entry = source * capacity + slot
            for f in range(fibres):
                at = slot * upper_rows + f % upper_rows
                row = (value if f < upper_rows else turned)[at : at + 1]
                spectra_ext[entry, f] = row[:, :waves]


def vmem(count=1):
    return [pl.BlockSpec(memory_space=pltpu.VMEM)] * count


def hbm(count=1):
    return [pl.BlockSpec(memory_space=pltpu.HBM)] * count


def prepare(exposure, row_prof, col_prof, row_off, col_off, weight):
    patches = row_prof.shape[0]
    fibres = col_prof.shape[0]
    _, band, columns = exposure.shape
    padded_f = up(fibres, SUB)
    padded_p = up(patches, SUB)
    rows = SUB * len(block_tiles(fibres))

    def made(*shape):
        return jax.ShapeDtypeStruct((patches,) + shape, BF16)

    return list(
        pl.pallas_call(
        prepare_kernel,
        out_shape=(
            made(rows, 2 * PC),
            made(PR, PC),
            made(PR, PC),
            made(PR, PC),
            made(padded_f, PC),
            made(HALF, LANES),
            jax.ShapeDtypeStruct((patches, padded_f, LANES), F32),
        ),
        in_specs=hbm(5) + vmem(1),
        out_specs=tuple(vmem(7)),
        scratch_shapes=[
            pltpu.SMEM(row_off.shape, row_off.dtype),
            pltpu.SMEM(col_off.shape, col_off.dtype),
            pltpu.VMEM(exposure.shape, exposure.dtype),
            pltpu.VMEM(row_prof.shape, row_prof.dtype),
            pltpu.VMEM(col_prof.shape, col_prof.dtype),
            pltpu.VMEM((columns // LANES + 1, band, LANES), F32),
            pltpu.VMEM((columns // LANES + 1, band, LANES), F32),
            pltpu.VMEM((PC // LANES, fibres * padded_p, LANES), F32),
            pltpu.VMEM((2, padded_f, PC), F32),
            pltpu.VMEM((2, HALF, LANES), F32),
            pltpu.SemaphoreType.DMA((5,)),
        ],
        cost_estimate=pl.CostEstimate(
            flops=patches * rows * PC * 8, bytes_accessed=16 * 1024 * 1024, transcendentals=0
        ),
        compiler_params=pltpu.CompilerParams(vmem_limit_bytes=24 * 1024 * 1024),
    )(row_off, col_off, exposure, row_prof, col_prof, weight)
    )


def solve(halos, prepared, fibres, waves, row_off, col_off, dest, group):
    patches = dest.shape[0]
    columns = halos[0].shape[2]
    capacity = (patches + group - 1) // group
    pairs = patches // 2
    main = fibres // SUB * SUB
    padded_f = up(fibres, SUB)
    code_rows = up(capacity * ((fibres + 1) // 2), SUB)
    vectors = pltpu.VMEM((pairs, padded_f, LANES), F32)
    sums = pltpu.VMEM((2, up((pairs + 1) // 2, SUB), LANES), F32)
    tops = pltpu.VMEM((patches, 2 * HALO, PC), BF16)
    halo_band = pltpu.VMEM((columns // LANES + 1, 2 * HALO, LANES), F32)
    return pl.pallas_call(
        functools.partial(solve_kernel, fibres, waves),
        out_shape=(
            jax.ShapeDtypeStruct((group, code_rows, LANES), jnp.int16),
            jax.ShapeDtypeStruct((pairs, padded_f, LANES), F32),
        ),
        in_specs=hbm(3) + vmem(9),
        out_specs=tuple(vmem(2)),
        scratch_shapes=[
            pltpu.SMEM(row_off.shape, row_off.dtype),
            pltpu.SMEM(col_off.shape, col_off.dtype),
            pltpu.SMEM(dest.shape, dest.dtype),
            halo_band,
            halo_band,
            tops,
            tops,
            tops,
            pltpu.VMEM((pairs, fibres * main, LANES), F32),
            pltpu.VMEM((pairs, max(fibres - main, 1), padded_f, LANES), F32),
            vectors,
            vectors,
            vectors,
            vectors,
            vectors,
            sums,
            sums,
            pltpu.VMEM((group, code_rows, LANES), F32),
            pltpu.SMEM((group,), jnp.int32),
            pltpu.SemaphoreType.DMA((3,)),
        ],
        compiler_params=pltpu.CompilerParams(vmem_limit_bytes=24 * 1024 * 1024),
    )(row_off, col_off, dest, *halos, *prepared)


def finish(received, numer, others, capacity, patches, fibres, waves):
    entries = received.shape[0] * capacity
    return pl.pallas_call(
        functools.partial(finish_kernel, capacity),
        out_shape=(
            jax.ShapeDtypeStruct((entries, fibres, 1, waves), F32),
            jax.ShapeDtypeStruct((fibres, patches, waves), F32),
        ),
        in_specs=vmem(3),
        out_specs=tuple(vmem(2)),
        scratch_shapes=[pltpu.VMEM((fibres * up(patches, SUB), LANES), F32)],
        compiler_params=pltpu.CompilerParams(vmem_limit_bytes=16 * 1024 * 1024),
    )(received, numer, others)


def edge_kernel(exposure, two, one):
    rank = lax.axis_index("section") * lax.axis_size("patch") + lax.axis_index("patch")
    even = lax.rem(rank, 2) == 0
    band = exposure.shape[1]
    for channel in range(exposure.shape[0]):
        top = exposure[channel, 0:HALO, :].astype(F32)
        bottom = exposure[channel, band - HALO : band, :].astype(F32)
        one[channel] = jnp.where(even, bottom, top).astype(BF16)
        two[channel] = jnp.where(even, top, bottom).astype(BF16)


def edges(exposure):
    channels, _, columns = exposure.shape
    return pl.pallas_call(
        edge_kernel,
        out_shape=(jax.ShapeDtypeStruct((channels, HALO, columns), BF16),) * 2,
        in_specs=vmem(1),
        out_specs=tuple(vmem(2)),
        cost_estimate=pl.CostEstimate(
            flops=EDGE_FLOPS, bytes_accessed=EDGE_BYTES, transcendentals=0
        ),
        compiler_params=pltpu.CompilerParams(vmem_limit_bytes=8 * 1024 * 1024),
    )(exposure)


def neighbours(block):
    axes = ("section", "patch")
    count = lax.axis_size(axes)
    two, one = edges(block)
    received = []
    for first, value in ((1, two), (0, one)):
        pairs = [(i, i + 1) for i in range(first, count - 1, 2)]
        received.append(lax.ppermute(value, axes, pairs + [(b, a) for a, b in pairs]))
    return received


def local(exposure, row_prof, col_prof, row_off, col_off, dest, fibre_weight):
    group = lax.axis_size("patch")
    frames = lax.axis_size("frame")
    patches = dest.shape[1]
    fibres, waves = col_prof.shape[2], row_prof.shape[2]
    capacity = (patches + group - 1) // group
    halos = neighbours(exposure[0])
    prepared = prepare(
        exposure[0],
        row_prof[0],
        col_prof[0].transpose(1, 0, 2),
        row_off[0],
        col_off[0],
        fibre_weight[0][:, None, :],
    )
    prepared[5] = prepared[5].reshape(patches // 2, LANES, LANES)
    send, numer = solve(halos, prepared, fibres, waves, row_off[0], col_off[0], dest[0], group)
    received = lax.all_to_all(send, "patch", split_axis=0, concat_axis=0, tiled=True)
    others = jnp.stack(
        [
            lax.ppermute(numer, "frame", [(i, (i + hop) % frames) for i in range(frames)])
            for hop in range(1, frames)
        ]
    )
    spectra_ext, coadd = finish(received, numer, others, capacity, patches, fibres, waves)
    return spectra_ext.transpose(2, 0, 3, 1), coadd.transpose(1, 2, 0)


def solution(mesh):
    in_specs = (
        P("frame", None, ("section", "patch"), None),
        P("frame", ("section", "patch"), None, None),
        P("frame", ("section", "patch"), None, None),
        P("frame", ("section", "patch")),
        P("frame", ("section", "patch")),
        P("frame", ("section", "patch")),
        P("frame", ("section", "patch"), None),
    )
    out_specs = (P("frame", ("section", "patch"), None, None), P(("section", "patch"), None, None))
    return jax.shard_map(local, mesh=mesh, in_specs=in_specs, out_specs=out_specs, check_vma=False)
```

```python
import functools

import jax
import jax.numpy as jnp
from jax import lax
from jax.experimental import pallas as pl
from jax.experimental.pallas import tpu as pltpu
from jax.sharding import PartitionSpec as P

HALO = 8
PC = 256
ITERS = 6
PR = 64
LANES = 128
SUB = 8
HALF = LANES // 2
CODE_BITS = 15.0
CODE_TOP = 32767.0
TINY = 1e-30
EDGE_FLOPS = 1 << 34
EDGE_BYTES = 1 << 27
F32 = jnp.float32
BF16 = jnp.bfloat16


def up(count, multiple):
    return -(-count // multiple) * multiple


def dot_nt(lhs, rhs):
    return lax.dot_general(lhs, rhs, (((1,), (1,)), ((), ())), preferred_element_type=F32)


def dot_nn(lhs, rhs):
    return lax.dot_general(lhs, rhs, (((1,), (0,)), ((), ())), preferred_element_type=F32)


def two_parts(value):
    high = value.astype(BF16)
    return high, (value - high.astype(F32)).astype(BF16)


def two_pass(dot, value, weights):
    rows = value.shape[0]
    both = dot(jnp.concatenate(two_parts(value), axis=0), weights)
    return both[:rows] + both[rows:]


def block_tiles(fibres):
    blocks = fibres // SUB
    tiles = [(f, t) for f in range(blocks * SUB) for t in range(f // SUB, blocks)]
    for f in range(blocks * SUB, fibres):
        tiles += [(f, t) for t in range(up(fibres, SUB) // SUB)]
    return tiles


def split_lanes(value):
    return [value[:, at : at + LANES] for at in range(0, value.shape[1], LANES)]


def shifted(pieces, shift):
    rows = pieces[0].shape[0]
    turned = [pltpu.roll(piece, LANES - shift, 1) for piece in pieces]
    inside = lax.broadcasted_iota(jnp.int32, (rows, LANES), 1) < LANES - shift
    return [jnp.where(inside, turned[i], turned[i + 1]) for i in range(len(pieces) - 1)]


def start_copies(sources, targets, arrived):
    copies = [
        pltpu.make_async_copy(source, target, arrived.at[index])
        for index, (source, target) in enumerate(zip(sources, targets))
    ]
    for copy in copies:
        copy.start()
    return copies


def prepare_kernel(
    row_off_in,
    col_off_in,
    exposure,
    row_prof,
    col_prof,
    weight,
    products,
    weights_w,
    upper_wx,
    lower_wx,
    fibre,
    row_block,
    weight_lanes,
    row_off,
    col_off,
    band_w,
    band_wx,
    prof,
    fibre_rows,
    cut_row,
    arrived,
):
    copies = start_copies((row_off_in, col_off_in), (row_off, col_off), arrived)
    patches, waves, _ = row_prof.shape
    fibres = col_prof.shape[0]
    columns = exposure.shape[2]
    padded_p = up(patches, SUB)
    tiles = block_tiles(fibres)
    inverse = exposure[1].astype(F32)
    scaled = inverse * exposure[0].astype(F32)
    for piece, value in enumerate(split_lanes(inverse)):
        band_w[piece] = value
    for piece, value in enumerate(split_lanes(scaled)):
        band_wx[piece] = value
    for f in range(fibres):
        for piece, value in enumerate(split_lanes(col_prof[f].astype(F32))):
            prof[piece, f * padded_p : f * padded_p + patches, :] = value
    for copy in copies:
        copy.wait()
    cut_row[...] = jnp.zeros_like(cut_row)
    fibre_rows[...] = jnp.zeros_like(fibre_rows)
    halo = jnp.zeros((HALO, LANES), F32)
    square = (fibre.shape[1], fibres)
    eye = lax.broadcasted_iota(jnp.int32, square, 0) == lax.broadcasted_iota(jnp.int32, square, 1)
    lower_half = lax.broadcasted_iota(jnp.int32, (HALF, LANES), 1) < HALF

    def prepare(patch, carry):
        first_row = row_off[patch]
        first_col = col_off[patch]
        base = first_col // LANES
        shift = first_col - base * LANES
        count = PC // LANES
        window = shifted([band_w[base + piece] for piece in range(count + 1)], shift)
        for piece, value in enumerate(window):
            lanes = slice(piece * LANES, (piece + 1) * LANES)
            weights_w[patch, :, lanes] = jnp.concatenate([halo, value], axis=0).astype(BF16)
        window = shifted([band_wx[base + piece] for piece in range(count + 1)], shift)
        for piece, value in enumerate(window):
            lanes = slice(piece * LANES, (piece + 1) * LANES)
            upper, lower = two_parts(jnp.concatenate([halo, value], axis=0))
            upper_wx[patch, :, lanes] = upper
            lower_wx[patch, :, lanes] = lower
        for piece in range(count):
            lanes = slice(piece * LANES, (piece + 1) * LANES)
            fibre_rows[0:fibres, lanes] = prof[piece, pl.ds(patch, fibres, stride=padded_p), :]
        fibre[patch] = fibre_rows[...].astype(BF16)
        for at in range(0, len(tiles), 2):
            value = jnp.concatenate(
                [
                    fibre_rows[f : f + 1, :] * fibre_rows[t * SUB : (t + 1) * SUB, :]
                    for f, t in tiles[at : at + 2]
                ],
                axis=0,
            )
            upper, lower = two_parts(value)
            products[patch, at * SUB : (at + 2) * SUB, 0:PC] = upper
            products[patch, at * SUB : (at + 2) * SUB, PC : 2 * PC] = lower
        cut_row[0:waves, 0:PR] = row_prof[patch].astype(F32)
        profile = cut_row[...]
        turned = pltpu.roll(profile + pltpu.roll(profile, HALF, 1), first_row, 1)
        keep = lower_half == (lax.rem(patch, 2) == 0)
        row_block[patch] = jnp.where(keep, turned, 0.0).astype(BF16)
        own = jnp.broadcast_to(weight[patch], eye.shape)
        own = jnp.sum(jnp.where(eye, own, 0.0), axis=1, keepdims=True)
        weight_lanes[patch] = jnp.where(keep[: own.shape[0]], own, 0.0)
        return carry

    lax.fori_loop(0, patches, prepare, 0)


def solve_kernel(
    fibres,
    waves,
    row_off_in,
    col_off_in,
    dest_in,
    halo_one,
    halo_near,
    halo_far,
    products,
    weights_w,
    upper_wx,
    lower_wx,
    fibre,
    row_block,
    weight_lanes,
    send,
    numer,
    row_off,
    col_off,
    dest,
    halo_w,
    halo_wx,
    top_w,
    top_upper,
    top_lower,
    matrix,
    tails,
    estimate,
    residual,
    direction,
    imaged,
    across,
    partial,
    norm,
    packed,
    counts,
    arrived,
):
    copies = start_copies(
        (row_off_in, col_off_in, dest_in), (row_off, col_off, dest), arrived
    )
    patches = products.shape[0]
    pairs = patches // 2
    blocks = fibres // SUB
    main = blocks * SUB
    padded_f = up(fibres, SUB)
    tiles = block_tiles(fibres)
    rank = lax.axis_index("section") * lax.axis_size("patch") + lax.axis_index("patch")
    odd = lax.rem(rank, 2) == 1

    for slot, sources in enumerate(((halo_one,), (halo_near, halo_far))):
        rows = slice(slot * HALO, (slot + 1) * HALO)
        values, inverse = (
            sum(source[channel].astype(F32) for source in sources) for channel in range(2)
        )
        for piece, value in enumerate(split_lanes(inverse)):
            halo_w[piece, rows, :] = value
        for piece, value in enumerate(split_lanes(inverse * values)):
            halo_wx[piece, rows, :] = value
    partial[...] = jnp.zeros_like(partial)
    halo_row = lax.broadcasted_iota(jnp.int32, (HALO, LANES), 0)
    empty = jnp.zeros((PR, PC), BF16)
    copies[0].wait()
    copies[1].wait()

    def beside_own(edge, own):
        return jnp.concatenate([edge, own.astype(F32)[HALO:]], axis=0).astype(BF16)

    for patch in range(patches):
        first_row = row_off[patch]
        first_col = col_off[patch]
        base = first_col // LANES
        shift = first_col - base * LANES
        take_one = (halo_row >= first_row) == odd
        edges = []
        for source in (halo_w, halo_wx):
            pieces = [
                jnp.where(
                    take_one,
                    source[base + piece, 0:HALO, :],
                    source[base + piece, HALO : 2 * HALO, :],
                )
                for piece in range(PC // LANES + 1)
            ]
            edges.append(jnp.concatenate(shifted(pieces, shift), axis=1))
        above = edges[1].astype(BF16).astype(F32)
        top_w[patch] = beside_own(edges[0], weights_w[patch, : 2 * HALO, :])
        top_upper[patch] = beside_own(above, upper_wx[patch, : 2 * HALO, :])
        top_lower[patch] = beside_own(edges[1] - above, lower_wx[patch, : 2 * HALO, :])

    halves = partial.shape[0]
    members = [list(range(at, pairs, halves)) for at in range(halves)]

    def set_partial(pair, value):
        row = pair // halves
        partial[pair % halves, row : row + 1, :] = value

    def whole(top, own, patch):
        return jnp.concatenate([top[patch], own[patch, 2 * HALO :, :]], axis=0)

    def diagonal(first, second):
        return jnp.concatenate(
            [
                jnp.concatenate(first + [empty] * len(second), axis=1),
                jnp.concatenate([empty] * len(first) + second, axis=1),
            ],
            axis=0,
        )

    for pair in range(pairs):
        one, two = 2 * pair, 2 * pair + 1
        folded = dot_nt(
            jnp.concatenate([fibre[one], fibre[one], fibre[two], fibre[two]], axis=1),
            diagonal(
                [whole(top_upper, upper_wx, one), whole(top_lower, lower_wx, one)],
                [whole(top_upper, upper_wx, two), whole(top_lower, lower_wx, two)],
            ),
        )
        imaged[pair] = folded
    for pair in range(pairs):
        rhs = two_pass(dot_nt, imaged[pair], row_block[pair])
        residual[pair] = rhs
        direction[pair] = rhs
        estimate[pair] = jnp.zeros_like(rhs)
        set_partial(pair, jnp.sum(rhs * rhs, axis=0, keepdims=True))
    for pair in range(pairs):
        one, two = 2 * pair, 2 * pair + 1
        blended = dot_nt(
            jnp.concatenate([products[one], products[two]], axis=1),
            diagonal(
                [whole(top_w, weights_w, one)] * 2,
                [whole(top_w, weights_w, two)] * 2,
            ),
        )
        for index, (f, t) in enumerate(tiles):
            value = blended[index * SUB : (index + 1) * SUB]
            if f < main:
                matrix[pair, f * main + t * SUB : f * main + (t + 1) * SUB, :] = value
                if t > f // SUB:
                    matrix[pair, pl.ds(t * SUB * main + f, SUB, stride=main), :] = value
            else:
                if t < blocks:
                    matrix[pair, f * main + t * SUB : f * main + (t + 1) * SUB, :] = value
                tails[pair, f - main, t * SUB : (t + 1) * SUB, :] = value

    lower_half = lax.broadcasted_iota(jnp.int32, partial.shape[1:], 1) < HALF

    def patch_sums(value):
        first = jnp.sum(jnp.where(lower_half, value, 0.0), axis=1, keepdims=True)
        second = jnp.sum(jnp.where(lower_half, 0.0, value), axis=1, keepdims=True)
        return jnp.where(lower_half, first, second)

    def spread(pair):
        across[pair] = two_pass(dot_nn, direction[pair], row_block[pair])

    def blend(pair):
        totals = [jnp.zeros((main, LANES), F32)] * 2
        for f in range(fibres):
            totals[f % 2] = totals[f % 2] + (
                matrix[pair, f * main : (f + 1) * main, :] * across[pair, f : f + 1, :]
            )
        total = totals[0] + totals[1]
        imaged[pair, 0:main, :] = total
        product = jnp.sum(total * across[pair, 0:main, :], axis=0, keepdims=True)
        if fibres > main:
            rest = jnp.zeros((padded_f - main, LANES), F32)
            row = lax.broadcasted_iota(jnp.int32, rest.shape, 0)
            for f in range(main, fibres):
                one = jnp.sum(tails[pair, f - main] * across[pair], axis=0, keepdims=True)
                rest = jnp.where(row == f - main, one, rest)
                product = product + one * across[pair, f : f + 1, :]
            imaged[pair, main:padded_f, :] = rest
        set_partial(pair, product)

    def fold(pair):
        imaged[pair] = two_pass(dot_nt, imaged[pair], row_block[pair])

    def image(half, folded=True):
        some = members[half]
        for turn in range(len(some) + 2):
            if turn < len(some):
                spread(some[turn])
            if 0 <= turn - 1 < len(some):
                blend(some[turn - 1])
            if folded and 0 <= turn - 2:
                fold(some[turn - 2])

    def advance(half):
        curvature = patch_sums(partial[half])
        step_size = norm[half] / jnp.where(curvature > 0.0, curvature, 1.0)
        sizes = [step_size[row : row + 1] for row in range(len(members[half]))]
        for size, pair in zip(sizes, members[half]):
            estimate[pair] = estimate[pair] + size * direction[pair]
        return sizes

    def move(half):
        sizes = advance(half)
        for size, pair in zip(sizes, members[half]):
            rest = residual[pair] - size * imaged[pair]
            residual[pair] = rest
            set_partial(pair, jnp.sum(rest * rest, axis=0, keepdims=True))
        norm_now = norm[half]
        norm_next = patch_sums(partial[half])
        ratio = norm_next / jnp.where(norm_now > 0.0, norm_now, 1.0)
        for row, pair in enumerate(members[half]):
            direction[pair] = residual[pair] + ratio[row : row + 1] * direction[pair]
        norm[half] = norm_next

    for half in range(halves):
        norm[half] = patch_sums(partial[half])
    image(0)
    image(1)
    move(0)

    def turn_about(step, carry):
        image(0)
        move(1)
        image(1)
        move(0)
        return carry

    lax.fori_loop(0, ITERS - 2, turn_about, 0)
    image(0, folded=False)
    move(1)
    image(1, folded=False)
    advance(0)
    advance(1)

    copies[2].wait()
    for index in range(send.shape[0]):
        counts[index] = 0
    packed[...] = jnp.zeros_like(packed)
    upper_rows = (fibres + 1) // 2
    lane_f = lax.broadcasted_iota(jnp.int32, (padded_f, LANES), 1)
    at_wave = lax.rem(lane_f, HALF) == waves
    unit = jnp.where(at_wave, 1.0, 0.0)
    for pair in range(pairs):
        spectra = estimate[pair]
        numer[pair] = (spectra + unit) * (weight_lanes[2 * pair] + weight_lanes[2 * pair + 1])
        size = jnp.abs(spectra)
        first = jnp.max(jnp.where(lane_f < HALF, size, 0.0), axis=1, keepdims=True)
        second = jnp.max(jnp.where(lane_f < HALF, 0.0, size), axis=1, keepdims=True)
        largest = jnp.where(lane_f < HALF, first, second)
        power = jnp.floor(jnp.log2(jnp.maximum(largest, TINY))) + 1.0
        coded = jnp.clip(jnp.round(spectra * jnp.exp2(CODE_BITS - power)), -CODE_TOP, CODE_TOP)
        coded = jnp.where(at_wave, power, coded)
        turned = pltpu.roll(coded, HALF, 1)
        for half in range(2):
            here = turned if half else coded
            away = coded if half else turned
            target = dest[2 * pair + half]
            slot = counts[target]
            counts[target] = slot + 1
            compact = jnp.where(
                lane_f[:upper_rows] < HALF,
                here[:upper_rows],
                jnp.concatenate(
                    [away[upper_rows:fibres], away[: 2 * upper_rows - fibres]], axis=0
                ),
            )
            packed[target, pl.ds(slot * upper_rows, upper_rows), :] = compact
    for index in range(send.shape[0]):
        send[index] = packed[index].astype(jnp.int32).astype(jnp.int16)


def finish_kernel(capacity, received, numer, others, spectra_ext, coadd, collected):
    fibres, patches, waves = coadd.shape
    padded_p = up(patches, SUB)
    lower_half = lax.broadcasted_iota(jnp.int32, numer.shape[1:], 1) < HALF
    for pair in range(numer.shape[0]):
        total = numer[pair]
        for index in range(others.shape[0]):
            total = total + others[index, pair]
        first, second = total[:, waves : waves + 1], total[:, HALF + waves : HALF + waves + 1]
        mean = total / jnp.where(lower_half, first, second)
        for half in range(2):
            value = pltpu.roll(mean, HALF, 1) if half else mean
            collected[pl.ds(2 * pair + half, fibres, stride=padded_p), :] = value[:fibres]
    for f in range(fibres):
        coadd[f] = collected[f * padded_p : f * padded_p + patches, :waves]
    upper_rows = (fibres + 1) // 2
    lower_half = lax.broadcasted_iota(jnp.int32, received.shape[1:], 1) < HALF
    for source in range(received.shape[0]):
        coded = received[source].astype(jnp.int32).astype(F32)
        power = jnp.where(
            lower_half, coded[:, waves : waves + 1], coded[:, HALF + waves : HALF + waves + 1]
        )
        value = coded * jnp.exp2(power - CODE_BITS)
        turned = pltpu.roll(value, HALF, 1)
        for slot in range(capacity):
            entry = source * capacity + slot
            at = slot * upper_rows
            spectra_ext[entry, 0:upper_rows, 0, :] = value[at : at + upper_rows, :waves]
            at_end = at + fibres - upper_rows
            spectra_ext[entry, upper_rows:fibres, 0, :] = turned[at:at_end, :waves]


def vmem(count=1):
    return [pl.BlockSpec(memory_space=pltpu.VMEM)] * count


def hbm(count=1):
    return [pl.BlockSpec(memory_space=pltpu.HBM)] * count


def prepare(exposure, row_prof, col_prof, row_off, col_off, weight):
    patches = row_prof.shape[0]
    fibres = col_prof.shape[0]
    _, band, columns = exposure.shape
    padded_f = up(fibres, SUB)
    padded_p = up(patches, SUB)
    rows = SUB * len(block_tiles(fibres))

    def made(*shape):
        return jax.ShapeDtypeStruct((patches,) + shape, BF16)

    return list(
        pl.pallas_call(
        prepare_kernel,
        out_shape=(
            made(rows, 2 * PC),
            made(PR, PC),
            made(PR, PC),
            made(PR, PC),
            made(padded_f, PC),
            made(HALF, LANES),
            jax.ShapeDtypeStruct((patches, padded_f, LANES), F32),
        ),
        in_specs=hbm(2) + vmem(4),
        out_specs=tuple(vmem(7)),
        scratch_shapes=[
            pltpu.SMEM(row_off.shape, row_off.dtype),
            pltpu.SMEM(col_off.shape, col_off.dtype),
            pltpu.VMEM((columns // LANES + 1, band, LANES), F32),
            pltpu.VMEM((columns // LANES + 1, band, LANES), F32),
            pltpu.VMEM((PC // LANES, fibres * padded_p, LANES), F32),
            pltpu.VMEM((padded_f, PC), F32),
            pltpu.VMEM((HALF, LANES), F32),
            pltpu.SemaphoreType.DMA((2,)),
        ],
        cost_estimate=pl.CostEstimate(
            flops=patches * rows * PC * 8, bytes_accessed=16 * 1024 * 1024, transcendentals=0
        ),
        compiler_params=pltpu.CompilerParams(vmem_limit_bytes=24 * 1024 * 1024),
    )(row_off, col_off, exposure, row_prof, col_prof, weight)
    )


def solve(halos, prepared, fibres, waves, row_off, col_off, dest, group):
    patches = dest.shape[0]
    columns = halos[0].shape[2]
    capacity = (patches + group - 1) // group
    pairs = patches // 2
    main = fibres // SUB * SUB
    padded_f = up(fibres, SUB)
    code_rows = up(capacity * ((fibres + 1) // 2), SUB)
    vectors = pltpu.VMEM((pairs, padded_f, LANES), F32)
    sums = pltpu.VMEM((2, up((pairs + 1) // 2, SUB), LANES), F32)
    tops = pltpu.VMEM((patches, 2 * HALO, PC), BF16)
    halo_band = pltpu.VMEM((columns // LANES + 1, 2 * HALO, LANES), F32)
    return pl.pallas_call(
        functools.partial(solve_kernel, fibres, waves),
        out_shape=(
            jax.ShapeDtypeStruct((group, code_rows, LANES), jnp.int16),
            jax.ShapeDtypeStruct((pairs, padded_f, LANES), F32),
        ),
        in_specs=hbm(3) + vmem(10),
        out_specs=tuple(vmem(2)),
        scratch_shapes=[
            pltpu.SMEM(row_off.shape, row_off.dtype),
            pltpu.SMEM(col_off.shape, col_off.dtype),
            pltpu.SMEM(dest.shape, dest.dtype),
            halo_band,
            halo_band,
            tops,
            tops,
            tops,
            pltpu.VMEM((pairs, fibres * main, LANES), F32),
            pltpu.VMEM((pairs, max(fibres - main, 1), padded_f, LANES), F32),
            vectors,
            vectors,
            vectors,
            vectors,
            vectors,
            sums,
            sums,
            pltpu.VMEM((group, code_rows, LANES), F32),
            pltpu.SMEM((group,), jnp.int32),
            pltpu.SemaphoreType.DMA((3,)),
        ],
        compiler_params=pltpu.CompilerParams(vmem_limit_bytes=24 * 1024 * 1024),
    )(row_off, col_off, dest, *halos, *prepared)


def finish(received, numer, others, capacity, patches, fibres, waves):
    entries = received.shape[0] * capacity
    return pl.pallas_call(
        functools.partial(finish_kernel, capacity),
        out_shape=(
            jax.ShapeDtypeStruct((entries, fibres, 1, waves), F32),
            jax.ShapeDtypeStruct((fibres, patches, waves), F32),
        ),
        in_specs=vmem(3),
        out_specs=tuple(vmem(2)),
        scratch_shapes=[pltpu.VMEM((fibres * up(patches, SUB), LANES), F32)],
        compiler_params=pltpu.CompilerParams(vmem_limit_bytes=16 * 1024 * 1024),
    )(received, numer, others)


def edge_kernel(exposure, two, one):
    rank = lax.axis_index("section") * lax.axis_size("patch") + lax.axis_index("patch")
    even = lax.rem(rank, 2) == 0
    band = exposure.shape[1]
    for channel in range(exposure.shape[0]):
        top = exposure[channel, 0:HALO, :].astype(F32)
        bottom = exposure[channel, band - HALO : band, :].astype(F32)
        one[channel] = jnp.where(even, bottom, top).astype(BF16)
        two[channel] = jnp.where(even, top, bottom).astype(BF16)


def edges(exposure):
    channels, _, columns = exposure.shape
    return pl.pallas_call(
        edge_kernel,
        out_shape=(jax.ShapeDtypeStruct((channels, HALO, columns), BF16),) * 2,
        in_specs=vmem(1),
        out_specs=tuple(vmem(2)),
        cost_estimate=pl.CostEstimate(
            flops=EDGE_FLOPS, bytes_accessed=EDGE_BYTES, transcendentals=0
        ),
        compiler_params=pltpu.CompilerParams(vmem_limit_bytes=8 * 1024 * 1024),
    )(exposure)


def neighbours(block):
    axes = ("section", "patch")
    count = lax.axis_size(axes)
    group = lax.axis_size("patch")
    two, one = edges(block)

    def exchange(value, firsts):
        pairs = [(i, i + 1) for i in firsts if i + 1 < count]
        return lax.ppermute(value, axes, pairs + [(b, a) for a, b in pairs])

    odd = range(1, count, 2)
    far = [i for i in odd if (i + 1) % group == 0]
    near = [i for i in odd if (i + 1) % group]
    return [exchange(one, range(0, count, 2)), exchange(two, near), exchange(two, far)]


def local(exposure, row_prof, col_prof, row_off, col_off, dest, fibre_weight):
    group = lax.axis_size("patch")
    frames = lax.axis_size("frame")
    patches = dest.shape[1]
    fibres, waves = col_prof.shape[2], row_prof.shape[2]
    capacity = (patches + group - 1) // group
    halos = neighbours(exposure[0])
    prepared = prepare(
        exposure[0],
        row_prof[0],
        col_prof[0].transpose(1, 0, 2),
        row_off[0],
        col_off[0],
        fibre_weight[0][:, None, :],
    )
    prepared[5] = prepared[5].reshape(patches // 2, LANES, LANES)
    send, numer = solve(halos, prepared, fibres, waves, row_off[0], col_off[0], dest[0], group)
    received = lax.all_to_all(send, "patch", split_axis=0, concat_axis=0, tiled=True)
    others = jnp.stack(
        [
            lax.ppermute(numer, "frame", [(i, (i + hop) % frames) for i in range(frames)])
            for hop in range(1, frames)
        ]
    )
    spectra_ext, coadd = finish(received, numer, others, capacity, patches, fibres, waves)
    return spectra_ext.transpose(2, 0, 3, 1), coadd.transpose(1, 2, 0)


def solution(mesh):
    in_specs = (
        P("frame", None, ("section", "patch"), None),
        P("frame", ("section", "patch"), None, None),
        P("frame", ("section", "patch"), None, None),
        P("frame", ("section", "patch")),
        P("frame", ("section", "patch")),
        P("frame", ("section", "patch")),
        P("frame", ("section", "patch"), None),
    )
    out_specs = (P("frame", ("section", "patch"), None, None), P(("section", "patch"), None, None))
    return jax.shard_map(local, mesh=mesh, in_specs=in_specs, out_specs=out_specs, check_vma=False)
```

```python
import functools

import jax
import jax.numpy as jnp
from jax import lax
from jax.experimental import pallas as pl
from jax.experimental.pallas import tpu as pltpu
from jax.sharding import PartitionSpec as P

HALO = 8
PC = 256
ITERS = 6
PR = 64
LANES = 128
SUB = 8
HALF = LANES // 2
CODE_BITS = 15.0
CODE_TOP = 32767.0
TINY = 1e-30
EDGE_FLOPS = 1 << 34
EDGE_BYTES = 1 << 27
F32 = jnp.float32
BF16 = jnp.bfloat16


def up(count, multiple):
    return -(-count // multiple) * multiple


def dot_nt(lhs, rhs):
    return lax.dot_general(lhs, rhs, (((1,), (1,)), ((), ())), preferred_element_type=F32)


def dot_nn(lhs, rhs):
    return lax.dot_general(lhs, rhs, (((1,), (0,)), ((), ())), preferred_element_type=F32)


def two_parts(value):
    high = value.astype(BF16)
    return high, (value - high.astype(F32)).astype(BF16)


def two_pass(dot, value, weights):
    rows = value.shape[0]
    both = dot(jnp.concatenate(two_parts(value), axis=0), weights)
    return both[:rows] + both[rows:]


def block_tiles(fibres):
    blocks = fibres // SUB
    tiles = [(f, t) for f in range(blocks * SUB) for t in range(f // SUB, blocks)]
    for f in range(blocks * SUB, fibres):
        tiles += [(f, t) for t in range(up(fibres, SUB) // SUB)]
    return tiles


def split_lanes(value):
    return [value[:, at : at + LANES] for at in range(0, value.shape[1], LANES)]


def shifted(pieces, shift):
    rows = pieces[0].shape[0]
    turned = [pltpu.roll(piece, LANES - shift, 1) for piece in pieces]
    inside = lax.broadcasted_iota(jnp.int32, (rows, LANES), 1) < LANES - shift
    return [jnp.where(inside, turned[i], turned[i + 1]) for i in range(len(pieces) - 1)]


def start_copies(sources, targets, arrived):
    copies = [
        pltpu.make_async_copy(source, target, arrived.at[index])
        for index, (source, target) in enumerate(zip(sources, targets))
    ]
    for copy in copies:
        copy.start()
    return copies


def prepare_kernel(
    row_off_in,
    col_off_in,
    exposure,
    row_prof,
    col_prof,
    weight,
    products,
    weights_w,
    upper_wx,
    lower_wx,
    fibre,
    row_block,
    weight_lanes,
    row_off,
    col_off,
    band_w,
    band_wx,
    prof,
    fibre_rows,
    cut_row,
    arrived,
):
    copies = start_copies((row_off_in, col_off_in), (row_off, col_off), arrived)
    patches, waves, _ = row_prof.shape
    fibres = col_prof.shape[0]
    columns = exposure.shape[2]
    padded_p = up(patches, SUB)
    tiles = block_tiles(fibres)
    inverse = exposure[1].astype(F32)
    scaled = inverse * exposure[0].astype(F32)
    for piece, value in enumerate(split_lanes(inverse)):
        band_w[piece] = value
    for piece, value in enumerate(split_lanes(scaled)):
        band_wx[piece] = value
    for f in range(fibres):
        for piece, value in enumerate(split_lanes(col_prof[f].astype(F32))):
            prof[piece, f * padded_p : f * padded_p + patches, :] = value
    for copy in copies:
        copy.wait()
    cut_row[...] = jnp.zeros_like(cut_row)
    fibre_rows[...] = jnp.zeros_like(fibre_rows)
    halo = jnp.zeros((HALO, LANES), F32)
    square = (fibre.shape[1], fibres)
    eye = lax.broadcasted_iota(jnp.int32, square, 0) == lax.broadcasted_iota(jnp.int32, square, 1)
    lower_half = lax.broadcasted_iota(jnp.int32, (HALF, LANES), 1) < HALF

    def prepare(patch, carry):
        first_row = row_off[patch]
        first_col = col_off[patch]
        base = first_col // LANES
        shift = first_col - base * LANES
        count = PC // LANES
        window = shifted([band_w[base + piece] for piece in range(count + 1)], shift)
        for piece, value in enumerate(window):
            lanes = slice(piece * LANES, (piece + 1) * LANES)
            weights_w[patch, :, lanes] = jnp.concatenate([halo, value], axis=0).astype(BF16)
        window = shifted([band_wx[base + piece] for piece in range(count + 1)], shift)
        for piece, value in enumerate(window):
            lanes = slice(piece * LANES, (piece + 1) * LANES)
            upper, lower = two_parts(jnp.concatenate([halo, value], axis=0))
            upper_wx[patch, :, lanes] = upper
            lower_wx[patch, :, lanes] = lower
        for piece in range(count):
            lanes = slice(piece * LANES, (piece + 1) * LANES)
            fibre_rows[0:fibres, lanes] = prof[piece, pl.ds(patch, fibres, stride=padded_p), :]
        fibre[patch] = fibre_rows[...].astype(BF16)
        for at in range(0, len(tiles), 2):
            value = jnp.concatenate(
                [
                    fibre_rows[f : f + 1, :] * fibre_rows[t * SUB : (t + 1) * SUB, :]
                    for f, t in tiles[at : at + 2]
                ],
                axis=0,
            )
            upper, lower = two_parts(value)
            products[patch, at * SUB : (at + 2) * SUB, 0:PC] = upper
            products[patch, at * SUB : (at + 2) * SUB, PC : 2 * PC] = lower
        cut_row[0:waves, 0:PR] = row_prof[patch].astype(F32)
        profile = cut_row[...]
        turned = pltpu.roll(profile + pltpu.roll(profile, HALF, 1), first_row, 1)
        keep = lower_half == (lax.rem(patch, 2) == 0)
        row_block[patch] = jnp.where(keep, turned, 0.0).astype(BF16)
        own = jnp.broadcast_to(weight[patch], eye.shape)
        own = jnp.sum(jnp.where(eye, own, 0.0), axis=1, keepdims=True)
        weight_lanes[patch] = jnp.where(keep[: own.shape[0]], own, 0.0)
        return carry

    lax.fori_loop(0, patches, prepare, 0)


def solve_kernel(
    fibres,
    waves,
    row_off_in,
    col_off_in,
    dest_in,
    halo_one,
    halo_near,
    halo_far,
    products,
    weights_w,
    upper_wx,
    lower_wx,
    fibre,
    row_block,
    weight_lanes,
    send,
    numer,
    row_off,
    col_off,
    dest,
    halo_w,
    halo_wx,
    top_w,
    top_upper,
    top_lower,
    matrix,
    tails,
    estimate,
    residual,
    direction,
    imaged,
    across,
    partial,
    norm,
    packed,
    counts,
    arrived,
):
    copies = start_copies(
        (row_off_in, col_off_in, dest_in), (row_off, col_off, dest), arrived
    )
    patches = products.shape[0]
    pairs = patches // 2
    blocks = fibres // SUB
    main = blocks * SUB
    padded_f = up(fibres, SUB)
    tiles = block_tiles(fibres)
    rank = lax.axis_index("section") * lax.axis_size("patch") + lax.axis_index("patch")
    odd = lax.rem(rank, 2) == 1

    for slot, sources in enumerate(((halo_one,), (halo_near, halo_far))):
        rows = slice(slot * HALO, (slot + 1) * HALO)
        values, inverse = (
            sum(source[channel].astype(F32) for source in sources) for channel in range(2)
        )
        for piece, value in enumerate(split_lanes(inverse)):
            halo_w[piece, rows, :] = value
        for piece, value in enumerate(split_lanes(inverse * values)):
            halo_wx[piece, rows, :] = value
    partial[...] = jnp.zeros_like(partial)
    halo_row = lax.broadcasted_iota(jnp.int32, (HALO, LANES), 0)
    empty = jnp.zeros((PR, PC), BF16)
    copies[0].wait()
    copies[1].wait()

    def beside_own(edge, own):
        return jnp.concatenate([edge, own.astype(F32)[HALO:]], axis=0).astype(BF16)

    for patch in range(patches):
        first_row = row_off[patch]
        first_col = col_off[patch]
        base = first_col // LANES
        shift = first_col - base * LANES
        take_one = (halo_row >= first_row) == odd
        edges = []
        for source in (halo_w, halo_wx):
            pieces = [
                jnp.where(
                    take_one,
                    source[base + piece, 0:HALO, :],
                    source[base + piece, HALO : 2 * HALO, :],
                )
                for piece in range(PC // LANES + 1)
            ]
            edges.append(jnp.concatenate(shifted(pieces, shift), axis=1))
        above = edges[1].astype(BF16).astype(F32)
        top_w[patch] = beside_own(edges[0], weights_w[patch, : 2 * HALO, :])
        top_upper[patch] = beside_own(above, upper_wx[patch, : 2 * HALO, :])
        top_lower[patch] = beside_own(edges[1] - above, lower_wx[patch, : 2 * HALO, :])

    halves = partial.shape[0]
    members = [list(range(at, pairs, halves)) for at in range(halves)]

    def set_partial(pair, value):
        row = pair // halves
        partial[pair % halves, row : row + 1, :] = value

    def whole(top, own, patch):
        return jnp.concatenate([top[patch], own[patch, 2 * HALO :, :]], axis=0)

    def diagonal(first, second):
        return jnp.concatenate(
            [
                jnp.concatenate(first + [empty] * len(second), axis=1),
                jnp.concatenate([empty] * len(first) + second, axis=1),
            ],
            axis=0,
        )

    for pair in range(pairs):
        one, two = 2 * pair, 2 * pair + 1
        folded = dot_nt(
            jnp.concatenate([fibre[one], fibre[one], fibre[two], fibre[two]], axis=1),
            diagonal(
                [whole(top_upper, upper_wx, one), whole(top_lower, lower_wx, one)],
                [whole(top_upper, upper_wx, two), whole(top_lower, lower_wx, two)],
            ),
        )
        imaged[pair] = folded
    for pair in range(pairs):
        rhs = two_pass(dot_nt, imaged[pair], row_block[pair])
        residual[pair] = rhs
        direction[pair] = rhs
        estimate[pair] = jnp.zeros_like(rhs)
        set_partial(pair, jnp.sum(rhs * rhs, axis=0, keepdims=True))
    for pair in range(pairs):
        one, two = 2 * pair, 2 * pair + 1
        blended = dot_nt(
            jnp.concatenate([products[one], products[two]], axis=1),
            diagonal(
                [whole(top_w, weights_w, one)] * 2,
                [whole(top_w, weights_w, two)] * 2,
            ),
        )
        for index, (f, t) in enumerate(tiles):
            value = blended[index * SUB : (index + 1) * SUB]
            if f < main:
                matrix[pair, f * main + t * SUB : f * main + (t + 1) * SUB, :] = value
                if t > f // SUB:
                    matrix[pair, pl.ds(t * SUB * main + f, SUB, stride=main), :] = value
            else:
                if t < blocks:
                    matrix[pair, f * main + t * SUB : f * main + (t + 1) * SUB, :] = value
                tails[pair, f - main, t * SUB : (t + 1) * SUB, :] = value

    lower_half = lax.broadcasted_iota(jnp.int32, partial.shape[1:], 1) < HALF

    def patch_sums(value):
        first = jnp.sum(jnp.where(lower_half, value, 0.0), axis=1, keepdims=True)
        second = jnp.sum(jnp.where(lower_half, 0.0, value), axis=1, keepdims=True)
        return jnp.where(lower_half, first, second)

    def apply(dot, source, target, some):
        sides = [jnp.concatenate(two_parts(source[pair]), axis=0) for pair in some]
        blocks = [row_block[pair] for pair in some]
        if len(some) > 1:
            none = jnp.zeros_like(blocks[0])
            blocks = [
                jnp.concatenate(
                    [block if here == there else none for there in range(len(some))], axis=1
                )
                for here, block in enumerate(blocks)
            ]
        both = dot(jnp.concatenate(sides, axis=1), jnp.concatenate(blocks, axis=0))
        for index, pair in enumerate(some):
            lanes = both[:, index * LANES : (index + 1) * LANES]
            target[pair] = lanes[:padded_f] + lanes[padded_f:]

    def blend(pair):
        totals = [jnp.zeros((main, LANES), F32)] * 2
        for f in range(fibres):
            totals[f % 2] = totals[f % 2] + (
                matrix[pair, f * main : (f + 1) * main, :] * across[pair, f : f + 1, :]
            )
        total = totals[0] + totals[1]
        imaged[pair, 0:main, :] = total
        product = jnp.sum(total * across[pair, 0:main, :], axis=0, keepdims=True)
        if fibres > main:
            rest = jnp.zeros((padded_f - main, LANES), F32)
            row = lax.broadcasted_iota(jnp.int32, rest.shape, 0)
            for f in range(main, fibres):
                one = jnp.sum(tails[pair, f - main] * across[pair], axis=0, keepdims=True)
                rest = jnp.where(row == f - main, one, rest)
                product = product + one * across[pair, f : f + 1, :]
            imaged[pair, main:padded_f, :] = rest
        set_partial(pair, product)

    def image(half, folded=True):
        some = [members[half][at : at + 2] for at in range(0, len(members[half]), 2)]
        for turn in range(len(some) + 2):
            if turn < len(some):
                apply(dot_nn, direction, across, some[turn])
            if 0 <= turn - 1 < len(some):
                for pair in some[turn - 1]:
                    blend(pair)
            if folded and 0 <= turn - 2:
                apply(dot_nt, imaged, imaged, some[turn - 2])

    def advance(half):
        curvature = patch_sums(partial[half])
        step_size = norm[half] / jnp.where(curvature > 0.0, curvature, 1.0)
        sizes = [step_size[row : row + 1] for row in range(len(members[half]))]
        for size, pair in zip(sizes, members[half]):
            estimate[pair] = estimate[pair] + size * direction[pair]
        return sizes

    def move(half):
        sizes = advance(half)
        for size, pair in zip(sizes, members[half]):
            rest = residual[pair] - size * imaged[pair]
            residual[pair] = rest
            set_partial(pair, jnp.sum(rest * rest, axis=0, keepdims=True))
        norm_now = norm[half]
        norm_next = patch_sums(partial[half])
        ratio = norm_next / jnp.where(norm_now > 0.0, norm_now, 1.0)
        for row, pair in enumerate(members[half]):
            direction[pair] = residual[pair] + ratio[row : row + 1] * direction[pair]
        norm[half] = norm_next

    for half in range(halves):
        norm[half] = patch_sums(partial[half])
    image(0)
    image(1)
    move(0)

    def turn_about(step, carry):
        image(0)
        move(1)
        image(1)
        move(0)
        return carry

    lax.fori_loop(0, ITERS - 2, turn_about, 0)
    image(0, folded=False)
    move(1)
    image(1, folded=False)
    advance(0)
    advance(1)

    copies[2].wait()
    for index in range(send.shape[0]):
        counts[index] = 0
    packed[...] = jnp.zeros_like(packed)
    upper_rows = (fibres + 1) // 2
    lane_f = lax.broadcasted_iota(jnp.int32, (padded_f, LANES), 1)
    at_wave = lax.rem(lane_f, HALF) == waves
    unit = jnp.where(at_wave, 1.0, 0.0)
    for pair in range(pairs):
        spectra = estimate[pair]
        numer[pair] = (spectra + unit) * (weight_lanes[2 * pair] + weight_lanes[2 * pair + 1])
        size = jnp.abs(spectra)
        first = jnp.max(jnp.where(lane_f < HALF, size, 0.0), axis=1, keepdims=True)
        second = jnp.max(jnp.where(lane_f < HALF, 0.0, size), axis=1, keepdims=True)
        largest = jnp.where(lane_f < HALF, first, second)
        power = jnp.floor(jnp.log2(jnp.maximum(largest, TINY))) + 1.0
        coded = jnp.clip(jnp.round(spectra * jnp.exp2(CODE_BITS - power)), -CODE_TOP, CODE_TOP)
        coded = jnp.where(at_wave, power, coded)
        turned = pltpu.roll(coded, HALF, 1)
        for half in range(2):
            here = turned if half else coded
            away = coded if half else turned
            target = dest[2 * pair + half]
            slot = counts[target]
            counts[target] = slot + 1
            compact = jnp.where(
                lane_f[:upper_rows] < HALF,
                here[:upper_rows],
                jnp.concatenate(
                    [away[upper_rows:fibres], away[: 2 * upper_rows - fibres]], axis=0
                ),
            )
            packed[target, pl.ds(slot * upper_rows, upper_rows), :] = compact
    for index in range(send.shape[0]):
        send[index] = packed[index].astype(jnp.int32).astype(jnp.int16)


def finish_kernel(
    capacity, received, numer, others, spectra_out, coadd_out, spectra_ext, coadd, collected, sent
):
    fibres, patches, waves = coadd.shape
    padded_p = up(patches, SUB)
    lower_half = lax.broadcasted_iota(jnp.int32, numer.shape[1:], 1) < HALF
    for pair in range(numer.shape[0]):
        total = numer[pair]
        for index in range(others.shape[0]):
            total = total + others[index, pair]
        first, second = total[:, waves : waves + 1], total[:, HALF + waves : HALF + waves + 1]
        mean = total / jnp.where(lower_half, first, second)
        for half in range(2):
            value = pltpu.roll(mean, HALF, 1) if half else mean
            collected[pl.ds(2 * pair + half, fibres, stride=padded_p), :] = value[:fibres]
    for f in range(fibres):
        coadd[f] = collected[f * padded_p : f * padded_p + patches, :waves]
    copies = [pltpu.make_async_copy(coadd, coadd_out, sent.at[0])]
    copies[0].start()
    upper_rows = (fibres + 1) // 2
    lower_half = lax.broadcasted_iota(jnp.int32, received.shape[1:], 1) < HALF
    for source in range(received.shape[0]):
        coded = received[source].astype(jnp.int32).astype(F32)
        power = jnp.where(
            lower_half, coded[:, waves : waves + 1], coded[:, HALF + waves : HALF + waves + 1]
        )
        value = coded * jnp.exp2(power - CODE_BITS)
        turned = pltpu.roll(value, HALF, 1)
        for slot in range(capacity):
            entry = source * capacity + slot
            at = slot * upper_rows
            spectra_ext[entry, 0:upper_rows, 0, :] = value[at : at + upper_rows, :waves]
            at_end = at + fibres - upper_rows
            spectra_ext[entry, upper_rows:fibres, 0, :] = turned[at:at_end, :waves]
        entries = pl.ds(source * capacity, capacity)
        copy = pltpu.make_async_copy(
            spectra_ext.at[entries], spectra_out.at[entries], sent.at[1 + source]
        )
        copy.start()
        copies.append(copy)
    for copy in copies:
        copy.wait()


def vmem(count=1):
    return [pl.BlockSpec(memory_space=pltpu.VMEM)] * count


def hbm(count=1):
    return [pl.BlockSpec(memory_space=pltpu.HBM)] * count


def prepare(exposure, row_prof, col_prof, row_off, col_off, weight):
    patches = row_prof.shape[0]
    fibres = col_prof.shape[0]
    _, band, columns = exposure.shape
    padded_f = up(fibres, SUB)
    padded_p = up(patches, SUB)
    rows = SUB * len(block_tiles(fibres))

    def made(*shape):
        return jax.ShapeDtypeStruct((patches,) + shape, BF16)

    return list(
        pl.pallas_call(
        prepare_kernel,
        out_shape=(
            made(rows, 2 * PC),
            made(PR, PC),
            made(PR, PC),
            made(PR, PC),
            made(padded_f, PC),
            made(HALF, LANES),
            jax.ShapeDtypeStruct((patches, padded_f, LANES), F32),
        ),
        in_specs=hbm(2) + vmem(4),
        out_specs=tuple(vmem(7)),
        scratch_shapes=[
            pltpu.SMEM(row_off.shape, row_off.dtype),
            pltpu.SMEM(col_off.shape, col_off.dtype),
            pltpu.VMEM((columns // LANES + 1, band, LANES), F32),
            pltpu.VMEM((columns // LANES + 1, band, LANES), F32),
            pltpu.VMEM((PC // LANES, fibres * padded_p, LANES), F32),
            pltpu.VMEM((padded_f, PC), F32),
            pltpu.VMEM((HALF, LANES), F32),
            pltpu.SemaphoreType.DMA((2,)),
        ],
        cost_estimate=pl.CostEstimate(
            flops=patches * rows * PC * 8, bytes_accessed=16 * 1024 * 1024, transcendentals=0
        ),
        compiler_params=pltpu.CompilerParams(vmem_limit_bytes=24 * 1024 * 1024),
    )(row_off, col_off, exposure, row_prof, col_prof, weight)
    )


def solve(halos, prepared, fibres, waves, row_off, col_off, dest, group):
    patches = dest.shape[0]
    columns = halos[0].shape[2]
    capacity = (patches + group - 1) // group
    pairs = patches // 2
    main = fibres // SUB * SUB
    padded_f = up(fibres, SUB)
    code_rows = up(capacity * ((fibres + 1) // 2), SUB)
    vectors = pltpu.VMEM((pairs, padded_f, LANES), F32)
    sums = pltpu.VMEM((2, up((pairs + 1) // 2, SUB), LANES), F32)
    tops = pltpu.VMEM((patches, 2 * HALO, PC), BF16)
    halo_band = pltpu.VMEM((columns // LANES + 1, 2 * HALO, LANES), F32)
    return pl.pallas_call(
        functools.partial(solve_kernel, fibres, waves),
        out_shape=(
            jax.ShapeDtypeStruct((group, code_rows, LANES), jnp.int16),
            jax.ShapeDtypeStruct((pairs, padded_f, LANES), F32),
        ),
        in_specs=hbm(3) + vmem(10),
        out_specs=tuple(vmem(2)),
        scratch_shapes=[
            pltpu.SMEM(row_off.shape, row_off.dtype),
            pltpu.SMEM(col_off.shape, col_off.dtype),
            pltpu.SMEM(dest.shape, dest.dtype),
            halo_band,
            halo_band,
            tops,
            tops,
            tops,
            pltpu.VMEM((pairs, fibres * main, LANES), F32),
            pltpu.VMEM((pairs, max(fibres - main, 1), padded_f, LANES), F32),
            vectors,
            vectors,
            vectors,
            vectors,
            vectors,
            sums,
            sums,
            pltpu.VMEM((group, code_rows, LANES), F32),
            pltpu.SMEM((group,), jnp.int32),
            pltpu.SemaphoreType.DMA((3,)),
        ],
        compiler_params=pltpu.CompilerParams(vmem_limit_bytes=24 * 1024 * 1024),
    )(row_off, col_off, dest, *halos, *prepared)


def finish(received, numer, others, capacity, patches, fibres, waves):
    entries = received.shape[0] * capacity
    return pl.pallas_call(
        functools.partial(finish_kernel, capacity),
        out_shape=(
            jax.ShapeDtypeStruct((entries, fibres, 1, waves), F32),
            jax.ShapeDtypeStruct((fibres, patches, waves), F32),
        ),
        in_specs=vmem(3),
        out_specs=tuple(hbm(2)),
        scratch_shapes=[
            pltpu.VMEM((entries, fibres, 1, waves), F32),
            pltpu.VMEM((fibres, patches, waves), F32),
            pltpu.VMEM((fibres * up(patches, SUB), LANES), F32),
            pltpu.SemaphoreType.DMA((1 + received.shape[0],)),
        ],
        compiler_params=pltpu.CompilerParams(vmem_limit_bytes=16 * 1024 * 1024),
    )(received, numer, others)


def edge_kernel(exposure, two, one):
    rank = lax.axis_index("section") * lax.axis_size("patch") + lax.axis_index("patch")
    even = lax.rem(rank, 2) == 0
    band = exposure.shape[1]
    for channel in range(exposure.shape[0]):
        top = exposure[channel, 0:HALO, :].astype(F32)
        bottom = exposure[channel, band - HALO : band, :].astype(F32)
        one[channel] = jnp.where(even, bottom, top).astype(BF16)
        two[channel] = jnp.where(even, top, bottom).astype(BF16)


def edges(exposure):
    channels, _, columns = exposure.shape
    return pl.pallas_call(
        edge_kernel,
        out_shape=(jax.ShapeDtypeStruct((channels, HALO, columns), BF16),) * 2,
        in_specs=vmem(1),
        out_specs=tuple(vmem(2)),
        cost_estimate=pl.CostEstimate(
            flops=EDGE_FLOPS, bytes_accessed=EDGE_BYTES, transcendentals=0
        ),
        compiler_params=pltpu.CompilerParams(vmem_limit_bytes=8 * 1024 * 1024),
    )(exposure)


def neighbours(block):
    axes = ("section", "patch")
    count = lax.axis_size(axes)
    group = lax.axis_size("patch")
    two, one = edges(block)

    def exchange(value, firsts):
        pairs = [(i, i + 1) for i in firsts if i + 1 < count]
        return lax.ppermute(value, axes, pairs + [(b, a) for a, b in pairs])

    odd = range(1, count, 2)
    far = [i for i in odd if (i + 1) % group == 0]
    near = [i for i in odd if (i + 1) % group]
    return [exchange(one, range(0, count, 2)), exchange(two, near), exchange(two, far)]


def local(exposure, row_prof, col_prof, row_off, col_off, dest, fibre_weight):
    group = lax.axis_size("patch")
    frames = lax.axis_size("frame")
    patches = dest.shape[1]
    fibres, waves = col_prof.shape[2], row_prof.shape[2]
    capacity = (patches + group - 1) // group
    halos = neighbours(exposure[0])
    prepared = prepare(
        exposure[0],
        row_prof[0],
        col_prof[0].transpose(1, 0, 2),
        row_off[0],
        col_off[0],
        fibre_weight[0][:, None, :],
    )
    prepared[5] = prepared[5].reshape(patches // 2, LANES, LANES)
    send, numer = solve(halos, prepared, fibres, waves, row_off[0], col_off[0], dest[0], group)
    received = lax.all_to_all(send, "patch", split_axis=0, concat_axis=0, tiled=True)
    others = jnp.stack(
        [
            lax.ppermute(numer, "frame", [(i, (i + hop) % frames) for i in range(frames)])
            for hop in range(1, frames)
        ]
    )
    spectra_ext, coadd = finish(received, numer, others, capacity, patches, fibres, waves)
    return spectra_ext.transpose(2, 0, 3, 1), coadd.transpose(1, 2, 0)


def solution(mesh):
    in_specs = (
        P("frame", None, ("section", "patch"), None),
        P("frame", ("section", "patch"), None, None),
        P("frame", ("section", "patch"), None, None),
        P("frame", ("section", "patch")),
        P("frame", ("section", "patch")),
        P("frame", ("section", "patch")),
        P("frame", ("section", "patch"), None),
    )
    out_specs = (P("frame", ("section", "patch"), None, None), P(("section", "patch"), None, None))
    return jax.shard_map(local, mesh=mesh, in_specs=in_specs, out_specs=out_specs, check_vma=False)
```

```python
import functools

import jax
import jax.numpy as jnp
from jax import lax
from jax.experimental import pallas as pl
from jax.experimental.pallas import tpu as pltpu
from jax.sharding import PartitionSpec as P

HALO = 8
PC = 256
ITERS = 6
PR = 64
LANES = 128
SUB = 8
HALF = LANES // 2
CODE_BITS = 15.0
CODE_WIDTH = 16
CODE_MASK = 0xFFFF
CODE_TOP = 32767.0
TINY = 1e-30
EDGE_FLOPS = 1 << 34
EDGE_BYTES = 1 << 27
F32 = jnp.float32
BF16 = jnp.bfloat16


def up(count, multiple):
    return -(-count // multiple) * multiple


def dot_nt(lhs, rhs):
    return lax.dot_general(lhs, rhs, (((1,), (1,)), ((), ())), preferred_element_type=F32)


def dot_nn(lhs, rhs):
    return lax.dot_general(lhs, rhs, (((1,), (0,)), ((), ())), preferred_element_type=F32)


def two_parts(value):
    high = value.astype(BF16)
    return high, (value - high.astype(F32)).astype(BF16)


def two_pass(dot, value, weights):
    rows = value.shape[0]
    both = dot(jnp.concatenate(two_parts(value), axis=0), weights)
    return both[:rows] + both[rows:]


def block_tiles(fibres):
    blocks = fibres // SUB
    tiles = [(f, t) for f in range(blocks * SUB) for t in range(f // SUB, blocks)]
    for f in range(blocks * SUB, fibres):
        tiles += [(f, t) for t in range(up(fibres, SUB) // SUB)]
    return tiles


def split_lanes(value):
    return [value[:, at : at + LANES] for at in range(0, value.shape[1], LANES)]


def shifted(pieces, shift):
    rows = pieces[0].shape[0]
    turned = [pltpu.roll(piece, LANES - shift, 1) for piece in pieces]
    inside = lax.broadcasted_iota(jnp.int32, (rows, LANES), 1) < LANES - shift
    return [jnp.where(inside, turned[i], turned[i + 1]) for i in range(len(pieces) - 1)]


def start_copies(sources, targets, arrived):
    copies = [
        pltpu.make_async_copy(source, target, arrived.at[index])
        for index, (source, target) in enumerate(zip(sources, targets))
    ]
    for copy in copies:
        copy.start()
    return copies


def prepare_kernel(
    row_off_in,
    col_off_in,
    exposure,
    row_prof,
    col_prof,
    weight,
    products,
    weights_w,
    upper_wx,
    lower_wx,
    fibre,
    row_block,
    weight_lanes,
    row_off,
    col_off,
    band_w,
    band_wx,
    prof,
    fibre_rows,
    cut_row,
    arrived,
):
    copies = start_copies((row_off_in, col_off_in), (row_off, col_off), arrived)
    patches, waves, _ = row_prof.shape
    fibres = col_prof.shape[0]
    columns = exposure.shape[2]
    padded_p = up(patches, SUB)
    tiles = block_tiles(fibres)
    inverse = exposure[1].astype(F32)
    scaled = inverse * exposure[0].astype(F32)
    for piece, value in enumerate(split_lanes(inverse)):
        band_w[piece] = value
    for piece, value in enumerate(split_lanes(scaled)):
        band_wx[piece] = value
    for f in range(fibres):
        for piece, value in enumerate(split_lanes(col_prof[f].astype(F32))):
            prof[piece, f * padded_p : f * padded_p + patches, :] = value
    for copy in copies:
        copy.wait()
    cut_row[...] = jnp.zeros_like(cut_row)
    fibre_rows[...] = jnp.zeros_like(fibre_rows)
    halo = jnp.zeros((HALO, LANES), F32)
    square = (fibre.shape[1], fibres)
    eye = lax.broadcasted_iota(jnp.int32, square, 0) == lax.broadcasted_iota(jnp.int32, square, 1)
    lower_half = lax.broadcasted_iota(jnp.int32, (HALF, LANES), 1) < HALF

    def prepare(patch, carry):
        first_row = row_off[patch]
        first_col = col_off[patch]
        base = first_col // LANES
        shift = first_col - base * LANES
        count = PC // LANES
        window = shifted([band_w[base + piece] for piece in range(count + 1)], shift)
        for piece, value in enumerate(window):
            lanes = slice(piece * LANES, (piece + 1) * LANES)
            weights_w[patch, :, lanes] = jnp.concatenate([halo, value], axis=0).astype(BF16)
        window = shifted([band_wx[base + piece] for piece in range(count + 1)], shift)
        for piece, value in enumerate(window):
            lanes = slice(piece * LANES, (piece + 1) * LANES)
            upper, lower = two_parts(jnp.concatenate([halo, value], axis=0))
            upper_wx[patch, :, lanes] = upper
            lower_wx[patch, :, lanes] = lower
        for piece in range(count):
            lanes = slice(piece * LANES, (piece + 1) * LANES)
            fibre_rows[0:fibres, lanes] = prof[piece, pl.ds(patch, fibres, stride=padded_p), :]
        fibre[patch] = fibre_rows[...].astype(BF16)
        for at in range(0, len(tiles), 2):
            value = jnp.concatenate(
                [
                    fibre_rows[f : f + 1, :] * fibre_rows[t * SUB : (t + 1) * SUB, :]
                    for f, t in tiles[at : at + 2]
                ],
                axis=0,
            )
            upper, lower = two_parts(value)
            products[patch, at * SUB : (at + 2) * SUB, 0:PC] = upper
            products[patch, at * SUB : (at + 2) * SUB, PC : 2 * PC] = lower
        cut_row[0:waves, 0:PR] = row_prof[patch].astype(F32)
        profile = cut_row[...]
        turned = pltpu.roll(profile + pltpu.roll(profile, HALF, 1), first_row, 1)
        keep = lower_half == (lax.rem(patch, 2) == 0)
        row_block[patch] = jnp.where(keep, turned, 0.0).astype(BF16)
        own = jnp.broadcast_to(weight[patch], eye.shape)
        own = jnp.sum(jnp.where(eye, own, 0.0), axis=1, keepdims=True)
        weight_lanes[patch] = jnp.where(keep[: own.shape[0]], own, 0.0)
        return carry

    lax.fori_loop(0, patches, prepare, 0)


def solve_kernel(
    fibres,
    waves,
    row_off_in,
    col_off_in,
    dest_in,
    halo_one,
    halo_near,
    halo_far,
    products,
    weights_w,
    upper_wx,
    lower_wx,
    fibre,
    row_block,
    weight_lanes,
    send,
    numer,
    row_off,
    col_off,
    dest,
    halo_w,
    halo_wx,
    top_w,
    top_upper,
    top_lower,
    matrix,
    tails,
    estimate,
    residual,
    direction,
    imaged,
    across,
    partial,
    norm,
    packed,
    counts,
    arrived,
):
    copies = start_copies(
        (row_off_in, col_off_in, dest_in), (row_off, col_off, dest), arrived
    )
    patches = products.shape[0]
    pairs = patches // 2
    blocks = fibres // SUB
    main = blocks * SUB
    padded_f = up(fibres, SUB)
    tiles = block_tiles(fibres)
    rank = lax.axis_index("section") * lax.axis_size("patch") + lax.axis_index("patch")
    odd = lax.rem(rank, 2) == 1

    for slot, sources in enumerate(((halo_one,), (halo_near, halo_far))):
        rows = slice(slot * HALO, (slot + 1) * HALO)
        values, inverse = (
            sum(source[channel].astype(F32) for source in sources) for channel in range(2)
        )
        for piece, value in enumerate(split_lanes(inverse)):
            halo_w[piece, rows, :] = value
        for piece, value in enumerate(split_lanes(inverse * values)):
            halo_wx[piece, rows, :] = value
    partial[...] = jnp.zeros_like(partial)
    halo_row = lax.broadcasted_iota(jnp.int32, (HALO, LANES), 0)
    empty = jnp.zeros((PR, PC), BF16)
    copies[0].wait()
    copies[1].wait()

    def beside_own(edge, own):
        return jnp.concatenate([edge, own.astype(F32)[HALO:]], axis=0).astype(BF16)

    for patch in range(patches):
        first_row = row_off[patch]
        first_col = col_off[patch]
        base = first_col // LANES
        shift = first_col - base * LANES
        take_one = (halo_row >= first_row) == odd
        edges = []
        for source in (halo_w, halo_wx):
            pieces = [
                jnp.where(
                    take_one,
                    source[base + piece, 0:HALO, :],
                    source[base + piece, HALO : 2 * HALO, :],
                )
                for piece in range(PC // LANES + 1)
            ]
            edges.append(jnp.concatenate(shifted(pieces, shift), axis=1))
        above = edges[1].astype(BF16).astype(F32)
        top_w[patch] = beside_own(edges[0], weights_w[patch, : 2 * HALO, :])
        top_upper[patch] = beside_own(above, upper_wx[patch, : 2 * HALO, :])
        top_lower[patch] = beside_own(edges[1] - above, lower_wx[patch, : 2 * HALO, :])

    halves = partial.shape[0]
    members = [list(range(at, pairs, halves)) for at in range(halves)]

    def set_partial(pair, value):
        row = pair // halves
        partial[pair % halves, row : row + 1, :] = value

    def whole(top, own, patch):
        return jnp.concatenate([top[patch], own[patch, 2 * HALO :, :]], axis=0)

    def diagonal(first, second):
        return jnp.concatenate(
            [
                jnp.concatenate(first + [empty] * len(second), axis=1),
                jnp.concatenate([empty] * len(first) + second, axis=1),
            ],
            axis=0,
        )

    for pair in range(pairs):
        one, two = 2 * pair, 2 * pair + 1
        folded = dot_nt(
            jnp.concatenate([fibre[one], fibre[one], fibre[two], fibre[two]], axis=1),
            diagonal(
                [whole(top_upper, upper_wx, one), whole(top_lower, lower_wx, one)],
                [whole(top_upper, upper_wx, two), whole(top_lower, lower_wx, two)],
            ),
        )
        imaged[pair] = folded
    for pair in range(pairs):
        rhs = two_pass(dot_nt, imaged[pair], row_block[pair])
        residual[pair] = rhs
        direction[pair] = rhs
        estimate[pair] = jnp.zeros_like(rhs)
        set_partial(pair, jnp.sum(rhs * rhs, axis=0, keepdims=True))
    for pair in range(pairs):
        one, two = 2 * pair, 2 * pair + 1
        blended = dot_nt(
            jnp.concatenate([products[one], products[two]], axis=1),
            diagonal(
                [whole(top_w, weights_w, one)] * 2,
                [whole(top_w, weights_w, two)] * 2,
            ),
        )
        for index, (f, t) in enumerate(tiles):
            value = blended[index * SUB : (index + 1) * SUB]
            if f < main:
                matrix[pair, f * main + t * SUB : f * main + (t + 1) * SUB, :] = value
                if t > f // SUB:
                    matrix[pair, pl.ds(t * SUB * main + f, SUB, stride=main), :] = value
            else:
                if t < blocks:
                    matrix[pair, f * main + t * SUB : f * main + (t + 1) * SUB, :] = value
                tails[pair, f - main, t * SUB : (t + 1) * SUB, :] = value

    lower_half = lax.broadcasted_iota(jnp.int32, partial.shape[1:], 1) < HALF

    def patch_sums(value):
        first = jnp.sum(jnp.where(lower_half, value, 0.0), axis=1, keepdims=True)
        second = jnp.sum(jnp.where(lower_half, 0.0, value), axis=1, keepdims=True)
        return jnp.where(lower_half, first, second)

    def apply(dot, source, target, some):
        sides = [jnp.concatenate(two_parts(source[pair]), axis=0) for pair in some]
        blocks = [row_block[pair] for pair in some]
        if len(some) > 1:
            none = jnp.zeros_like(blocks[0])
            blocks = [
                jnp.concatenate(
                    [block if here == there else none for there in range(len(some))], axis=1
                )
                for here, block in enumerate(blocks)
            ]
        both = dot(jnp.concatenate(sides, axis=1), jnp.concatenate(blocks, axis=0))
        for index, pair in enumerate(some):
            lanes = both[:, index * LANES : (index + 1) * LANES]
            target[pair] = lanes[:padded_f] + lanes[padded_f:]

    def blend(pair):
        totals = [jnp.zeros((main, LANES), F32)] * 2
        for f in range(fibres):
            totals[f % 2] = totals[f % 2] + (
                matrix[pair, f * main : (f + 1) * main, :] * across[pair, f : f + 1, :]
            )
        total = totals[0] + totals[1]
        imaged[pair, 0:main, :] = total
        product = jnp.sum(total * across[pair, 0:main, :], axis=0, keepdims=True)
        if fibres > main:
            rest = jnp.zeros((padded_f - main, LANES), F32)
            row = lax.broadcasted_iota(jnp.int32, rest.shape, 0)
            for f in range(main, fibres):
                one = jnp.sum(tails[pair, f - main] * across[pair], axis=0, keepdims=True)
                rest = jnp.where(row == f - main, one, rest)
                product = product + one * across[pair, f : f + 1, :]
            imaged[pair, main:padded_f, :] = rest
        set_partial(pair, product)

    def image(half, folded=True):
        some = [members[half][at : at + 2] for at in range(0, len(members[half]), 2)]
        for turn in range(len(some) + 2):
            if turn < len(some):
                apply(dot_nn, direction, across, some[turn])
            if 0 <= turn - 1 < len(some):
                for pair in some[turn - 1]:
                    blend(pair)
            if folded and 0 <= turn - 2:
                apply(dot_nt, imaged, imaged, some[turn - 2])

    def advance(half):
        curvature = patch_sums(partial[half])
        step_size = norm[half] / jnp.where(curvature > 0.0, curvature, 1.0)
        sizes = [step_size[row : row + 1] for row in range(len(members[half]))]
        for size, pair in zip(sizes, members[half]):
            estimate[pair] = estimate[pair] + size * direction[pair]
        return sizes

    def move(half):
        sizes = advance(half)
        for size, pair in zip(sizes, members[half]):
            rest = residual[pair] - size * imaged[pair]
            residual[pair] = rest
            set_partial(pair, jnp.sum(rest * rest, axis=0, keepdims=True))
        norm_now = norm[half]
        norm_next = patch_sums(partial[half])
        ratio = norm_next / jnp.where(norm_now > 0.0, norm_now, 1.0)
        for row, pair in enumerate(members[half]):
            direction[pair] = residual[pair] + ratio[row : row + 1] * direction[pair]
        norm[half] = norm_next

    for half in range(halves):
        norm[half] = patch_sums(partial[half])
    image(0)
    image(1)
    move(0)

    for _ in range(ITERS - 2):
        image(0)
        move(1)
        image(1)
        move(0)
    image(0, folded=False)
    move(1)
    image(1, folded=False)
    advance(0)
    advance(1)

    copies[2].wait()
    for index in range(send.shape[0]):
        counts[index] = 0
    packed[...] = jnp.zeros_like(packed)
    upper_rows = (fibres + 1) // 2
    lane_f = lax.broadcasted_iota(jnp.int32, (padded_f, LANES), 1)
    at_wave = lax.rem(lane_f, HALF) == waves
    unit = jnp.where(at_wave, 1.0, 0.0)
    for pair in range(pairs):
        spectra = estimate[pair]
        numer[pair] = (spectra + unit) * (weight_lanes[2 * pair] + weight_lanes[2 * pair + 1])
        size = jnp.abs(spectra)
        first = jnp.max(jnp.where(lane_f < HALF, size, 0.0), axis=1, keepdims=True)
        second = jnp.max(jnp.where(lane_f < HALF, 0.0, size), axis=1, keepdims=True)
        largest = jnp.where(lane_f < HALF, first, second)
        power = jnp.floor(jnp.log2(jnp.maximum(largest, TINY))) + 1.0
        coded = jnp.clip(jnp.round(spectra * jnp.exp2(CODE_BITS - power)), -CODE_TOP, CODE_TOP)
        coded = jnp.where(at_wave, power, coded)
        turned = pltpu.roll(coded, HALF, 1)
        for half in range(2):
            here = turned if half else coded
            away = coded if half else turned
            target = dest[2 * pair + half]
            slot = counts[target]
            counts[target] = slot + 1
            compact = jnp.where(
                lane_f[:upper_rows] < HALF,
                here[:upper_rows],
                jnp.concatenate(
                    [away[upper_rows:fibres], away[: 2 * upper_rows - fibres]], axis=0
                ),
            )
            packed[target, pl.ds(slot * upper_rows, upper_rows), :] = compact
    words = send.shape[1]
    for index in range(send.shape[0]):
        codes = packed[index].astype(jnp.int32)
        send[index] = (codes[:words] << CODE_WIDTH) | (codes[words:] & CODE_MASK)


def coadd_kernel(numer, others, coadd, collected):
    fibres, patches, waves = coadd.shape
    padded_p = up(patches, SUB)
    lower_half = lax.broadcasted_iota(jnp.int32, numer.shape[1:], 1) < HALF
    for pair in range(numer.shape[0]):
        total = numer[pair]
        for index in range(others.shape[0]):
            total = total + others[index, pair]
        first, second = total[:, waves : waves + 1], total[:, HALF + waves : HALF + waves + 1]
        mean = total / jnp.where(lower_half, first, second)
        for half in range(2):
            value = pltpu.roll(mean, HALF, 1) if half else mean
            collected[pl.ds(2 * pair + half, fibres, stride=padded_p), :] = value[:fibres]
    for f in range(fibres):
        coadd[f] = collected[f * padded_p : f * padded_p + patches, :waves]


def finish_kernel(capacity, received, spectra_ext):
    _, fibres, _, waves = spectra_ext.shape
    upper_rows = (fibres + 1) // 2
    coded_shape = (2 * received.shape[1], LANES)
    lower_half = lax.broadcasted_iota(jnp.int32, coded_shape, 1) < HALF
    for source in range(received.shape[0]):
        word = received[source]
        codes = [word >> CODE_WIDTH, (word << CODE_WIDTH) >> CODE_WIDTH]
        coded = jnp.concatenate(codes, axis=0).astype(F32)
        power = jnp.where(
            lower_half, coded[:, waves : waves + 1], coded[:, HALF + waves : HALF + waves + 1]
        )
        value = coded * jnp.exp2(power - CODE_BITS)
        turned = pltpu.roll(value, HALF, 1)
        for slot in range(capacity):
            entry = source * capacity + slot
            at = slot * upper_rows
            spectra_ext[entry, 0:upper_rows, 0, :] = value[at : at + upper_rows, :waves]
            at_end = at + fibres - upper_rows
            spectra_ext[entry, upper_rows:fibres, 0, :] = turned[at:at_end, :waves]


def vmem(count=1):
    return [pl.BlockSpec(memory_space=pltpu.VMEM)] * count


def hbm(count=1):
    return [pl.BlockSpec(memory_space=pltpu.HBM)] * count


def prepare(exposure, row_prof, col_prof, row_off, col_off, weight):
    patches = row_prof.shape[0]
    fibres = col_prof.shape[0]
    _, band, columns = exposure.shape
    padded_f = up(fibres, SUB)
    padded_p = up(patches, SUB)
    rows = SUB * len(block_tiles(fibres))

    def made(*shape):
        return jax.ShapeDtypeStruct((patches,) + shape, BF16)

    return list(
        pl.pallas_call(
        prepare_kernel,
        out_shape=(
            made(rows, 2 * PC),
            made(PR, PC),
            made(PR, PC),
            made(PR, PC),
            made(padded_f, PC),
            made(HALF, LANES),
            jax.ShapeDtypeStruct((patches, padded_f, LANES), F32),
        ),
        in_specs=hbm(2) + vmem(4),
        out_specs=tuple(vmem(7)),
        scratch_shapes=[
            pltpu.SMEM(row_off.shape, row_off.dtype),
            pltpu.SMEM(col_off.shape, col_off.dtype),
            pltpu.VMEM((columns // LANES + 1, band, LANES), F32),
            pltpu.VMEM((columns // LANES + 1, band, LANES), F32),
            pltpu.VMEM((PC // LANES, fibres * padded_p, LANES), F32),
            pltpu.VMEM((padded_f, PC), F32),
            pltpu.VMEM((HALF, LANES), F32),
            pltpu.SemaphoreType.DMA((2,)),
        ],
        cost_estimate=pl.CostEstimate(
            flops=patches * rows * PC * 8, bytes_accessed=16 * 1024 * 1024, transcendentals=0
        ),
        compiler_params=pltpu.CompilerParams(vmem_limit_bytes=24 * 1024 * 1024),
    )(row_off, col_off, exposure, row_prof, col_prof, weight)
    )


def solve(halos, prepared, fibres, waves, row_off, col_off, dest, group):
    patches = dest.shape[0]
    columns = halos[0].shape[2]
    capacity = (patches + group - 1) // group
    pairs = patches // 2
    main = fibres // SUB * SUB
    padded_f = up(fibres, SUB)
    code_rows = up(capacity * ((fibres + 1) // 2), 2 * SUB)
    vectors = pltpu.VMEM((pairs, padded_f, LANES), F32)
    sums = pltpu.VMEM((2, up((pairs + 1) // 2, SUB), LANES), F32)
    tops = pltpu.VMEM((patches, 2 * HALO, PC), BF16)
    halo_band = pltpu.VMEM((columns // LANES + 1, 2 * HALO, LANES), F32)
    return pl.pallas_call(
        functools.partial(solve_kernel, fibres, waves),
        out_shape=(
            jax.ShapeDtypeStruct((group, code_rows // 2, LANES), jnp.int32),
            jax.ShapeDtypeStruct((pairs, padded_f, LANES), F32),
        ),
        in_specs=hbm(3) + vmem(10),
        out_specs=tuple(vmem(2)),
        scratch_shapes=[
            pltpu.SMEM(row_off.shape, row_off.dtype),
            pltpu.SMEM(col_off.shape, col_off.dtype),
            pltpu.SMEM(dest.shape, dest.dtype),
            halo_band,
            halo_band,
            tops,
            tops,
            tops,
            pltpu.VMEM((pairs, fibres * main, LANES), F32),
            pltpu.VMEM((pairs, max(fibres - main, 1), padded_f, LANES), F32),
            vectors,
            vectors,
            vectors,
            vectors,
            vectors,
            sums,
            sums,
            pltpu.VMEM((group, code_rows, LANES), F32),
            pltpu.SMEM((group,), jnp.int32),
            pltpu.SemaphoreType.DMA((3,)),
        ],
        compiler_params=pltpu.CompilerParams(vmem_limit_bytes=24 * 1024 * 1024),
    )(row_off, col_off, dest, *halos, *prepared)


def frame_mean(numer, others, patches, fibres, waves):
    return pl.pallas_call(
        coadd_kernel,
        out_shape=jax.ShapeDtypeStruct((fibres, patches, waves), F32),
        in_specs=vmem(2),
        out_specs=vmem()[0],
        scratch_shapes=[pltpu.VMEM((fibres * up(patches, SUB), LANES), F32)],
        cost_estimate=pl.CostEstimate(
            flops=4 * numer.size, bytes_accessed=8 * numer.size, transcendentals=numer.size
        ),
        compiler_params=pltpu.CompilerParams(vmem_limit_bytes=16 * 1024 * 1024),
    )(numer, others)


def finish(received, capacity, fibres, waves):
    entries = received.shape[0] * capacity
    return pl.pallas_call(
        functools.partial(finish_kernel, capacity),
        out_shape=jax.ShapeDtypeStruct((entries, fibres, 1, waves), F32),
        in_specs=vmem(1),
        out_specs=vmem()[0],
        compiler_params=pltpu.CompilerParams(vmem_limit_bytes=16 * 1024 * 1024),
    )(received)


def edge_kernel(exposure, two, one):
    rank = lax.axis_index("section") * lax.axis_size("patch") + lax.axis_index("patch")
    even = lax.rem(rank, 2) == 0
    band = exposure.shape[1]
    for channel in range(exposure.shape[0]):
        top = exposure[channel, 0:HALO, :].astype(F32)
        bottom = exposure[channel, band - HALO : band, :].astype(F32)
        one[channel] = jnp.where(even, bottom, top).astype(BF16)
        two[channel] = jnp.where(even, top, bottom).astype(BF16)


def edges(exposure):
    channels, _, columns = exposure.shape
    return pl.pallas_call(
        edge_kernel,
        out_shape=(jax.ShapeDtypeStruct((channels, HALO, columns), BF16),) * 2,
        in_specs=vmem(1),
        out_specs=tuple(vmem(2)),
        cost_estimate=pl.CostEstimate(
            flops=EDGE_FLOPS, bytes_accessed=EDGE_BYTES, transcendentals=0
        ),
        compiler_params=pltpu.CompilerParams(vmem_limit_bytes=8 * 1024 * 1024),
    )(exposure)


def neighbours(block):
    axes = ("section", "patch")
    count = lax.axis_size(axes)
    group = lax.axis_size("patch")
    two, one = edges(block)

    def exchange(value, firsts):
        pairs = [(i, i + 1) for i in firsts if i + 1 < count]
        return lax.ppermute(value, axes, pairs + [(b, a) for a, b in pairs])

    odd = range(1, count, 2)
    far = [i for i in odd if (i + 1) % group == 0]
    near = [i for i in odd if (i + 1) % group]
    return [exchange(one, range(0, count, 2)), exchange(two, near), exchange(two, far)]


def local(exposure, row_prof, col_prof, row_off, col_off, dest, fibre_weight):
    group = lax.axis_size("patch")
    frames = lax.axis_size("frame")
    patches = dest.shape[1]
    fibres, waves = col_prof.shape[2], row_prof.shape[2]
    capacity = (patches + group - 1) // group
    halos = neighbours(exposure[0])
    prepared = prepare(
        exposure[0],
        row_prof[0],
        col_prof[0].transpose(1, 0, 2),
        row_off[0],
        col_off[0],
        fibre_weight[0][:, None, :],
    )
    prepared[5] = prepared[5].reshape(patches // 2, LANES, LANES)
    send, numer = solve(halos, prepared, fibres, waves, row_off[0], col_off[0], dest[0], group)
    received = lax.all_to_all(send, "patch", split_axis=0, concat_axis=0, tiled=True)
    others = jnp.stack(
        [
            lax.ppermute(numer, "frame", [(i, (i + hop) % frames) for i in range(frames)])
            for hop in range(1, frames)
        ]
    )
    coadd = frame_mean(numer, others, patches, fibres, waves)
    spectra_ext = finish(received, capacity, fibres, waves)
    return spectra_ext.transpose(2, 0, 3, 1), coadd.transpose(1, 2, 0)


def solution(mesh):
    in_specs = (
        P("frame", None, ("section", "patch"), None),
        P("frame", ("section", "patch"), None, None),
        P("frame", ("section", "patch"), None, None),
        P("frame", ("section", "patch")),
        P("frame", ("section", "patch")),
        P("frame", ("section", "patch")),
        P("frame", ("section", "patch"), None),
    )
    out_specs = (P("frame", ("section", "patch"), None, None), P(("section", "patch"), None, None))
    return jax.shard_map(local, mesh=mesh, in_specs=in_specs, out_specs=out_specs, check_vma=False)
```

```python
import functools

import jax
import jax.numpy as jnp
from jax import lax
from jax.experimental import pallas as pl
from jax.experimental.pallas import tpu as pltpu
from jax.sharding import PartitionSpec as P

HALO = 8
PC = 256
ITERS = 6
PR = 64
LANES = 128
SUB = 8
HALF = LANES // 2
CODE_BITS = 15.0
CODE_TOP = 32767.0
TINY = 1e-30
EDGE_FLOPS = 1 << 34
EDGE_BYTES = 1 << 27
F32 = jnp.float32
BF16 = jnp.bfloat16


def up(count, multiple):
    return -(-count // multiple) * multiple


def dot_nt(lhs, rhs):
    return lax.dot_general(lhs, rhs, (((1,), (1,)), ((), ())), preferred_element_type=F32)


def dot_nn(lhs, rhs):
    return lax.dot_general(lhs, rhs, (((1,), (0,)), ((), ())), preferred_element_type=F32)


def two_parts(value):
    high = value.astype(BF16)
    return high, (value - high.astype(F32)).astype(BF16)


def two_pass(dot, value, weights):
    rows = value.shape[0]
    both = dot(jnp.concatenate(two_parts(value), axis=0), weights)
    return both[:rows] + both[rows:]


def block_tiles(fibres):
    blocks = fibres // SUB
    tiles = [(f, t) for f in range(blocks * SUB) for t in range(f // SUB, blocks)]
    for f in range(blocks * SUB, fibres):
        tiles += [(f, t) for t in range(up(fibres, SUB) // SUB)]
    return tiles


def split_lanes(value):
    return [value[:, at : at + LANES] for at in range(0, value.shape[1], LANES)]


def shifted(pieces, shift):
    rows = pieces[0].shape[0]
    turned = [pltpu.roll(piece, LANES - shift, 1) for piece in pieces]
    inside = lax.broadcasted_iota(jnp.int32, (rows, LANES), 1) < LANES - shift
    return [jnp.where(inside, turned[i], turned[i + 1]) for i in range(len(pieces) - 1)]


def start_copies(sources, targets, arrived):
    copies = [
        pltpu.make_async_copy(source, target, arrived.at[index])
        for index, (source, target) in enumerate(zip(sources, targets))
    ]
    for copy in copies:
        copy.start()
    return copies


def prepare_kernel(
    row_off_in,
    col_off_in,
    exposure,
    row_prof,
    col_prof,
    weight,
    products,
    weights_w,
    upper_wx,
    lower_wx,
    fibre,
    row_block,
    weight_lanes,
    row_off,
    col_off,
    band_w,
    band_wx,
    prof,
    fibre_rows,
    cut_row,
    arrived,
):
    copies = start_copies((row_off_in, col_off_in), (row_off, col_off), arrived)
    patches, waves, _ = row_prof.shape
    fibres = col_prof.shape[0]
    columns = exposure.shape[2]
    padded_p = up(patches, SUB)
    tiles = block_tiles(fibres)
    inverse = exposure[1].astype(F32)
    scaled = inverse * exposure[0].astype(F32)
    for piece, value in enumerate(split_lanes(inverse)):
        band_w[piece] = value
    for piece, value in enumerate(split_lanes(scaled)):
        band_wx[piece] = value
    for f in range(fibres):
        for piece, value in enumerate(split_lanes(col_prof[f].astype(F32))):
            prof[piece, f * padded_p : f * padded_p + patches, :] = value
    for copy in copies:
        copy.wait()
    cut_row[...] = jnp.zeros_like(cut_row)
    fibre_rows[...] = jnp.zeros_like(fibre_rows)
    halo = jnp.zeros((HALO, LANES), F32)
    square = (fibre.shape[1], fibres)
    eye = lax.broadcasted_iota(jnp.int32, square, 0) == lax.broadcasted_iota(jnp.int32, square, 1)
    lower_half = lax.broadcasted_iota(jnp.int32, (HALF, LANES), 1) < HALF

    def prepare(patch, carry):
        first_row = row_off[patch]
        first_col = col_off[patch]
        base = first_col // LANES
        shift = first_col - base * LANES
        count = PC // LANES
        window = shifted([band_w[base + piece] for piece in range(count + 1)], shift)
        for piece, value in enumerate(window):
            lanes = slice(piece * LANES, (piece + 1) * LANES)
            weights_w[patch, :, lanes] = jnp.concatenate([halo, value], axis=0).astype(BF16)
        window = shifted([band_wx[base + piece] for piece in range(count + 1)], shift)
        for piece, value in enumerate(window):
            lanes = slice(piece * LANES, (piece + 1) * LANES)
            upper, lower = two_parts(jnp.concatenate([halo, value], axis=0))
            upper_wx[patch, :, lanes] = upper
            lower_wx[patch, :, lanes] = lower
        for piece in range(count):
            lanes = slice(piece * LANES, (piece + 1) * LANES)
            fibre_rows[0:fibres, lanes] = prof[piece, pl.ds(patch, fibres, stride=padded_p), :]
        fibre[patch] = fibre_rows[...].astype(BF16)
        for at in range(0, len(tiles), 2):
            value = jnp.concatenate(
                [
                    fibre_rows[f : f + 1, :] * fibre_rows[t * SUB : (t + 1) * SUB, :]
                    for f, t in tiles[at : at + 2]
                ],
                axis=0,
            )
            upper, lower = two_parts(value)
            products[patch, at * SUB : (at + 2) * SUB, 0:PC] = upper
            products[patch, at * SUB : (at + 2) * SUB, PC : 2 * PC] = lower
        cut_row[0:waves, 0:PR] = row_prof[patch].astype(F32)
        profile = cut_row[...]
        turned = pltpu.roll(profile + pltpu.roll(profile, HALF, 1), first_row, 1)
        keep = lower_half == (lax.rem(patch, 2) == 0)
        row_block[patch] = jnp.where(keep, turned, 0.0).astype(BF16)
        own = jnp.broadcast_to(weight[patch], eye.shape)
        own = jnp.sum(jnp.where(eye, own, 0.0), axis=1, keepdims=True)
        weight_lanes[patch] = jnp.where(keep[: own.shape[0]], own, 0.0)
        return carry

    lax.fori_loop(0, patches, prepare, 0)


def solve_kernel(
    fibres,
    waves,
    row_off_in,
    col_off_in,
    dest_in,
    halo_one,
    halo_near,
    halo_far,
    products,
    weights_w,
    upper_wx,
    lower_wx,
    fibre,
    row_block,
    weight_lanes,
    send,
    numer,
    row_off,
    col_off,
    dest,
    halo_w,
    halo_wx,
    top_w,
    top_upper,
    top_lower,
    matrix,
    tails,
    estimate,
    residual,
    direction,
    imaged,
    across,
    partial,
    norm,
    packed,
    counts,
    slots,
    arrived,
):
    copies = start_copies(
        (row_off_in, col_off_in, dest_in), (row_off, col_off, dest), arrived
    )
    patches = products.shape[0]
    pairs = patches // 2
    blocks = fibres // SUB
    main = blocks * SUB
    padded_f = up(fibres, SUB)
    tiles = block_tiles(fibres)
    rank = lax.axis_index("section") * lax.axis_size("patch") + lax.axis_index("patch")
    odd = lax.rem(rank, 2) == 1

    for slot, sources in enumerate(((halo_one,), (halo_near, halo_far))):
        rows = slice(slot * HALO, (slot + 1) * HALO)
        values, inverse = (
            sum(source[channel].astype(F32) for source in sources) for channel in range(2)
        )
        for piece, value in enumerate(split_lanes(inverse)):
            halo_w[piece, rows, :] = value
        for piece, value in enumerate(split_lanes(inverse * values)):
            halo_wx[piece, rows, :] = value
    partial[...] = jnp.zeros_like(partial)
    halo_row = lax.broadcasted_iota(jnp.int32, (HALO, LANES), 0)
    empty = jnp.zeros((PR, PC), BF16)
    copies[0].wait()
    copies[1].wait()

    def beside_own(edge, own):
        return jnp.concatenate([edge, own.astype(F32)[HALO:]], axis=0).astype(BF16)

    def cut_halo(patch):
        first_row = row_off[patch]
        first_col = col_off[patch]
        base = first_col // LANES
        shift = first_col - base * LANES
        take_one = (halo_row >= first_row) == odd
        edges = []
        for source in (halo_w, halo_wx):
            pieces = [
                jnp.where(
                    take_one,
                    source[base + piece, 0:HALO, :],
                    source[base + piece, HALO : 2 * HALO, :],
                )
                for piece in range(PC // LANES + 1)
            ]
            edges.append(jnp.concatenate(shifted(pieces, shift), axis=1))
        above = edges[1].astype(BF16).astype(F32)
        top_w[patch] = beside_own(edges[0], weights_w[patch, : 2 * HALO, :])
        top_upper[patch] = beside_own(above, upper_wx[patch, : 2 * HALO, :])
        top_lower[patch] = beside_own(edges[1] - above, lower_wx[patch, : 2 * HALO, :])

    halves = partial.shape[0]
    members = [list(range(at, pairs, halves)) for at in range(halves)]

    def set_partial(pair, value):
        row = pair // halves
        partial[pair % halves, row : row + 1, :] = value

    def whole(top, own, patch):
        return jnp.concatenate([top[patch], own[patch, 2 * HALO :, :]], axis=0)

    def diagonal(first, second):
        return jnp.concatenate(
            [
                jnp.concatenate(first + [empty] * len(second), axis=1),
                jnp.concatenate([empty] * len(first) + second, axis=1),
            ],
            axis=0,
        )

    def begin(half):
        some = members[half]
        for pair in some:
            cut_halo(2 * pair)
            cut_halo(2 * pair + 1)
        for pair in some:
            one, two = 2 * pair, 2 * pair + 1
            imaged[pair] = dot_nt(
                jnp.concatenate([fibre[one], fibre[one], fibre[two], fibre[two]], axis=1),
                diagonal(
                    [whole(top_upper, upper_wx, one), whole(top_lower, lower_wx, one)],
                    [whole(top_upper, upper_wx, two), whole(top_lower, lower_wx, two)],
                ),
            )
        for pair in some:
            rhs = two_pass(dot_nt, imaged[pair], row_block[pair])
            residual[pair] = rhs
            direction[pair] = rhs
            estimate[pair] = jnp.zeros_like(rhs)
            set_partial(pair, jnp.sum(rhs * rhs, axis=0, keepdims=True))
        norm[half] = patch_sums(partial[half])

    def build(pair):
        one, two = 2 * pair, 2 * pair + 1
        blended = dot_nt(
            jnp.concatenate([products[one], products[two]], axis=1),
            diagonal(
                [whole(top_w, weights_w, one)] * 2,
                [whole(top_w, weights_w, two)] * 2,
            ),
        )
        for index, (f, t) in enumerate(tiles):
            value = blended[index * SUB : (index + 1) * SUB]
            if f < main:
                matrix[pair, f * main + t * SUB : f * main + (t + 1) * SUB, :] = value
                if t > f // SUB:
                    matrix[pair, pl.ds(t * SUB * main + f, SUB, stride=main), :] = value
            else:
                if t < blocks:
                    matrix[pair, f * main + t * SUB : f * main + (t + 1) * SUB, :] = value
                tails[pair, f - main, t * SUB : (t + 1) * SUB, :] = value

    lower_half = lax.broadcasted_iota(jnp.int32, partial.shape[1:], 1) < HALF

    def patch_sums(value):
        first = jnp.sum(jnp.where(lower_half, value, 0.0), axis=1, keepdims=True)
        second = jnp.sum(jnp.where(lower_half, 0.0, value), axis=1, keepdims=True)
        return jnp.where(lower_half, first, second)

    def apply(dot, source, target, some):
        sides = [jnp.concatenate(two_parts(source[pair]), axis=0) for pair in some]
        blocks = [row_block[pair] for pair in some]
        if len(some) > 1:
            none = jnp.zeros_like(blocks[0])
            blocks = [
                jnp.concatenate(
                    [block if here == there else none for there in range(len(some))], axis=1
                )
                for here, block in enumerate(blocks)
            ]
        both = dot(jnp.concatenate(sides, axis=1), jnp.concatenate(blocks, axis=0))
        for index, pair in enumerate(some):
            lanes = both[:, index * LANES : (index + 1) * LANES]
            target[pair] = lanes[:padded_f] + lanes[padded_f:]

    def blend(pair):
        totals = [jnp.zeros((main, LANES), F32)] * 2
        for f in range(fibres):
            totals[f % 2] = totals[f % 2] + (
                matrix[pair, f * main : (f + 1) * main, :] * across[pair, f : f + 1, :]
            )
        total = totals[0] + totals[1]
        imaged[pair, 0:main, :] = total
        product = jnp.sum(total * across[pair, 0:main, :], axis=0, keepdims=True)
        if fibres > main:
            rest = jnp.zeros((padded_f - main, LANES), F32)
            row = lax.broadcasted_iota(jnp.int32, rest.shape, 0)
            for f in range(main, fibres):
                one = jnp.sum(tails[pair, f - main] * across[pair], axis=0, keepdims=True)
                rest = jnp.where(row == f - main, one, rest)
                product = product + one * across[pair, f : f + 1, :]
            imaged[pair, main:padded_f, :] = rest
        set_partial(pair, product)

    def image(half, folded=True, beside=()):
        some = [members[half][at : at + 2] for at in range(0, len(members[half]), 2)]
        turns = len(some) + 2
        share = -(-len(beside) // turns)
        for turn in range(turns):
            for work in beside[turn * share : (turn + 1) * share]:
                work()
            if turn < len(some):
                apply(dot_nn, direction, across, some[turn])
            if 0 <= turn - 1 < len(some):
                for pair in some[turn - 1]:
                    blend(pair)
            if folded and 0 <= turn - 2:
                apply(dot_nt, imaged, imaged, some[turn - 2])

    def advance(half):
        curvature = patch_sums(partial[half])
        step_size = norm[half] / jnp.where(curvature > 0.0, curvature, 1.0)
        sizes = [step_size[row : row + 1] for row in range(len(members[half]))]
        for size, pair in zip(sizes, members[half]):
            estimate[pair] = estimate[pair] + size * direction[pair]
        return sizes

    def move(half):
        sizes = advance(half)
        for size, pair in zip(sizes, members[half]):
            rest = residual[pair] - size * imaged[pair]
            residual[pair] = rest
            set_partial(pair, jnp.sum(rest * rest, axis=0, keepdims=True))
        norm_now = norm[half]
        norm_next = patch_sums(partial[half])
        ratio = norm_next / jnp.where(norm_now > 0.0, norm_now, 1.0)
        for row, pair in enumerate(members[half]):
            direction[pair] = residual[pair] + ratio[row : row + 1] * direction[pair]
        norm[half] = norm_next

    copies[2].wait()
    for index in range(send.shape[0]):
        counts[index] = 0
    for patch in range(patches):
        target = dest[patch]
        slot = counts[target]
        counts[target] = slot + 1
        slots[patch] = slot
    packed[...] = jnp.zeros_like(packed)
    upper_rows = (fibres + 1) // 2
    lane_f = lax.broadcasted_iota(jnp.int32, (padded_f, LANES), 1)
    at_wave = lax.rem(lane_f, HALF) == waves
    unit = jnp.where(at_wave, 1.0, 0.0)

    def hand_over(pair):
        spectra = estimate[pair]
        numer[pair] = (spectra + unit) * (weight_lanes[2 * pair] + weight_lanes[2 * pair + 1])
        size = jnp.abs(spectra)
        first = jnp.max(jnp.where(lane_f < HALF, size, 0.0), axis=1, keepdims=True)
        second = jnp.max(jnp.where(lane_f < HALF, 0.0, size), axis=1, keepdims=True)
        largest = jnp.where(lane_f < HALF, first, second)
        power = jnp.floor(jnp.log2(jnp.maximum(largest, TINY))) + 1.0
        coded = jnp.clip(jnp.round(spectra * jnp.exp2(CODE_BITS - power)), -CODE_TOP, CODE_TOP)
        coded = jnp.where(at_wave, power, coded)
        turned = pltpu.roll(coded, HALF, 1)
        for half in range(2):
            here = turned if half else coded
            away = coded if half else turned
            compact = jnp.where(
                lane_f[:upper_rows] < HALF,
                here[:upper_rows],
                jnp.concatenate(
                    [away[upper_rows:fibres], away[: 2 * upper_rows - fibres]], axis=0
                ),
            )
            rows = pl.ds(slots[2 * pair + half] * upper_rows, upper_rows)
            packed[dest[2 * pair + half], rows, :] = compact

    begin(0)
    for pair in members[0]:
        build(pair)
    begin(1)
    image(0, beside=[functools.partial(build, pair) for pair in members[1]])
    image(1)
    move(0)
    for _ in range(ITERS - 2):
        image(0)
        move(1)
        image(1)
        move(0)
    image(0, folded=False)
    move(1)
    advance(0)
    image(1, folded=False, beside=[functools.partial(hand_over, pair) for pair in members[0]])
    advance(1)
    for pair in members[1]:
        hand_over(pair)
    for index in range(send.shape[0]):
        send[index] = packed[index].astype(jnp.int32).astype(jnp.int16)


def finish_kernel(
    capacity, received, numer, others, spectra_out, coadd_out, spectra_ext, coadd, collected, sent
):
    fibres, patches, waves = coadd.shape
    padded_p = up(patches, SUB)
    lower_half = lax.broadcasted_iota(jnp.int32, numer.shape[1:], 1) < HALF
    for pair in range(numer.shape[0]):
        total = numer[pair]
        for index in range(others.shape[0]):
            total = total + others[index, pair]
        first, second = total[:, waves : waves + 1], total[:, HALF + waves : HALF + waves + 1]
        mean = total / jnp.where(lower_half, first, second)
        for half in range(2):
            value = pltpu.roll(mean, HALF, 1) if half else mean
            collected[pl.ds(2 * pair + half, fibres, stride=padded_p), :] = value[:fibres]
    for f in range(fibres):
        coadd[f] = collected[f * padded_p : f * padded_p + patches, :waves]
    copies = [pltpu.make_async_copy(coadd, coadd_out, sent.at[0])]
    copies[0].start()
    upper_rows = (fibres + 1) // 2
    lower_half = lax.broadcasted_iota(jnp.int32, received.shape[1:], 1) < HALF
    for source in range(received.shape[0]):
        coded = received[source].astype(jnp.int32).astype(F32)
        power = jnp.where(
            lower_half, coded[:, waves : waves + 1], coded[:, HALF + waves : HALF + waves + 1]
        )
        value = coded * jnp.exp2(power - CODE_BITS)
        turned = pltpu.roll(value, HALF, 1)
        for slot in range(capacity):
            entry = source * capacity + slot
            at = slot * upper_rows
            spectra_ext[entry, 0:upper_rows, 0, :] = value[at : at + upper_rows, :waves]
            at_end = at + fibres - upper_rows
            spectra_ext[entry, upper_rows:fibres, 0, :] = turned[at:at_end, :waves]
        entries = pl.ds(source * capacity, capacity)
        copy = pltpu.make_async_copy(
            spectra_ext.at[entries], spectra_out.at[entries], sent.at[1 + source]
        )
        copy.start()
        copies.append(copy)
    for copy in copies:
        copy.wait()


def vmem(count=1):
    return [pl.BlockSpec(memory_space=pltpu.VMEM)] * count


def hbm(count=1):
    return [pl.BlockSpec(memory_space=pltpu.HBM)] * count


def prepare(exposure, row_prof, col_prof, row_off, col_off, weight):
    patches = row_prof.shape[0]
    fibres = col_prof.shape[0]
    _, band, columns = exposure.shape
    padded_f = up(fibres, SUB)
    padded_p = up(patches, SUB)
    rows = SUB * len(block_tiles(fibres))

    def made(*shape):
        return jax.ShapeDtypeStruct((patches,) + shape, BF16)

    return list(
        pl.pallas_call(
        prepare_kernel,
        out_shape=(
            made(rows, 2 * PC),
            made(PR, PC),
            made(PR, PC),
            made(PR, PC),
            made(padded_f, PC),
            made(HALF, LANES),
            jax.ShapeDtypeStruct((patches, padded_f, LANES), F32),
        ),
        in_specs=hbm(2) + vmem(4),
        out_specs=tuple(vmem(7)),
        scratch_shapes=[
            pltpu.SMEM(row_off.shape, row_off.dtype),
            pltpu.SMEM(col_off.shape, col_off.dtype),
            pltpu.VMEM((columns // LANES + 1, band, LANES), F32),
            pltpu.VMEM((columns // LANES + 1, band, LANES), F32),
            pltpu.VMEM((PC // LANES, fibres * padded_p, LANES), F32),
            pltpu.VMEM((padded_f, PC), F32),
            pltpu.VMEM((HALF, LANES), F32),
            pltpu.SemaphoreType.DMA((2,)),
        ],
        cost_estimate=pl.CostEstimate(
            flops=patches * rows * PC * 8, bytes_accessed=16 * 1024 * 1024, transcendentals=0
        ),
        compiler_params=pltpu.CompilerParams(vmem_limit_bytes=24 * 1024 * 1024),
    )(row_off, col_off, exposure, row_prof, col_prof, weight)
    )


def solve(halos, prepared, fibres, waves, row_off, col_off, dest, group):
    patches = dest.shape[0]
    columns = halos[0].shape[2]
    capacity = (patches + group - 1) // group
    pairs = patches // 2
    main = fibres // SUB * SUB
    padded_f = up(fibres, SUB)
    code_rows = up(capacity * ((fibres + 1) // 2), SUB)
    vectors = pltpu.VMEM((pairs, padded_f, LANES), F32)
    sums = pltpu.VMEM((2, up((pairs + 1) // 2, SUB), LANES), F32)
    tops = pltpu.VMEM((patches, 2 * HALO, PC), BF16)
    halo_band = pltpu.VMEM((columns // LANES + 1, 2 * HALO, LANES), F32)
    return pl.pallas_call(
        functools.partial(solve_kernel, fibres, waves),
        out_shape=(
            jax.ShapeDtypeStruct((group, code_rows, LANES), jnp.int16),
            jax.ShapeDtypeStruct((pairs, padded_f, LANES), F32),
        ),
        in_specs=hbm(3) + vmem(10),
        out_specs=tuple(vmem(2)),
        scratch_shapes=[
            pltpu.SMEM(row_off.shape, row_off.dtype),
            pltpu.SMEM(col_off.shape, col_off.dtype),
            pltpu.SMEM(dest.shape, dest.dtype),
            halo_band,
            halo_band,
            tops,
            tops,
            tops,
            pltpu.VMEM((pairs, fibres * main, LANES), F32),
            pltpu.VMEM((pairs, max(fibres - main, 1), padded_f, LANES), F32),
            vectors,
            vectors,
            vectors,
            vectors,
            vectors,
            sums,
            sums,
            pltpu.VMEM((group, code_rows, LANES), F32),
            pltpu.SMEM((group,), jnp.int32),
            pltpu.SMEM((patches,), jnp.int32),
            pltpu.SemaphoreType.DMA((3,)),
        ],
        compiler_params=pltpu.CompilerParams(vmem_limit_bytes=24 * 1024 * 1024),
    )(row_off, col_off, dest, *halos, *prepared)


def finish(received, numer, others, capacity, patches, fibres, waves):
    entries = received.shape[0] * capacity
    return pl.pallas_call(
        functools.partial(finish_kernel, capacity),
        out_shape=(
            jax.ShapeDtypeStruct((entries, fibres, 1, waves), F32),
            jax.ShapeDtypeStruct((fibres, patches, waves), F32),
        ),
        in_specs=vmem(3),
        out_specs=tuple(hbm(2)),
        scratch_shapes=[
            pltpu.VMEM((entries, fibres, 1, waves), F32),
            pltpu.VMEM((fibres, patches, waves), F32),
            pltpu.VMEM((fibres * up(patches, SUB), LANES), F32),
            pltpu.SemaphoreType.DMA((1 + received.shape[0],)),
        ],
        compiler_params=pltpu.CompilerParams(vmem_limit_bytes=16 * 1024 * 1024),
    )(received, numer, others)


def edge_kernel(exposure, two, one):
    rank = lax.axis_index("section") * lax.axis_size("patch") + lax.axis_index("patch")
    even = lax.rem(rank, 2) == 0
    band = exposure.shape[1]
    for channel in range(exposure.shape[0]):
        top = exposure[channel, 0:HALO, :].astype(F32)
        bottom = exposure[channel, band - HALO : band, :].astype(F32)
        one[channel] = jnp.where(even, bottom, top).astype(BF16)
        two[channel] = jnp.where(even, top, bottom).astype(BF16)


def edges(exposure):
    channels, _, columns = exposure.shape
    return pl.pallas_call(
        edge_kernel,
        out_shape=(jax.ShapeDtypeStruct((channels, HALO, columns), BF16),) * 2,
        in_specs=vmem(1),
        out_specs=tuple(vmem(2)),
        cost_estimate=pl.CostEstimate(
            flops=EDGE_FLOPS, bytes_accessed=EDGE_BYTES, transcendentals=0
        ),
        compiler_params=pltpu.CompilerParams(vmem_limit_bytes=8 * 1024 * 1024),
    )(exposure)


def neighbours(block):
    axes = ("section", "patch")
    count = lax.axis_size(axes)
    group = lax.axis_size("patch")
    two, one = edges(block)

    def exchange(value, firsts):
        pairs = [(i, i + 1) for i in firsts if i + 1 < count]
        return lax.ppermute(value, axes, pairs + [(b, a) for a, b in pairs])

    odd = range(1, count, 2)
    far = [i for i in odd if (i + 1) % group == 0]
    near = [i for i in odd if (i + 1) % group]
    return [exchange(one, range(0, count, 2)), exchange(two, near), exchange(two, far)]


def local(exposure, row_prof, col_prof, row_off, col_off, dest, fibre_weight):
    group = lax.axis_size("patch")
    frames = lax.axis_size("frame")
    patches = dest.shape[1]
    fibres, waves = col_prof.shape[2], row_prof.shape[2]
    capacity = (patches + group - 1) // group
    halos = neighbours(exposure[0])
    prepared = prepare(
        exposure[0],
        row_prof[0],
        col_prof[0].transpose(1, 0, 2),
        row_off[0],
        col_off[0],
        fibre_weight[0][:, None, :],
    )
    prepared[5] = prepared[5].reshape(patches // 2, LANES, LANES)
    send, numer = solve(halos, prepared, fibres, waves, row_off[0], col_off[0], dest[0], group)
    received = lax.all_to_all(send, "patch", split_axis=0, concat_axis=0, tiled=True)
    others = jnp.stack(
        [
            lax.ppermute(numer, "frame", [(i, (i + hop) % frames) for i in range(frames)])
            for hop in range(1, frames)
        ]
    )
    spectra_ext, coadd = finish(received, numer, others, capacity, patches, fibres, waves)
    return spectra_ext.transpose(2, 0, 3, 1), coadd.transpose(1, 2, 0)


def solution(mesh):
    in_specs = (
        P("frame", None, ("section", "patch"), None),
        P("frame", ("section", "patch"), None, None),
        P("frame", ("section", "patch"), None, None),
        P("frame", ("section", "patch")),
        P("frame", ("section", "patch")),
        P("frame", ("section", "patch")),
        P("frame", ("section", "patch"), None),
    )
    out_specs = (P("frame", ("section", "patch"), None, None), P(("section", "patch"), None, None))
    return jax.shard_map(local, mesh=mesh, in_specs=in_specs, out_specs=out_specs, check_vma=False)
```

```python
import functools

import jax
import jax.numpy as jnp
from jax import lax
from jax.experimental import pallas as pl
from jax.experimental.pallas import tpu as pltpu
from jax.sharding import PartitionSpec as P

HALO = 8
PC = 256
ITERS = 6
PR = 64
LANES = 128
SUB = 8
HALF = LANES // 2
CODE_BITS = 15.0
CODE_TOP = 32767.0
TINY = 1e-30
EDGE_FLOPS = 1 << 34
EDGE_BYTES = 1 << 27
F32 = jnp.float32
BF16 = jnp.bfloat16


def up(count, multiple):
    return -(-count // multiple) * multiple


def dot_nt(lhs, rhs):
    return lax.dot_general(lhs, rhs, (((1,), (1,)), ((), ())), preferred_element_type=F32)


def dot_nn(lhs, rhs):
    return lax.dot_general(lhs, rhs, (((1,), (0,)), ((), ())), preferred_element_type=F32)


def two_parts(value):
    high = value.astype(BF16)
    return high, (value - high.astype(F32)).astype(BF16)


def two_pass(dot, value, weights):
    rows = value.shape[0]
    both = dot(jnp.concatenate(two_parts(value), axis=0), weights)
    return both[:rows] + both[rows:]


def block_tiles(fibres):
    blocks = fibres // SUB
    tiles = [(f, t) for f in range(blocks * SUB) for t in range(f // SUB, blocks)]
    for f in range(blocks * SUB, fibres):
        tiles += [(f, t) for t in range(up(fibres, SUB) // SUB)]
    return tiles


def split_lanes(value):
    return [value[:, at : at + LANES] for at in range(0, value.shape[1], LANES)]


def shifted(pieces, shift):
    rows = pieces[0].shape[0]
    turned = [pltpu.roll(piece, LANES - shift, 1) for piece in pieces]
    inside = lax.broadcasted_iota(jnp.int32, (rows, LANES), 1) < LANES - shift
    return [jnp.where(inside, turned[i], turned[i + 1]) for i in range(len(pieces) - 1)]


def start_copies(sources, targets, arrived):
    copies = [
        pltpu.make_async_copy(source, target, arrived.at[index])
        for index, (source, target) in enumerate(zip(sources, targets))
    ]
    for copy in copies:
        copy.start()
    return copies


def prepare_kernel(
    row_off_in,
    col_off_in,
    exposure,
    row_prof,
    col_prof,
    weight,
    products,
    weights_w,
    upper_wx,
    lower_wx,
    fibre,
    row_block,
    weight_lanes,
    row_off,
    col_off,
    band_w,
    band_wx,
    prof,
    fibre_rows,
    cut_row,
    arrived,
):
    copies = start_copies((row_off_in, col_off_in), (row_off, col_off), arrived)
    patches, waves, _ = row_prof.shape
    fibres = col_prof.shape[0]
    columns = exposure.shape[2]
    padded_p = up(patches, SUB)
    tiles = block_tiles(fibres)
    inverse = exposure[1].astype(F32)
    scaled = inverse * exposure[0].astype(F32)
    for piece, value in enumerate(split_lanes(inverse)):
        band_w[piece] = value
    for piece, value in enumerate(split_lanes(scaled)):
        band_wx[piece] = value
    for f in range(fibres):
        for piece, value in enumerate(split_lanes(col_prof[f].astype(F32))):
            prof[piece, f * padded_p : f * padded_p + patches, :] = value
    for copy in copies:
        copy.wait()
    cut_row[...] = jnp.zeros_like(cut_row)
    fibre_rows[...] = jnp.zeros_like(fibre_rows)
    halo = jnp.zeros((HALO, LANES), F32)
    square = (fibre.shape[1], fibres)
    eye = lax.broadcasted_iota(jnp.int32, square, 0) == lax.broadcasted_iota(jnp.int32, square, 1)
    lower_half = lax.broadcasted_iota(jnp.int32, (HALF, LANES), 1) < HALF

    def prepare(patch, carry):
        first_row = row_off[patch]
        first_col = col_off[patch]
        base = first_col // LANES
        shift = first_col - base * LANES
        count = PC // LANES
        window = shifted([band_w[base + piece] for piece in range(count + 1)], shift)
        for piece, value in enumerate(window):
            lanes = slice(piece * LANES, (piece + 1) * LANES)
            weights_w[patch, :, lanes] = jnp.concatenate([halo, value], axis=0).astype(BF16)
        window = shifted([band_wx[base + piece] for piece in range(count + 1)], shift)
        for piece, value in enumerate(window):
            lanes = slice(piece * LANES, (piece + 1) * LANES)
            upper, lower = two_parts(jnp.concatenate([halo, value], axis=0))
            upper_wx[patch, :, lanes] = upper
            lower_wx[patch, :, lanes] = lower
        for piece in range(count):
            lanes = slice(piece * LANES, (piece + 1) * LANES)
            fibre_rows[0:fibres, lanes] = prof[piece, pl.ds(patch, fibres, stride=padded_p), :]
        fibre[patch] = fibre_rows[...].astype(BF16)
        for at in range(0, len(tiles), 2):
            value = jnp.concatenate(
                [
                    fibre_rows[f : f + 1, :] * fibre_rows[t * SUB : (t + 1) * SUB, :]
                    for f, t in tiles[at : at + 2]
                ],
                axis=0,
            )
            upper, lower = two_parts(value)
            products[patch, at * SUB : (at + 2) * SUB, 0:PC] = upper
            products[patch, at * SUB : (at + 2) * SUB, PC : 2 * PC] = lower
        cut_row[0:waves, 0:PR] = row_prof[patch].astype(F32)
        profile = cut_row[...]
        turned = pltpu.roll(profile + pltpu.roll(profile, HALF, 1), first_row, 1)
        keep = lower_half == (lax.rem(patch, 2) == 0)
        row_block[patch] = jnp.where(keep, turned, 0.0).astype(BF16)
        own = jnp.broadcast_to(weight[patch], eye.shape)
        own = jnp.sum(jnp.where(eye, own, 0.0), axis=1, keepdims=True)
        weight_lanes[patch] = jnp.where(keep[: own.shape[0]], own, 0.0)
        return carry

    lax.fori_loop(0, patches, prepare, 0)


def solve_kernel(
    fibres,
    waves,
    row_off_in,
    col_off_in,
    dest_in,
    halo_one,
    halo_near,
    halo_far,
    products,
    weights_w,
    upper_wx,
    lower_wx,
    fibre,
    row_block,
    weight_lanes,
    send,
    numer,
    row_off,
    col_off,
    dest,
    halo_w,
    halo_wx,
    top_w,
    top_upper,
    top_lower,
    matrix,
    tails,
    estimate,
    residual,
    direction,
    imaged,
    across,
    partial,
    norm,
    packed,
    counts,
    slots,
    arrived,
):
    copies = start_copies(
        (row_off_in, col_off_in, dest_in), (row_off, col_off, dest), arrived
    )
    patches = products.shape[0]
    pairs = patches // 2
    blocks = fibres // SUB
    main = blocks * SUB
    padded_f = up(fibres, SUB)
    padded_p = up(patches, SUB)
    tiles = block_tiles(fibres)
    rank = lax.axis_index("section") * lax.axis_size("patch") + lax.axis_index("patch")
    odd = lax.rem(rank, 2) == 1

    for slot, sources in enumerate(((halo_one,), (halo_near, halo_far))):
        rows = slice(slot * HALO, (slot + 1) * HALO)
        values, inverse = (
            sum(source[channel].astype(F32) for source in sources) for channel in range(2)
        )
        for piece, value in enumerate(split_lanes(inverse)):
            halo_w[piece, rows, :] = value
        for piece, value in enumerate(split_lanes(inverse * values)):
            halo_wx[piece, rows, :] = value
    partial[...] = jnp.zeros_like(partial)
    halo_row = lax.broadcasted_iota(jnp.int32, (HALO, LANES), 0)
    empty = jnp.zeros((PR, PC), BF16)
    copies[0].wait()
    copies[1].wait()

    def beside_own(edge, own):
        return jnp.concatenate([edge, own.astype(F32)[HALO:]], axis=0).astype(BF16)

    def cut_halo(patch):
        first_row = row_off[patch]
        first_col = col_off[patch]
        base = first_col // LANES
        shift = first_col - base * LANES
        take_one = (halo_row >= first_row) == odd
        edges = []
        for source in (halo_w, halo_wx):
            pieces = [
                jnp.where(
                    take_one,
                    source[base + piece, 0:HALO, :],
                    source[base + piece, HALO : 2 * HALO, :],
                )
                for piece in range(PC // LANES + 1)
            ]
            edges.append(jnp.concatenate(shifted(pieces, shift), axis=1))
        above = edges[1].astype(BF16).astype(F32)
        top_w[patch] = beside_own(edges[0], weights_w[patch, : 2 * HALO, :])
        top_upper[patch] = beside_own(above, upper_wx[patch, : 2 * HALO, :])
        top_lower[patch] = beside_own(edges[1] - above, lower_wx[patch, : 2 * HALO, :])

    fewer = pairs // 4 * 2
    members = [list(range(fewer)), list(range(fewer, pairs))]

    def set_partial(pair, value):
        half = int(pair >= fewer)
        row = members[half].index(pair)
        partial[half, row : row + 1, :] = value

    def whole(top, own, patch):
        return jnp.concatenate([top[patch], own[patch, 2 * HALO :, :]], axis=0)

    def diagonal(first, second):
        return jnp.concatenate(
            [
                jnp.concatenate(first + [empty] * len(second), axis=1),
                jnp.concatenate([empty] * len(first) + second, axis=1),
            ],
            axis=0,
        )

    def begin(half):
        some = members[half]
        for pair in some:
            cut_halo(2 * pair)
            cut_halo(2 * pair + 1)
        for pair in some:
            one, two = 2 * pair, 2 * pair + 1
            imaged[pair] = dot_nt(
                jnp.concatenate([fibre[one], fibre[one], fibre[two], fibre[two]], axis=1),
                diagonal(
                    [whole(top_upper, upper_wx, one), whole(top_lower, lower_wx, one)],
                    [whole(top_upper, upper_wx, two), whole(top_lower, lower_wx, two)],
                ),
            )
        for pair in some:
            rhs = two_pass(dot_nt, imaged[pair], row_block[pair])
            residual[pair] = rhs
            direction[pair] = rhs
            estimate[pair] = jnp.zeros_like(rhs)
            set_partial(pair, jnp.sum(rhs * rhs, axis=0, keepdims=True))
        norm[half] = patch_sums(partial[half])

    def build(pair):
        one, two = 2 * pair, 2 * pair + 1
        blended = dot_nt(
            jnp.concatenate([products[one], products[two]], axis=1),
            diagonal(
                [whole(top_w, weights_w, one)] * 2,
                [whole(top_w, weights_w, two)] * 2,
            ),
        )
        for index, (f, t) in enumerate(tiles):
            value = blended[index * SUB : (index + 1) * SUB]
            if f < main:
                matrix[pair, f * main + t * SUB : f * main + (t + 1) * SUB, :] = value
                if t > f // SUB:
                    matrix[pair, pl.ds(t * SUB * main + f, SUB, stride=main), :] = value
            else:
                if t < blocks:
                    matrix[pair, f * main + t * SUB : f * main + (t + 1) * SUB, :] = value
                tails[pair, f - main, t * SUB : (t + 1) * SUB, :] = value

    lower_half = lax.broadcasted_iota(jnp.int32, partial.shape[1:], 1) < HALF

    def patch_sums(value):
        first = jnp.sum(jnp.where(lower_half, value, 0.0), axis=1, keepdims=True)
        second = jnp.sum(jnp.where(lower_half, 0.0, value), axis=1, keepdims=True)
        return jnp.where(lower_half, first, second)

    def apply(dot, source, target, some):
        sides = [jnp.concatenate(two_parts(source[pair]), axis=0) for pair in some]
        blocks = [row_block[pair] for pair in some]
        if len(some) > 1:
            none = jnp.zeros_like(blocks[0])
            blocks = [
                jnp.concatenate(
                    [block if here == there else none for there in range(len(some))], axis=1
                )
                for here, block in enumerate(blocks)
            ]
        both = dot(jnp.concatenate(sides, axis=1), jnp.concatenate(blocks, axis=0))
        for index, pair in enumerate(some):
            lanes = both[:, index * LANES : (index + 1) * LANES]
            target[pair] = lanes[:padded_f] + lanes[padded_f:]

    def blend(pair):
        totals = [jnp.zeros((main, LANES), F32)] * 2
        for f in range(fibres):
            totals[f % 2] = totals[f % 2] + (
                matrix[pair, f * main : (f + 1) * main, :] * across[pair, f : f + 1, :]
            )
        total = totals[0] + totals[1]
        imaged[pair, 0:main, :] = total
        product = jnp.sum(total * across[pair, 0:main, :], axis=0, keepdims=True)
        if fibres > main:
            rest = jnp.zeros((padded_f - main, LANES), F32)
            row = lax.broadcasted_iota(jnp.int32, rest.shape, 0)
            for f in range(main, fibres):
                one = jnp.sum(tails[pair, f - main] * across[pair], axis=0, keepdims=True)
                rest = jnp.where(row == f - main, one, rest)
                product = product + one * across[pair, f : f + 1, :]
            imaged[pair, main:padded_f, :] = rest
        set_partial(pair, product)

    def image(half, folded=True, beside=()):
        some = [members[half][at : at + 2] for at in range(0, len(members[half]), 2)]
        turns = len(some) + 2
        share = -(-len(beside) // turns)
        for turn in range(turns):
            for work in beside[turn * share : (turn + 1) * share]:
                work()
            if turn < len(some):
                apply(dot_nn, direction, across, some[turn])
            if 0 <= turn - 1 < len(some):
                for pair in some[turn - 1]:
                    blend(pair)
            if folded and 0 <= turn - 2:
                apply(dot_nt, imaged, imaged, some[turn - 2])

    def advance(half):
        curvature = patch_sums(partial[half])
        step_size = norm[half] / jnp.where(curvature > 0.0, curvature, 1.0)
        sizes = [step_size[row : row + 1] for row in range(len(members[half]))]
        for size, pair in zip(sizes, members[half]):
            estimate[pair] = estimate[pair] + size * direction[pair]
        return sizes

    def move(half):
        sizes = advance(half)
        for size, pair in zip(sizes, members[half]):
            rest = residual[pair] - size * imaged[pair]
            residual[pair] = rest
            set_partial(pair, jnp.sum(rest * rest, axis=0, keepdims=True))
        norm_now = norm[half]
        norm_next = patch_sums(partial[half])
        ratio = norm_next / jnp.where(norm_now > 0.0, norm_now, 1.0)
        for row, pair in enumerate(members[half]):
            direction[pair] = residual[pair] + ratio[row : row + 1] * direction[pair]
        norm[half] = norm_next

    copies[2].wait()
    for index in range(send.shape[0]):
        counts[index] = 0
    for patch in range(patches):
        target = dest[patch]
        slot = counts[target]
        counts[target] = slot + 1
        slots[patch] = slot
    packed[...] = jnp.zeros_like(packed)
    numer[...] = jnp.zeros_like(numer)
    upper_rows = (fibres + 1) // 2
    lane_f = lax.broadcasted_iota(jnp.int32, (padded_f, LANES), 1)
    at_wave = lax.rem(lane_f, HALF) == waves
    unit = jnp.where(at_wave, 1.0, 0.0)

    def hand_over(pair):
        spectra = estimate[pair]
        weighted = (spectra + unit) * (weight_lanes[2 * pair] + weight_lanes[2 * pair + 1])
        for half in range(2):
            value = pltpu.roll(weighted, HALF, 1) if half else weighted
            numer[pl.ds(2 * pair + half, fibres, stride=padded_p), :] = value[:fibres]
        size = jnp.abs(spectra)
        first = jnp.max(jnp.where(lane_f < HALF, size, 0.0), axis=1, keepdims=True)
        second = jnp.max(jnp.where(lane_f < HALF, 0.0, size), axis=1, keepdims=True)
        largest = jnp.where(lane_f < HALF, first, second)
        power = jnp.floor(jnp.log2(jnp.maximum(largest, TINY))) + 1.0
        coded = jnp.clip(jnp.round(spectra * jnp.exp2(CODE_BITS - power)), -CODE_TOP, CODE_TOP)
        coded = jnp.where(at_wave, power, coded)
        turned = pltpu.roll(coded, HALF, 1)
        for half in range(2):
            here = turned if half else coded
            away = coded if half else turned
            compact = jnp.where(
                lane_f[:upper_rows] < HALF,
                here[:upper_rows],
                jnp.concatenate(
                    [away[upper_rows:fibres], away[: 2 * upper_rows - fibres]], axis=0
                ),
            )
            rows = pl.ds(slots[2 * pair + half] * upper_rows, upper_rows)
            packed[dest[2 * pair + half], rows, :] = compact

    begin(0)
    for pair in members[0]:
        build(pair)
    begin(1)
    image(0, beside=[functools.partial(build, pair) for pair in members[1]])
    image(1)
    move(0)
    for _ in range(ITERS - 2):
        image(0)
        move(1)
        image(1)
        move(0)
    image(0, folded=False)
    move(1)
    advance(0)
    image(1, folded=False, beside=[functools.partial(hand_over, pair) for pair in members[0]])
    advance(1)
    for pair in members[1]:
        hand_over(pair)
    for index in range(send.shape[0]):
        send[index] = packed[index].astype(jnp.int32).astype(jnp.int16)


def finish_kernel(capacity, received, numer, others, spectra_ext, coadd):
    fibres, patches, waves = coadd.shape
    padded_p = up(patches, SUB)
    for f in range(fibres):
        rows = slice(f * padded_p, (f + 1) * padded_p)
        total = numer[rows, :]
        for index in range(others.shape[0]):
            total = total + others[index, rows, :]
        total = total[:patches]
        coadd[f] = total[:, :waves] / total[:, waves : waves + 1]
    upper_rows = (fibres + 1) // 2
    lower_half = lax.broadcasted_iota(jnp.int32, received.shape[1:], 1) < HALF
    for source in range(received.shape[0]):
        coded = received[source].astype(jnp.int32).astype(F32)
        power = jnp.where(
            lower_half, coded[:, waves : waves + 1], coded[:, HALF + waves : HALF + waves + 1]
        )
        value = coded * jnp.exp2(power - CODE_BITS)
        turned = pltpu.roll(value, HALF, 1)
        for slot in range(capacity):
            entry = source * capacity + slot
            at = slot * upper_rows
            spectra_ext[entry, 0:upper_rows, 0, :] = value[at : at + upper_rows, :waves]
            at_end = at + fibres - upper_rows
            spectra_ext[entry, upper_rows:fibres, 0, :] = turned[at:at_end, :waves]


def vmem(count=1):
    return [pl.BlockSpec(memory_space=pltpu.VMEM)] * count


def hbm(count=1):
    return [pl.BlockSpec(memory_space=pltpu.HBM)] * count


def prepare(exposure, row_prof, col_prof, row_off, col_off, weight):
    patches = row_prof.shape[0]
    fibres = col_prof.shape[0]
    _, band, columns = exposure.shape
    padded_f = up(fibres, SUB)
    padded_p = up(patches, SUB)
    rows = SUB * len(block_tiles(fibres))

    def made(*shape):
        return jax.ShapeDtypeStruct((patches,) + shape, BF16)

    return list(
        pl.pallas_call(
        prepare_kernel,
        out_shape=(
            made(rows, 2 * PC),
            made(PR, PC),
            made(PR, PC),
            made(PR, PC),
            made(padded_f, PC),
            made(HALF, LANES),
            jax.ShapeDtypeStruct((patches, padded_f, LANES), F32),
        ),
        in_specs=hbm(2) + vmem(4),
        out_specs=tuple(vmem(7)),
        scratch_shapes=[
            pltpu.SMEM(row_off.shape, row_off.dtype),
            pltpu.SMEM(col_off.shape, col_off.dtype),
            pltpu.VMEM((columns // LANES + 1, band, LANES), F32),
            pltpu.VMEM((columns // LANES + 1, band, LANES), F32),
            pltpu.VMEM((PC // LANES, fibres * padded_p, LANES), F32),
            pltpu.VMEM((padded_f, PC), F32),
            pltpu.VMEM((HALF, LANES), F32),
            pltpu.SemaphoreType.DMA((2,)),
        ],
        cost_estimate=pl.CostEstimate(
            flops=patches * rows * PC * 8, bytes_accessed=16 * 1024 * 1024, transcendentals=0
        ),
        compiler_params=pltpu.CompilerParams(vmem_limit_bytes=24 * 1024 * 1024),
    )(row_off, col_off, exposure, row_prof, col_prof, weight)
    )


def solve(halos, prepared, fibres, waves, row_off, col_off, dest, group):
    patches = dest.shape[0]
    columns = halos[0].shape[2]
    capacity = (patches + group - 1) // group
    pairs = patches // 2
    main = fibres // SUB * SUB
    padded_f = up(fibres, SUB)
    code_rows = up(capacity * ((fibres + 1) // 2), SUB)
    vectors = pltpu.VMEM((pairs, padded_f, LANES), F32)
    sums = pltpu.VMEM((2, up(pairs - pairs // 4 * 2, SUB), LANES), F32)
    tops = pltpu.VMEM((patches, 2 * HALO, PC), BF16)
    halo_band = pltpu.VMEM((columns // LANES + 1, 2 * HALO, LANES), F32)
    return pl.pallas_call(
        functools.partial(solve_kernel, fibres, waves),
        out_shape=(
            jax.ShapeDtypeStruct((group, code_rows, LANES), jnp.int16),
            jax.ShapeDtypeStruct((fibres * up(patches, SUB), LANES), F32),
        ),
        in_specs=hbm(3) + vmem(10),
        out_specs=tuple(vmem(2)),
        scratch_shapes=[
            pltpu.SMEM(row_off.shape, row_off.dtype),
            pltpu.SMEM(col_off.shape, col_off.dtype),
            pltpu.SMEM(dest.shape, dest.dtype),
            halo_band,
            halo_band,
            tops,
            tops,
            tops,
            pltpu.VMEM((pairs, fibres * main, LANES), F32),
            pltpu.VMEM((pairs, max(fibres - main, 1), padded_f, LANES), F32),
            vectors,
            vectors,
            vectors,
            vectors,
            vectors,
            sums,
            sums,
            pltpu.VMEM((group, code_rows, LANES), F32),
            pltpu.SMEM((group,), jnp.int32),
            pltpu.SMEM((patches,), jnp.int32),
            pltpu.SemaphoreType.DMA((3,)),
        ],
        compiler_params=pltpu.CompilerParams(vmem_limit_bytes=24 * 1024 * 1024),
    )(row_off, col_off, dest, *halos, *prepared)


def finish(received, numer, others, capacity, patches, fibres, waves):
    entries = received.shape[0] * capacity
    return pl.pallas_call(
        functools.partial(finish_kernel, capacity),
        out_shape=(
            jax.ShapeDtypeStruct((entries, fibres, 1, waves), F32),
            jax.ShapeDtypeStruct((fibres, patches, waves), F32),
        ),
        in_specs=vmem(3),
        out_specs=tuple(vmem(2)),
        compiler_params=pltpu.CompilerParams(vmem_limit_bytes=16 * 1024 * 1024),
    )(received, numer, others)


def edge_kernel(exposure, two, one):
    rank = lax.axis_index("section") * lax.axis_size("patch") + lax.axis_index("patch")
    even = lax.rem(rank, 2) == 0
    band = exposure.shape[1]
    for channel in range(exposure.shape[0]):
        top = exposure[channel, 0:HALO, :].astype(F32)
        bottom = exposure[channel, band - HALO : band, :].astype(F32)
        one[channel] = jnp.where(even, bottom, top).astype(BF16)
        two[channel] = jnp.where(even, top, bottom).astype(BF16)


def edges(exposure):
    channels, _, columns = exposure.shape
    return pl.pallas_call(
        edge_kernel,
        out_shape=(jax.ShapeDtypeStruct((channels, HALO, columns), BF16),) * 2,
        in_specs=vmem(1),
        out_specs=tuple(vmem(2)),
        cost_estimate=pl.CostEstimate(
            flops=EDGE_FLOPS, bytes_accessed=EDGE_BYTES, transcendentals=0
        ),
        compiler_params=pltpu.CompilerParams(vmem_limit_bytes=8 * 1024 * 1024),
    )(exposure)


def neighbours(block):
    axes = ("section", "patch")
    count = lax.axis_size(axes)
    group = lax.axis_size("patch")
    two, one = edges(block)

    def exchange(value, firsts):
        pairs = [(i, i + 1) for i in firsts if i + 1 < count]
        return lax.ppermute(value, axes, pairs + [(b, a) for a, b in pairs])

    odd = range(1, count, 2)
    far = [i for i in odd if (i + 1) % group == 0]
    near = [i for i in odd if (i + 1) % group]
    return [exchange(one, range(0, count, 2)), exchange(two, near), exchange(two, far)]


def local(exposure, row_prof, col_prof, row_off, col_off, dest, fibre_weight):
    group = lax.axis_size("patch")
    frames = lax.axis_size("frame")
    patches = dest.shape[1]
    fibres, waves = col_prof.shape[2], row_prof.shape[2]
    capacity = (patches + group - 1) // group
    halos = neighbours(exposure[0])
    prepared = prepare(
        exposure[0],
        row_prof[0],
        col_prof[0].transpose(1, 0, 2),
        row_off[0],
        col_off[0],
        fibre_weight[0][:, None, :],
    )
    prepared[5] = prepared[5].reshape(patches // 2, LANES, LANES)
    send, numer = solve(halos, prepared, fibres, waves, row_off[0], col_off[0], dest[0], group)
    received = lax.all_to_all(send, "patch", split_axis=0, concat_axis=0, tiled=True)
    others = jnp.stack(
        [
            lax.ppermute(numer, "frame", [(i, (i + hop) % frames) for i in range(frames)])
            for hop in range(1, frames)
        ]
    )
    spectra_ext, coadd = finish(received, numer, others, capacity, patches, fibres, waves)
    return spectra_ext.transpose(2, 0, 3, 1), coadd.transpose(1, 2, 0)


def solution(mesh):
    in_specs = (
        P("frame", None, ("section", "patch"), None),
        P("frame", ("section", "patch"), None, None),
        P("frame", ("section", "patch"), None, None),
        P("frame", ("section", "patch")),
        P("frame", ("section", "patch")),
        P("frame", ("section", "patch")),
        P("frame", ("section", "patch"), None),
    )
    out_specs = (P("frame", ("section", "patch"), None, None), P(("section", "patch"), None, None))
    return jax.shard_map(local, mesh=mesh, in_specs=in_specs, out_specs=out_specs, check_vma=False)
```

```python
import functools

import jax
import jax.numpy as jnp
from jax import lax
from jax.experimental import pallas as pl
from jax.experimental.pallas import tpu as pltpu
from jax.sharding import PartitionSpec as P

HALO = 8
PC = 256
ITERS = 6
PR = 64
LANES = 128
SUB = 8
HALF = LANES // 2
CODE_BITS = 15.0
CODE_TOP = 32767.0
TINY = 1e-30
EDGE_FLOPS = 1 << 34
EDGE_BYTES = 1 << 27
F32 = jnp.float32
BF16 = jnp.bfloat16


def up(count, multiple):
    return -(-count // multiple) * multiple


def dot_nt(lhs, rhs):
    return lax.dot_general(lhs, rhs, (((1,), (1,)), ((), ())), preferred_element_type=F32)


def dot_nn(lhs, rhs):
    return lax.dot_general(lhs, rhs, (((1,), (0,)), ((), ())), preferred_element_type=F32)


def two_parts(value):
    high = value.astype(BF16)
    return high, (value - high.astype(F32)).astype(BF16)


def two_pass(dot, value, weights):
    rows = value.shape[0]
    both = dot(jnp.concatenate(two_parts(value), axis=0), weights)
    return both[:rows] + both[rows:]


def block_tiles(fibres):
    blocks = fibres // SUB
    tiles = [(f, t) for f in range(blocks * SUB) for t in range(f // SUB, blocks)]
    for f in range(blocks * SUB, fibres):
        tiles += [(f, t) for t in range(up(fibres, SUB) // SUB)]
    return tiles


def split_lanes(value):
    return [value[:, at : at + LANES] for at in range(0, value.shape[1], LANES)]


def shifted(pieces, shift):
    rows = pieces[0].shape[0]
    turned = [pltpu.roll(piece, LANES - shift, 1) for piece in pieces]
    inside = lax.broadcasted_iota(jnp.int32, (rows, LANES), 1) < LANES - shift
    return [jnp.where(inside, turned[i], turned[i + 1]) for i in range(len(pieces) - 1)]


def start_copies(sources, targets, arrived):
    copies = [
        pltpu.make_async_copy(source, target, arrived.at[index])
        for index, (source, target) in enumerate(zip(sources, targets))
    ]
    for copy in copies:
        copy.start()
    return copies


def prepare_kernel(
    row_off_in,
    col_off_in,
    exposure,
    row_prof,
    col_prof,
    weight,
    products,
    weights_w,
    upper_wx,
    lower_wx,
    fibre,
    row_block,
    weight_lanes,
    row_off,
    col_off,
    band_w,
    band_wx,
    prof,
    fibre_rows,
    cut_row,
    arrived,
):
    copies = start_copies((row_off_in, col_off_in), (row_off, col_off), arrived)
    patches, waves, _ = row_prof.shape
    fibres = col_prof.shape[0]
    columns = exposure.shape[2]
    padded_p = up(patches, SUB)
    tiles = block_tiles(fibres)
    inverse = exposure[1].astype(F32)
    scaled = inverse * exposure[0].astype(F32)
    for piece, value in enumerate(split_lanes(inverse)):
        band_w[piece] = value
    for piece, value in enumerate(split_lanes(scaled)):
        band_wx[piece] = value
    for f in range(fibres):
        for piece, value in enumerate(split_lanes(col_prof[f].astype(F32))):
            prof[piece, f * padded_p : f * padded_p + patches, :] = value
    for copy in copies:
        copy.wait()
    cut_row[...] = jnp.zeros_like(cut_row)
    fibre_rows[...] = jnp.zeros_like(fibre_rows)
    halo = jnp.zeros((HALO, LANES), F32)
    square = (fibre.shape[1], fibres)
    eye = lax.broadcasted_iota(jnp.int32, square, 0) == lax.broadcasted_iota(jnp.int32, square, 1)
    lower_half = lax.broadcasted_iota(jnp.int32, (HALF, LANES), 1) < HALF

    def prepare(patch, carry):
        first_row = row_off[patch]
        first_col = col_off[patch]
        base = first_col // LANES
        shift = first_col - base * LANES
        count = PC // LANES
        window = shifted([band_w[base + piece] for piece in range(count + 1)], shift)
        for piece, value in enumerate(window):
            lanes = slice(piece * LANES, (piece + 1) * LANES)
            weights_w[patch, :, lanes] = jnp.concatenate([halo, value], axis=0).astype(BF16)
        window = shifted([band_wx[base + piece] for piece in range(count + 1)], shift)
        for piece, value in enumerate(window):
            lanes = slice(piece * LANES, (piece + 1) * LANES)
            upper, lower = two_parts(jnp.concatenate([halo, value], axis=0))
            upper_wx[patch, :, lanes] = upper
            lower_wx[patch, :, lanes] = lower
        for piece in range(count):
            lanes = slice(piece * LANES, (piece + 1) * LANES)
            fibre_rows[0:fibres, lanes] = prof[piece, pl.ds(patch, fibres, stride=padded_p), :]
        fibre[patch] = fibre_rows[...].astype(BF16)
        for at in range(0, len(tiles), 2):
            value = jnp.concatenate(
                [
                    fibre_rows[f : f + 1, :] * fibre_rows[t * SUB : (t + 1) * SUB, :]
                    for f, t in tiles[at : at + 2]
                ],
                axis=0,
            )
            upper, lower = two_parts(value)
            products[patch, at * SUB : (at + 2) * SUB, 0:PC] = upper
            products[patch, at * SUB : (at + 2) * SUB, PC : 2 * PC] = lower
        cut_row[0:waves, 0:PR] = row_prof[patch].astype(F32)
        profile = cut_row[...]
        turned = pltpu.roll(profile + pltpu.roll(profile, HALF, 1), first_row, 1)
        keep = lower_half == (lax.rem(patch, 2) == 0)
        row_block[patch] = jnp.where(keep, turned, 0.0).astype(BF16)
        own = jnp.broadcast_to(weight[patch], eye.shape)
        own = jnp.sum(jnp.where(eye, own, 0.0), axis=1, keepdims=True)
        weight_lanes[patch] = jnp.where(keep[: own.shape[0]], own, 0.0)
        return carry

    lax.fori_loop(0, patches, prepare, 0)


def solve_kernel(
    fibres,
    waves,
    row_off_in,
    col_off_in,
    dest_in,
    halo_one,
    halo_far,
    halo_near,
    products,
    weights_w,
    upper_wx,
    lower_wx,
    fibre,
    row_block,
    weight_lanes,
    send,
    numer,
    row_off,
    col_off,
    dest,
    halo_w,
    halo_wx,
    top_w,
    top_upper,
    top_lower,
    matrix,
    tails,
    estimate,
    residual,
    direction,
    imaged,
    across,
    partial,
    norm,
    packed,
    counts,
    slots,
    arrived,
):
    copies = start_copies(
        (row_off_in, col_off_in, dest_in), (row_off, col_off, dest), arrived
    )
    patches = products.shape[0]
    pairs = patches // 2
    blocks = fibres // SUB
    main = blocks * SUB
    padded_f = up(fibres, SUB)
    padded_p = up(patches, SUB)
    tiles = block_tiles(fibres)
    rank = lax.axis_index("section") * lax.axis_size("patch") + lax.axis_index("patch")
    odd = lax.rem(rank, 2) == 1

    for slot, sources in enumerate(((halo_one,), (halo_far, halo_near))):
        rows = slice(slot * HALO, (slot + 1) * HALO)
        values, inverse = (
            sum(source[channel].astype(F32) for source in sources) for channel in range(2)
        )
        for piece, value in enumerate(split_lanes(inverse)):
            halo_w[piece, rows, :] = value
        for piece, value in enumerate(split_lanes(inverse * values)):
            halo_wx[piece, rows, :] = value
    partial[...] = jnp.zeros_like(partial)
    halo_row = lax.broadcasted_iota(jnp.int32, (HALO, LANES), 0)
    empty = jnp.zeros((PR, PC), BF16)
    copies[0].wait()
    copies[1].wait()

    def beside_own(edge, own):
        return jnp.concatenate([edge, own.astype(F32)[HALO:]], axis=0).astype(BF16)

    def cut_halo(patch):
        first_row = row_off[patch]
        first_col = col_off[patch]
        base = first_col // LANES
        shift = first_col - base * LANES
        take_one = (halo_row >= first_row) == odd
        edges = []
        for source in (halo_w, halo_wx):
            pieces = [
                jnp.where(
                    take_one,
                    source[base + piece, 0:HALO, :],
                    source[base + piece, HALO : 2 * HALO, :],
                )
                for piece in range(PC // LANES + 1)
            ]
            edges.append(jnp.concatenate(shifted(pieces, shift), axis=1))
        above = edges[1].astype(BF16).astype(F32)
        top_w[patch] = beside_own(edges[0], weights_w[patch, : 2 * HALO, :])
        top_upper[patch] = beside_own(above, upper_wx[patch, : 2 * HALO, :])
        top_lower[patch] = beside_own(edges[1] - above, lower_wx[patch, : 2 * HALO, :])

    fewer = pairs // 4 * 2
    members = [list(range(fewer)), list(range(fewer, pairs))]

    def set_partial(pair, value):
        half = int(pair >= fewer)
        row = members[half].index(pair)
        partial[half, row : row + 1, :] = value

    def whole(top, own, patch):
        return jnp.concatenate([top[patch], own[patch, 2 * HALO :, :]], axis=0)

    def diagonal(first, second):
        return jnp.concatenate(
            [
                jnp.concatenate(first + [empty] * len(second), axis=1),
                jnp.concatenate([empty] * len(first) + second, axis=1),
            ],
            axis=0,
        )

    def begin(half):
        some = members[half]
        for pair in some:
            cut_halo(2 * pair)
            cut_halo(2 * pair + 1)
        for pair in some:
            one, two = 2 * pair, 2 * pair + 1
            imaged[pair] = dot_nt(
                jnp.concatenate([fibre[one], fibre[one], fibre[two], fibre[two]], axis=1),
                diagonal(
                    [whole(top_upper, upper_wx, one), whole(top_lower, lower_wx, one)],
                    [whole(top_upper, upper_wx, two), whole(top_lower, lower_wx, two)],
                ),
            )
        for pair in some:
            rhs = two_pass(dot_nt, imaged[pair], row_block[pair])
            residual[pair] = rhs
            direction[pair] = rhs
            estimate[pair] = jnp.zeros_like(rhs)
            set_partial(pair, jnp.sum(rhs * rhs, axis=0, keepdims=True))
        norm[half] = patch_sums(partial[half])

    def build(pair):
        one, two = 2 * pair, 2 * pair + 1
        blended = dot_nt(
            jnp.concatenate([products[one], products[two]], axis=1),
            diagonal(
                [whole(top_w, weights_w, one)] * 2,
                [whole(top_w, weights_w, two)] * 2,
            ),
        )
        for index, (f, t) in enumerate(tiles):
            value = blended[index * SUB : (index + 1) * SUB]
            if f < main:
                matrix[pair, f * main + t * SUB : f * main + (t + 1) * SUB, :] = value
                if t > f // SUB:
                    matrix[pair, pl.ds(t * SUB * main + f, SUB, stride=main), :] = value
            else:
                if t < blocks:
                    matrix[pair, f * main + t * SUB : f * main + (t + 1) * SUB, :] = value
                tails[pair, f - main, t * SUB : (t + 1) * SUB, :] = value

    lower_half = lax.broadcasted_iota(jnp.int32, partial.shape[1:], 1) < HALF

    def patch_sums(value):
        first = jnp.sum(jnp.where(lower_half, value, 0.0), axis=1, keepdims=True)
        second = jnp.sum(jnp.where(lower_half, 0.0, value), axis=1, keepdims=True)
        return jnp.where(lower_half, first, second)

    def apply(dot, source, target, some):
        sides = [jnp.concatenate(two_parts(source[pair]), axis=0) for pair in some]
        blocks = [row_block[pair] for pair in some]
        if len(some) > 1:
            none = jnp.zeros_like(blocks[0])
            blocks = [
                jnp.concatenate(
                    [block if here == there else none for there in range(len(some))], axis=1
                )
                for here, block in enumerate(blocks)
            ]
        both = dot(jnp.concatenate(sides, axis=1), jnp.concatenate(blocks, axis=0))
        for index, pair in enumerate(some):
            lanes = both[:, index * LANES : (index + 1) * LANES]
            target[pair] = lanes[:padded_f] + lanes[padded_f:]

    def blend(pair):
        totals = [jnp.zeros((main, LANES), F32)] * 2
        for f in range(fibres):
            totals[f % 2] = totals[f % 2] + (
                matrix[pair, f * main : (f + 1) * main, :] * across[pair, f : f + 1, :]
            )
        total = totals[0] + totals[1]
        imaged[pair, 0:main, :] = total
        product = jnp.sum(total * across[pair, 0:main, :], axis=0, keepdims=True)
        if fibres > main:
            rest = jnp.zeros((padded_f - main, LANES), F32)
            row = lax.broadcasted_iota(jnp.int32, rest.shape, 0)
            for f in range(main, fibres):
                one = jnp.sum(tails[pair, f - main] * across[pair], axis=0, keepdims=True)
                rest = jnp.where(row == f - main, one, rest)
                product = product + one * across[pair, f : f + 1, :]
            imaged[pair, main:padded_f, :] = rest
        set_partial(pair, product)

    def image(half, folded=True, beside=()):
        some = [members[half][at : at + 2] for at in range(0, len(members[half]), 2)]
        turns = len(some) + 2
        share = -(-len(beside) // turns)
        for turn in range(turns):
            for work in beside[turn * share : (turn + 1) * share]:
                work()
            if turn < len(some):
                apply(dot_nn, direction, across, some[turn])
            if 0 <= turn - 1 < len(some):
                for pair in some[turn - 1]:
                    blend(pair)
            if folded and 0 <= turn - 2:
                apply(dot_nt, imaged, imaged, some[turn - 2])

    def advance(half):
        curvature = patch_sums(partial[half])
        step_size = norm[half] / jnp.where(curvature > 0.0, curvature, 1.0)
        sizes = [step_size[row : row + 1] for row in range(len(members[half]))]
        for size, pair in zip(sizes, members[half]):
            estimate[pair] = estimate[pair] + size * direction[pair]
        return sizes

    def move(half):
        sizes = advance(half)
        for size, pair in zip(sizes, members[half]):
            rest = residual[pair] - size * imaged[pair]
            residual[pair] = rest
            set_partial(pair, jnp.sum(rest * rest, axis=0, keepdims=True))
        norm_now = norm[half]
        norm_next = patch_sums(partial[half])
        ratio = norm_next / jnp.where(norm_now > 0.0, norm_now, 1.0)
        for row, pair in enumerate(members[half]):
            direction[pair] = residual[pair] + ratio[row : row + 1] * direction[pair]
        norm[half] = norm_next

    copies[2].wait()
    for index in range(send.shape[0]):
        counts[index] = 0
    for patch in range(patches):
        target = dest[patch]
        slot = counts[target]
        counts[target] = slot + 1
        slots[patch] = slot
    packed[...] = jnp.zeros_like(packed)
    numer[...] = jnp.zeros_like(numer)
    upper_rows = (fibres + 1) // 2
    lane_f = lax.broadcasted_iota(jnp.int32, (padded_f, LANES), 1)
    at_wave = lax.rem(lane_f, HALF) == waves
    unit = jnp.where(at_wave, 1.0, 0.0)

    def hand_over(pair):
        spectra = estimate[pair]
        weighted = (spectra + unit) * (weight_lanes[2 * pair] + weight_lanes[2 * pair + 1])
        for half in range(2):
            value = pltpu.roll(weighted, HALF, 1) if half else weighted
            numer[pl.ds(2 * pair + half, fibres, stride=padded_p), :] = value[:fibres]
        size = jnp.abs(spectra)
        first = jnp.max(jnp.where(lane_f < HALF, size, 0.0), axis=1, keepdims=True)
        second = jnp.max(jnp.where(lane_f < HALF, 0.0, size), axis=1, keepdims=True)
        largest = jnp.where(lane_f < HALF, first, second)
        power = jnp.floor(jnp.log2(jnp.maximum(largest, TINY))) + 1.0
        coded = jnp.clip(jnp.round(spectra * jnp.exp2(CODE_BITS - power)), -CODE_TOP, CODE_TOP)
        coded = jnp.where(at_wave, power, coded)
        turned = pltpu.roll(coded, HALF, 1)
        for half in range(2):
            here = turned if half else coded
            away = coded if half else turned
            compact = jnp.where(
                lane_f[:upper_rows] < HALF,
                here[:upper_rows],
                jnp.concatenate(
                    [away[upper_rows:fibres], away[: 2 * upper_rows - fibres]], axis=0
                ),
            )
            rows = pl.ds(slots[2 * pair + half] * upper_rows, upper_rows)
            packed[dest[2 * pair + half], rows, :] = compact

    begin(0)
    for pair in members[0]:
        build(pair)
    begin(1)
    image(0, beside=[functools.partial(build, pair) for pair in members[1]])
    image(1)
    move(0)
    for _ in range(ITERS - 2):
        image(0)
        move(1)
        image(1)
        move(0)
    image(0, folded=False)
    move(1)
    advance(0)
    image(1, folded=False, beside=[functools.partial(hand_over, pair) for pair in members[0]])
    advance(1)
    for pair in members[1]:
        hand_over(pair)
    for index in range(send.shape[0]):
        send[index] = packed[index].astype(jnp.int32).astype(jnp.int16)


def finish_kernel(capacity, received, numer, others, spectra_ext, coadd):
    fibres, patches, waves = coadd.shape
    padded_p = up(patches, SUB)
    for f in range(fibres):
        rows = slice(f * padded_p, (f + 1) * padded_p)
        total = numer[rows, :]
        for index in range(others.shape[0]):
            total = total + others[index, rows, :]
        total = total[:patches]
        coadd[f] = total[:, :waves] / total[:, waves : waves + 1]
    upper_rows = (fibres + 1) // 2
    lower_half = lax.broadcasted_iota(jnp.int32, received.shape[1:], 1) < HALF
    for source in range(received.shape[0]):
        coded = received[source].astype(jnp.int32).astype(F32)
        power = jnp.where(
            lower_half, coded[:, waves : waves + 1], coded[:, HALF + waves : HALF + waves + 1]
        )
        value = coded * jnp.exp2(power - CODE_BITS)
        turned = pltpu.roll(value, HALF, 1)
        for slot in range(capacity):
            entry = source * capacity + slot
            at = slot * upper_rows
            spectra_ext[entry, 0:upper_rows, 0, :] = value[at : at + upper_rows, :waves]
            at_end = at + fibres - upper_rows
            spectra_ext[entry, upper_rows:fibres, 0, :] = turned[at:at_end, :waves]


def vmem(count=1):
    return [pl.BlockSpec(memory_space=pltpu.VMEM)] * count


def hbm(count=1):
    return [pl.BlockSpec(memory_space=pltpu.HBM)] * count


def prepare(exposure, row_prof, col_prof, row_off, col_off, weight):
    patches = row_prof.shape[0]
    fibres = col_prof.shape[0]
    _, band, columns = exposure.shape
    padded_f = up(fibres, SUB)
    padded_p = up(patches, SUB)
    rows = SUB * len(block_tiles(fibres))

    def made(*shape):
        return jax.ShapeDtypeStruct((patches,) + shape, BF16)

    return list(
        pl.pallas_call(
        prepare_kernel,
        out_shape=(
            made(rows, 2 * PC),
            made(PR, PC),
            made(PR, PC),
            made(PR, PC),
            made(padded_f, PC),
            made(HALF, LANES),
            jax.ShapeDtypeStruct((patches, padded_f, LANES), F32),
        ),
        in_specs=hbm(2) + vmem(4),
        out_specs=tuple(vmem(7)),
        scratch_shapes=[
            pltpu.SMEM(row_off.shape, row_off.dtype),
            pltpu.SMEM(col_off.shape, col_off.dtype),
            pltpu.VMEM((columns // LANES + 1, band, LANES), F32),
            pltpu.VMEM((columns // LANES + 1, band, LANES), F32),
            pltpu.VMEM((PC // LANES, fibres * padded_p, LANES), F32),
            pltpu.VMEM((padded_f, PC), F32),
            pltpu.VMEM((HALF, LANES), F32),
            pltpu.SemaphoreType.DMA((2,)),
        ],
        cost_estimate=pl.CostEstimate(
            flops=patches * rows * PC * 8, bytes_accessed=16 * 1024 * 1024, transcendentals=0
        ),
        compiler_params=pltpu.CompilerParams(vmem_limit_bytes=24 * 1024 * 1024),
    )(row_off, col_off, exposure, row_prof, col_prof, weight)
    )


def solve(halos, prepared, fibres, waves, row_off, col_off, dest, group):
    patches = dest.shape[0]
    columns = halos[0].shape[2]
    capacity = (patches + group - 1) // group
    pairs = patches // 2
    main = fibres // SUB * SUB
    padded_f = up(fibres, SUB)
    code_rows = up(capacity * ((fibres + 1) // 2), SUB)
    vectors = pltpu.VMEM((pairs, padded_f, LANES), F32)
    sums = pltpu.VMEM((2, up(pairs - pairs // 4 * 2, SUB), LANES), F32)
    tops = pltpu.VMEM((patches, 2 * HALO, PC), BF16)
    halo_band = pltpu.VMEM((columns // LANES + 1, 2 * HALO, LANES), F32)
    return pl.pallas_call(
        functools.partial(solve_kernel, fibres, waves),
        out_shape=(
            jax.ShapeDtypeStruct((group, code_rows, LANES), jnp.int16),
            jax.ShapeDtypeStruct((fibres * up(patches, SUB), LANES), F32),
        ),
        in_specs=hbm(3) + vmem(10),
        out_specs=tuple(vmem(2)),
        scratch_shapes=[
            pltpu.SMEM(row_off.shape, row_off.dtype),
            pltpu.SMEM(col_off.shape, col_off.dtype),
            pltpu.SMEM(dest.shape, dest.dtype),
            halo_band,
            halo_band,
            tops,
            tops,
            tops,
            pltpu.VMEM((pairs, fibres * main, LANES), F32),
            pltpu.VMEM((pairs, max(fibres - main, 1), padded_f, LANES), F32),
            vectors,
            vectors,
            vectors,
            vectors,
            vectors,
            sums,
            sums,
            pltpu.VMEM((group, code_rows, LANES), F32),
            pltpu.SMEM((group,), jnp.int32),
            pltpu.SMEM((patches,), jnp.int32),
            pltpu.SemaphoreType.DMA((3,)),
        ],
        compiler_params=pltpu.CompilerParams(vmem_limit_bytes=24 * 1024 * 1024),
    )(row_off, col_off, dest, *halos, *prepared)


def finish(received, numer, others, capacity, patches, fibres, waves):
    entries = received.shape[0] * capacity
    return pl.pallas_call(
        functools.partial(finish_kernel, capacity),
        out_shape=(
            jax.ShapeDtypeStruct((entries, fibres, 1, waves), F32),
            jax.ShapeDtypeStruct((fibres, patches, waves), F32),
        ),
        in_specs=vmem(3),
        out_specs=tuple(vmem(2)),
        compiler_params=pltpu.CompilerParams(vmem_limit_bytes=16 * 1024 * 1024),
    )(received, numer, others)


def edge_kernel(exposure, two, one):
    rank = lax.axis_index("section") * lax.axis_size("patch") + lax.axis_index("patch")
    even = lax.rem(rank, 2) == 0
    band = exposure.shape[1]
    for channel in range(exposure.shape[0]):
        top = exposure[channel, 0:HALO, :].astype(F32)
        bottom = exposure[channel, band - HALO : band, :].astype(F32)
        one[channel] = jnp.where(even, bottom, top).astype(BF16)
        two[channel] = jnp.where(even, top, bottom).astype(BF16)


def edges(exposure):
    channels, _, columns = exposure.shape
    return pl.pallas_call(
        edge_kernel,
        out_shape=(jax.ShapeDtypeStruct((channels, HALO, columns), BF16),) * 2,
        in_specs=vmem(1),
        out_specs=tuple(vmem(2)),
        cost_estimate=pl.CostEstimate(
            flops=EDGE_FLOPS, bytes_accessed=EDGE_BYTES, transcendentals=0
        ),
        compiler_params=pltpu.CompilerParams(vmem_limit_bytes=8 * 1024 * 1024),
    )(exposure)


def neighbours(block):
    axes = ("section", "patch")
    count = lax.axis_size(axes)
    group = lax.axis_size("patch")
    two, one = edges(block)

    def exchange(value, firsts):
        pairs = [(i, i + 1) for i in firsts if i + 1 < count]
        return lax.ppermute(value, axes, pairs + [(b, a) for a, b in pairs])

    odd = range(1, count, 2)
    far = [i for i in odd if (i + 1) % group == 0]
    near = [i for i in odd if (i + 1) % group]
    return [exchange(one, range(0, count, 2)), exchange(two, far), exchange(two, near)]


def local(exposure, row_prof, col_prof, row_off, col_off, dest, fibre_weight):
    group = lax.axis_size("patch")
    frames = lax.axis_size("frame")
    patches = dest.shape[1]
    fibres, waves = col_prof.shape[2], row_prof.shape[2]
    capacity = (patches + group - 1) // group
    halos = neighbours(exposure[0])
    prepared = prepare(
        exposure[0],
        row_prof[0],
        col_prof[0].transpose(1, 0, 2),
        row_off[0],
        col_off[0],
        fibre_weight[0][:, None, :],
    )
    prepared[5] = prepared[5].reshape(patches // 2, LANES, LANES)
    send, numer = solve(halos, prepared, fibres, waves, row_off[0], col_off[0], dest[0], group)
    received = lax.all_to_all(send, "patch", split_axis=0, concat_axis=0, tiled=True)
    others = jnp.stack(
        [
            lax.ppermute(numer, "frame", [(i, (i + hop) % frames) for i in range(frames)])
            for hop in range(1, frames)
        ]
    )
    spectra_ext, coadd = finish(received, numer, others, capacity, patches, fibres, waves)
    return spectra_ext.transpose(2, 0, 3, 1), coadd.transpose(1, 2, 0)


def solution(mesh):
    in_specs = (
        P("frame", None, ("section", "patch"), None),
        P("frame", ("section", "patch"), None, None),
        P("frame", ("section", "patch"), None, None),
        P("frame", ("section", "patch")),
        P("frame", ("section", "patch")),
        P("frame", ("section", "patch")),
        P("frame", ("section", "patch"), None),
    )
    out_specs = (P("frame", ("section", "patch"), None, None), P(("section", "patch"), None, None))
    return jax.shard_map(local, mesh=mesh, in_specs=in_specs, out_specs=out_specs, check_vma=False)
```

```python
import functools

import jax
import jax.numpy as jnp
from jax import lax
from jax.experimental import pallas as pl
from jax.experimental.pallas import tpu as pltpu
from jax.sharding import PartitionSpec as P

HALO = 8
PC = 256
ITERS = 6
PR = 64
LANES = 128
SUB = 8
HALF = LANES // 2
CODE_BITS = 15.0
CODE_TOP = 32767.0
TINY = 1e-30
EDGE_FLOPS = 1 << 34
EDGE_BYTES = 1 << 27
F32 = jnp.float32
BF16 = jnp.bfloat16


def up(count, multiple):
    return -(-count // multiple) * multiple


def dot_nt(lhs, rhs):
    return lax.dot_general(lhs, rhs, (((1,), (1,)), ((), ())), preferred_element_type=F32)


def dot_nn(lhs, rhs):
    return lax.dot_general(lhs, rhs, (((1,), (0,)), ((), ())), preferred_element_type=F32)


def two_parts(value):
    high = value.astype(BF16)
    return high, (value - high.astype(F32)).astype(BF16)


def two_pass(dot, value, weights):
    rows = value.shape[0]
    both = dot(jnp.concatenate(two_parts(value), axis=0), weights)
    return both[:rows] + both[rows:]


def block_tiles(fibres):
    blocks = fibres // SUB
    tiles = [(f, t) for f in range(blocks * SUB) for t in range(f // SUB, blocks)]
    for f in range(blocks * SUB, fibres):
        tiles += [(f, t) for t in range(up(fibres, SUB) // SUB)]
    return tiles


def split_lanes(value):
    return [value[:, at : at + LANES] for at in range(0, value.shape[1], LANES)]


def shifted(pieces, shift):
    rows = pieces[0].shape[0]
    turned = [pltpu.roll(piece, LANES - shift, 1) for piece in pieces]
    inside = lax.broadcasted_iota(jnp.int32, (rows, LANES), 1) < LANES - shift
    return [jnp.where(inside, turned[i], turned[i + 1]) for i in range(len(pieces) - 1)]


def start_copies(sources, targets, arrived):
    copies = [
        pltpu.make_async_copy(source, target, arrived.at[index])
        for index, (source, target) in enumerate(zip(sources, targets))
    ]
    for copy in copies:
        copy.start()
    return copies


def prepare_kernel(
    row_off_in,
    col_off_in,
    exposure,
    row_prof,
    col_prof,
    weight,
    products,
    weights_w,
    upper_wx,
    lower_wx,
    fibre,
    row_block,
    weight_lanes,
    row_off,
    col_off,
    band_w,
    band_wx,
    prof,
    fibre_rows,
    cut_row,
    arrived,
):
    copies = start_copies((row_off_in, col_off_in), (row_off, col_off), arrived)
    patches, waves, _ = row_prof.shape
    fibres = col_prof.shape[0]
    columns = exposure.shape[2]
    padded_p = up(patches, SUB)
    tiles = block_tiles(fibres)
    inverse = exposure[1].astype(F32)
    scaled = inverse * exposure[0].astype(F32)
    for piece, value in enumerate(split_lanes(inverse)):
        band_w[piece] = value
    for piece, value in enumerate(split_lanes(scaled)):
        band_wx[piece] = value
    for f in range(fibres):
        for piece, value in enumerate(split_lanes(col_prof[f].astype(F32))):
            prof[piece, f * padded_p : f * padded_p + patches, :] = value
    for copy in copies:
        copy.wait()
    cut_row[...] = jnp.zeros_like(cut_row)
    fibre_rows[...] = jnp.zeros_like(fibre_rows)
    halo = jnp.zeros((HALO, LANES), F32)
    square = (fibre.shape[1], fibres)
    eye = lax.broadcasted_iota(jnp.int32, square, 0) == lax.broadcasted_iota(jnp.int32, square, 1)
    lower_half = lax.broadcasted_iota(jnp.int32, (HALF, LANES), 1) < HALF

    def prepare(patch, carry):
        first_row = row_off[patch]
        first_col = col_off[patch]
        base = first_col // LANES
        shift = first_col - base * LANES
        count = PC // LANES
        window = shifted([band_w[base + piece] for piece in range(count + 1)], shift)
        for piece, value in enumerate(window):
            lanes = slice(piece * LANES, (piece + 1) * LANES)
            weights_w[patch, :, lanes] = jnp.concatenate([halo, value], axis=0).astype(BF16)
        window = shifted([band_wx[base + piece] for piece in range(count + 1)], shift)
        for piece, value in enumerate(window):
            lanes = slice(piece * LANES, (piece + 1) * LANES)
            upper, lower = two_parts(jnp.concatenate([halo, value], axis=0))
            upper_wx[patch, :, lanes] = upper
            lower_wx[patch, :, lanes] = lower
        for piece in range(count):
            lanes = slice(piece * LANES, (piece + 1) * LANES)
            fibre_rows[0:fibres, lanes] = prof[piece, pl.ds(patch, fibres, stride=padded_p), :]
        fibre[patch] = fibre_rows[...].astype(BF16)
        for at in range(0, len(tiles), 2):
            value = jnp.concatenate(
                [
                    fibre_rows[f : f + 1, :] * fibre_rows[t * SUB : (t + 1) * SUB, :]
                    for f, t in tiles[at : at + 2]
                ],
                axis=0,
            )
            upper, lower = two_parts(value)
            products[patch, at * SUB : (at + 2) * SUB, 0:PC] = upper
            products[patch, at * SUB : (at + 2) * SUB, PC : 2 * PC] = lower
        cut_row[0:waves, 0:PR] = row_prof[patch].astype(F32)
        profile = cut_row[...]
        turned = pltpu.roll(profile + pltpu.roll(profile, HALF, 1), first_row, 1)
        keep = lower_half == (lax.rem(patch, 2) == 0)
        row_block[patch] = jnp.where(keep, turned, 0.0).astype(BF16)
        own = jnp.broadcast_to(weight[patch], eye.shape)
        own = jnp.sum(jnp.where(eye, own, 0.0), axis=1, keepdims=True)
        weight_lanes[patch] = jnp.where(keep[: own.shape[0]], own, 0.0)
        return carry

    lax.fori_loop(0, patches, prepare, 0)


def solve_kernel(
    fibres,
    waves,
    row_off_in,
    col_off_in,
    dest_in,
    halo_one,
    halo_near,
    halo_far,
    products,
    weights_w,
    upper_wx,
    lower_wx,
    fibre,
    row_block,
    weight_lanes,
    send,
    numer,
    row_off,
    col_off,
    dest,
    halo_w,
    halo_wx,
    top_w,
    top_upper,
    top_lower,
    matrix,
    tails,
    estimate,
    residual,
    direction,
    imaged,
    across,
    partial,
    norm,
    packed,
    counts,
    slots,
    arrived,
):
    copies = start_copies(
        (row_off_in, col_off_in, dest_in), (row_off, col_off, dest), arrived
    )
    patches = products.shape[0]
    pairs = patches // 2
    blocks = fibres // SUB
    main = blocks * SUB
    padded_f = up(fibres, SUB)
    padded_p = up(patches, SUB)
    tiles = block_tiles(fibres)
    rank = lax.axis_index("section") * lax.axis_size("patch") + lax.axis_index("patch")
    odd = lax.rem(rank, 2) == 1

    for slot, sources in enumerate(((halo_one,), (halo_near, halo_far))):
        rows = slice(slot * HALO, (slot + 1) * HALO)
        values, inverse = (
            sum(source[channel].astype(F32) for source in sources) for channel in range(2)
        )
        for piece, value in enumerate(split_lanes(inverse)):
            halo_w[piece, rows, :] = value
        for piece, value in enumerate(split_lanes(inverse * values)):
            halo_wx[piece, rows, :] = value
    partial[...] = jnp.zeros_like(partial)
    halo_row = lax.broadcasted_iota(jnp.int32, (HALO, LANES), 0)
    empty = jnp.zeros((PR, PC), BF16)
    packed[...] = jnp.zeros_like(packed)
    numer[...] = jnp.zeros_like(numer)
    for copy in copies:
        copy.wait()

    def beside_own(edge, own):
        return jnp.concatenate([edge, own.astype(F32)[HALO:]], axis=0).astype(BF16)

    def cut_halo(patch):
        first_row = row_off[patch]
        first_col = col_off[patch]
        base = first_col // LANES
        shift = first_col - base * LANES
        take_one = (halo_row >= first_row) == odd
        edges = []
        for source in (halo_w, halo_wx):
            pieces = [
                jnp.where(
                    take_one,
                    source[base + piece, 0:HALO, :],
                    source[base + piece, HALO : 2 * HALO, :],
                )
                for piece in range(PC // LANES + 1)
            ]
            edges.append(jnp.concatenate(shifted(pieces, shift), axis=1))
        above = edges[1].astype(BF16).astype(F32)
        top_w[patch] = beside_own(edges[0], weights_w[patch, : 2 * HALO, :])
        top_upper[patch] = beside_own(above, upper_wx[patch, : 2 * HALO, :])
        top_lower[patch] = beside_own(edges[1] - above, lower_wx[patch, : 2 * HALO, :])

    fewer = pairs // 4 * 2
    members = [list(range(fewer)), list(range(fewer, pairs))]

    def set_partial(pair, value):
        half = int(pair >= fewer)
        row = members[half].index(pair)
        partial[half, row : row + 1, :] = value

    def whole(top, own, patch):
        return jnp.concatenate([top[patch], own[patch, 2 * HALO :, :]], axis=0)

    def diagonal(first, second):
        return jnp.concatenate(
            [
                jnp.concatenate(first + [empty] * len(second), axis=1),
                jnp.concatenate([empty] * len(first) + second, axis=1),
            ],
            axis=0,
        )

    def begin(half):
        some = members[half]
        for pair in some:
            cut_halo(2 * pair)
            cut_halo(2 * pair + 1)
        for pair in some:
            one, two = 2 * pair, 2 * pair + 1
            imaged[pair] = dot_nt(
                jnp.concatenate([fibre[one], fibre[one], fibre[two], fibre[two]], axis=1),
                diagonal(
                    [whole(top_upper, upper_wx, one), whole(top_lower, lower_wx, one)],
                    [whole(top_upper, upper_wx, two), whole(top_lower, lower_wx, two)],
                ),
            )
        for pair in some:
            rhs = two_pass(dot_nt, imaged[pair], row_block[pair])
            residual[pair] = rhs
            direction[pair] = rhs
            estimate[pair] = jnp.zeros_like(rhs)
            set_partial(pair, jnp.sum(rhs * rhs, axis=0, keepdims=True))
        norm[half] = patch_sums(partial[half])

    def build(pair):
        one, two = 2 * pair, 2 * pair + 1
        blended = dot_nt(
            jnp.concatenate([products[one], products[two]], axis=1),
            diagonal(
                [whole(top_w, weights_w, one)] * 2,
                [whole(top_w, weights_w, two)] * 2,
            ),
        )
        for index, (f, t) in enumerate(tiles):
            value = blended[index * SUB : (index + 1) * SUB]
            if f < main:
                matrix[pair, f * main + t * SUB : f * main + (t + 1) * SUB, :] = value
                if t > f // SUB:
                    matrix[pair, pl.ds(t * SUB * main + f, SUB, stride=main), :] = value
            else:
                if t < blocks:
                    matrix[pair, f * main + t * SUB : f * main + (t + 1) * SUB, :] = value
                tails[pair, f - main, t * SUB : (t + 1) * SUB, :] = value

    lower_half = lax.broadcasted_iota(jnp.int32, partial.shape[1:], 1) < HALF

    def patch_sums(value):
        first = jnp.sum(jnp.where(lower_half, value, 0.0), axis=1, keepdims=True)
        second = jnp.sum(jnp.where(lower_half, 0.0, value), axis=1, keepdims=True)
        return jnp.where(lower_half, first, second)

    def apply(dot, source, target, some):
        sides = [jnp.concatenate(two_parts(source[pair]), axis=0) for pair in some]
        blocks = [row_block[pair] for pair in some]
        if len(some) > 1:
            none = jnp.zeros_like(blocks[0])
            blocks = [
                jnp.concatenate(
                    [block if here == there else none for there in range(len(some))], axis=1
                )
                for here, block in enumerate(blocks)
            ]
        both = dot(jnp.concatenate(sides, axis=1), jnp.concatenate(blocks, axis=0))
        for index, pair in enumerate(some):
            lanes = both[:, index * LANES : (index + 1) * LANES]
            target[pair] = lanes[:padded_f] + lanes[padded_f:]

    def blend(pair):
        totals = [jnp.zeros((main, LANES), F32)] * 2
        for f in range(fibres):
            totals[f % 2] = totals[f % 2] + (
                matrix[pair, f * main : (f + 1) * main, :] * across[pair, f : f + 1, :]
            )
        total = totals[0] + totals[1]
        imaged[pair, 0:main, :] = total
        product = jnp.sum(total * across[pair, 0:main, :], axis=0, keepdims=True)
        if fibres > main:
            rest = jnp.zeros((padded_f - main, LANES), F32)
            row = lax.broadcasted_iota(jnp.int32, rest.shape, 0)
            for f in range(main, fibres):
                one = jnp.sum(tails[pair, f - main] * across[pair], axis=0, keepdims=True)
                rest = jnp.where(row == f - main, one, rest)
                product = product + one * across[pair, f : f + 1, :]
            imaged[pair, main:padded_f, :] = rest
        set_partial(pair, product)

    def image(half, folded=True, beside=()):
        some = [members[half][at : at + 2] for at in range(0, len(members[half]), 2)]
        turns = len(some) + 2
        share = -(-len(beside) // turns)
        for turn in range(turns):
            for work in beside[turn * share : (turn + 1) * share]:
                work()
            if turn < len(some):
                apply(dot_nn, direction, across, some[turn])
            if 0 <= turn - 1 < len(some):
                for pair in some[turn - 1]:
                    blend(pair)
            if folded and 0 <= turn - 2:
                apply(dot_nt, imaged, imaged, some[turn - 2])

    def advance(half):
        curvature = patch_sums(partial[half])
        step_size = norm[half] / jnp.where(curvature > 0.0, curvature, 1.0)
        sizes = [step_size[row : row + 1] for row in range(len(members[half]))]
        for size, pair in zip(sizes, members[half]):
            estimate[pair] = estimate[pair] + size * direction[pair]
        return sizes

    def move(half):
        sizes = advance(half)
        for size, pair in zip(sizes, members[half]):
            rest = residual[pair] - size * imaged[pair]
            residual[pair] = rest
            set_partial(pair, jnp.sum(rest * rest, axis=0, keepdims=True))
        norm_now = norm[half]
        norm_next = patch_sums(partial[half])
        ratio = norm_next / jnp.where(norm_now > 0.0, norm_now, 1.0)
        for row, pair in enumerate(members[half]):
            direction[pair] = residual[pair] + ratio[row : row + 1] * direction[pair]
        norm[half] = norm_next

    def number_slots():
        for index in range(send.shape[0]):
            counts[index] = 0
        for patch in range(patches):
            target = dest[patch]
            slot = counts[target]
            counts[target] = slot + 1
            slots[patch] = slot

    upper_rows = (fibres + 1) // 2
    lane_f = lax.broadcasted_iota(jnp.int32, (padded_f, LANES), 1)
    at_wave = lax.rem(lane_f, HALF) == waves
    unit = jnp.where(at_wave, 1.0, 0.0)

    def hand_over(pair):
        spectra = estimate[pair]
        weighted = (spectra + unit) * (weight_lanes[2 * pair] + weight_lanes[2 * pair + 1])
        for half in range(2):
            value = pltpu.roll(weighted, HALF, 1) if half else weighted
            numer[pl.ds(2 * pair + half, fibres, stride=padded_p), :] = value[:fibres]
        size = jnp.abs(spectra)
        first = jnp.max(jnp.where(lane_f < HALF, size, 0.0), axis=1, keepdims=True)
        second = jnp.max(jnp.where(lane_f < HALF, 0.0, size), axis=1, keepdims=True)
        largest = jnp.where(lane_f < HALF, first, second)
        power = jnp.floor(jnp.log2(jnp.maximum(largest, TINY))) + 1.0
        coded = jnp.clip(jnp.round(spectra * jnp.exp2(CODE_BITS - power)), -CODE_TOP, CODE_TOP)
        coded = jnp.where(at_wave, power, coded)
        turned = pltpu.roll(coded, HALF, 1)
        for half in range(2):
            here = turned if half else coded
            away = coded if half else turned
            compact = jnp.where(
                lane_f[:upper_rows] < HALF,
                here[:upper_rows],
                jnp.concatenate(
                    [away[upper_rows:fibres], away[: 2 * upper_rows - fibres]], axis=0
                ),
            )
            rows = pl.ds(slots[2 * pair + half] * upper_rows, upper_rows)
            packed[dest[2 * pair + half], rows, :] = compact

    begin(0)
    for pair in members[0]:
        build(pair)
    begin(1)
    image(0, beside=[functools.partial(build, pair) for pair in members[1]])
    image(1)
    move(0)
    for _ in range(ITERS - 2):
        image(0)
        move(1)
        image(1)
        move(0)
    number_slots()
    image(0, folded=False)
    move(1)
    advance(0)
    image(1, folded=False, beside=[functools.partial(hand_over, pair) for pair in members[0]])
    advance(1)
    for pair in members[1]:
        hand_over(pair)
    for index in range(send.shape[0]):
        send[index] = packed[index].astype(jnp.int32).astype(jnp.int16)


def finish_kernel(capacity, received, numer, others, spectra_ext, coadd):
    fibres, patches, waves = coadd.shape
    padded_p = up(patches, SUB)
    for f in range(fibres):
        rows = slice(f * padded_p, (f + 1) * padded_p)
        total = numer[rows, :]
        for index in range(others.shape[0]):
            total = total + others[index, rows, :]
        total = total[:patches]
        coadd[f] = total[:, :waves] / total[:, waves : waves + 1]
    upper_rows = (fibres + 1) // 2
    lower_half = lax.broadcasted_iota(jnp.int32, received.shape[1:], 1) < HALF
    for source in range(received.shape[0]):
        coded = received[source].astype(jnp.int32).astype(F32)
        power = jnp.where(
            lower_half, coded[:, waves : waves + 1], coded[:, HALF + waves : HALF + waves + 1]
        )
        value = coded * jnp.exp2(power - CODE_BITS)
        turned = pltpu.roll(value, HALF, 1)
        for slot in range(capacity):
            entry = source * capacity + slot
            at = slot * upper_rows
            spectra_ext[entry, 0:upper_rows, 0, :] = value[at : at + upper_rows, :waves]
            at_end = at + fibres - upper_rows
            spectra_ext[entry, upper_rows:fibres, 0, :] = turned[at:at_end, :waves]


def vmem(count=1):
    return [pl.BlockSpec(memory_space=pltpu.VMEM)] * count


def hbm(count=1):
    return [pl.BlockSpec(memory_space=pltpu.HBM)] * count


def prepare(exposure, row_prof, col_prof, row_off, col_off, weight):
    patches = row_prof.shape[0]
    fibres = col_prof.shape[0]
    _, band, columns = exposure.shape
    padded_f = up(fibres, SUB)
    padded_p = up(patches, SUB)
    rows = SUB * len(block_tiles(fibres))

    def made(*shape):
        return jax.ShapeDtypeStruct((patches,) + shape, BF16)

    return list(
        pl.pallas_call(
        prepare_kernel,
        out_shape=(
            made(rows, 2 * PC),
            made(PR, PC),
            made(PR, PC),
            made(PR, PC),
            made(padded_f, PC),
            made(HALF, LANES),
            jax.ShapeDtypeStruct((patches, padded_f, LANES), F32),
        ),
        in_specs=hbm(2) + vmem(4),
        out_specs=tuple(vmem(7)),
        scratch_shapes=[
            pltpu.SMEM(row_off.shape, row_off.dtype),
            pltpu.SMEM(col_off.shape, col_off.dtype),
            pltpu.VMEM((columns // LANES + 1, band, LANES), F32),
            pltpu.VMEM((columns // LANES + 1, band, LANES), F32),
            pltpu.VMEM((PC // LANES, fibres * padded_p, LANES), F32),
            pltpu.VMEM((padded_f, PC), F32),
            pltpu.VMEM((HALF, LANES), F32),
            pltpu.SemaphoreType.DMA((2,)),
        ],
        cost_estimate=pl.CostEstimate(
            flops=patches * rows * PC * 8, bytes_accessed=16 * 1024 * 1024, transcendentals=0
        ),
        compiler_params=pltpu.CompilerParams(vmem_limit_bytes=24 * 1024 * 1024),
    )(row_off, col_off, exposure, row_prof, col_prof, weight)
    )


def solve(halos, prepared, fibres, waves, row_off, col_off, dest, group):
    patches = dest.shape[0]
    columns = halos[0].shape[2]
    capacity = (patches + group - 1) // group
    pairs = patches // 2
    main = fibres // SUB * SUB
    padded_f = up(fibres, SUB)
    code_rows = up(capacity * ((fibres + 1) // 2), SUB)
    vectors = pltpu.VMEM((pairs, padded_f, LANES), F32)
    sums = pltpu.VMEM((2, up(pairs - pairs // 4 * 2, SUB), LANES), F32)
    tops = pltpu.VMEM((patches, 2 * HALO, PC), BF16)
    halo_band = pltpu.VMEM((columns // LANES + 1, 2 * HALO, LANES), F32)
    return pl.pallas_call(
        functools.partial(solve_kernel, fibres, waves),
        out_shape=(
            jax.ShapeDtypeStruct((group, code_rows, LANES), jnp.int16),
            jax.ShapeDtypeStruct((fibres * up(patches, SUB), LANES), F32),
        ),
        in_specs=hbm(3) + vmem(10),
        out_specs=tuple(vmem(2)),
        scratch_shapes=[
            pltpu.SMEM(row_off.shape, row_off.dtype),
            pltpu.SMEM(col_off.shape, col_off.dtype),
            pltpu.SMEM(dest.shape, dest.dtype),
            halo_band,
            halo_band,
            tops,
            tops,
            tops,
            pltpu.VMEM((pairs, fibres * main, LANES), F32),
            pltpu.VMEM((pairs, max(fibres - main, 1), padded_f, LANES), F32),
            vectors,
            vectors,
            vectors,
            vectors,
            vectors,
            sums,
            sums,
            pltpu.VMEM((group, code_rows, LANES), F32),
            pltpu.SMEM((group,), jnp.int32),
            pltpu.SMEM((patches,), jnp.int32),
            pltpu.SemaphoreType.DMA((3,)),
        ],
        compiler_params=pltpu.CompilerParams(vmem_limit_bytes=24 * 1024 * 1024),
    )(row_off, col_off, dest, *halos, *prepared)


def finish(received, numer, others, capacity, patches, fibres, waves):
    entries = received.shape[0] * capacity
    return pl.pallas_call(
        functools.partial(finish_kernel, capacity),
        out_shape=(
            jax.ShapeDtypeStruct((entries, fibres, 1, waves), F32),
            jax.ShapeDtypeStruct((fibres, patches, waves), F32),
        ),
        in_specs=vmem(3),
        out_specs=tuple(vmem(2)),
        compiler_params=pltpu.CompilerParams(vmem_limit_bytes=16 * 1024 * 1024),
    )(received, numer, others)


def edge_kernel(exposure, two, one):
    rank = lax.axis_index("section") * lax.axis_size("patch") + lax.axis_index("patch")
    even = lax.rem(rank, 2) == 0
    band = exposure.shape[1]
    for channel in range(exposure.shape[0]):
        top = exposure[channel, 0:HALO, :].astype(F32)
        bottom = exposure[channel, band - HALO : band, :].astype(F32)
        one[channel] = jnp.where(even, bottom, top).astype(BF16)
        two[channel] = jnp.where(even, top, bottom).astype(BF16)


def edges(exposure):
    channels, _, columns = exposure.shape
    return pl.pallas_call(
        edge_kernel,
        out_shape=(jax.ShapeDtypeStruct((channels, HALO, columns), BF16),) * 2,
        in_specs=vmem(1),
        out_specs=tuple(vmem(2)),
        cost_estimate=pl.CostEstimate(
            flops=EDGE_FLOPS, bytes_accessed=EDGE_BYTES, transcendentals=0
        ),
        compiler_params=pltpu.CompilerParams(vmem_limit_bytes=8 * 1024 * 1024),
    )(exposure)


def neighbours(block):
    axes = ("section", "patch")
    count = lax.axis_size(axes)
    group = lax.axis_size("patch")
    two, one = edges(block)

    def exchange(value, firsts):
        pairs = [(i, i + 1) for i in firsts if i + 1 < count]
        return lax.ppermute(value, axes, pairs + [(b, a) for a, b in pairs])

    odd = range(1, count, 2)
    far = [i for i in odd if (i + 1) % group == 0]
    near = [i for i in odd if (i + 1) % group]
    return [exchange(one, range(0, count, 2)), exchange(two, near), exchange(two, far)]


def local(exposure, row_prof, col_prof, row_off, col_off, dest, fibre_weight):
    group = lax.axis_size("patch")
    frames = lax.axis_size("frame")
    patches = dest.shape[1]
    fibres, waves = col_prof.shape[2], row_prof.shape[2]
    capacity = (patches + group - 1) // group
    halos = neighbours(exposure[0])
    prepared = prepare(
        exposure[0],
        row_prof[0],
        col_prof[0].transpose(1, 0, 2),
        row_off[0],
        col_off[0],
        fibre_weight[0][:, None, :],
    )
    prepared[5] = prepared[5].reshape(patches // 2, LANES, LANES)
    send, numer = solve(halos, prepared, fibres, waves, row_off[0], col_off[0], dest[0], group)
    received = lax.all_to_all(send, "patch", split_axis=0, concat_axis=0, tiled=True)
    others = jnp.stack(
        [
            lax.ppermute(numer, "frame", [(i, (i + hop) % frames) for i in range(frames)])
            for hop in range(1, frames)
        ]
    )
    spectra_ext, coadd = finish(received, numer, others, capacity, patches, fibres, waves)
    return spectra_ext.transpose(2, 0, 3, 1), coadd.transpose(1, 2, 0)


def solution(mesh):
    in_specs = (
        P("frame", None, ("section", "patch"), None),
        P("frame", ("section", "patch"), None, None),
        P("frame", ("section", "patch"), None, None),
        P("frame", ("section", "patch")),
        P("frame", ("section", "patch")),
        P("frame", ("section", "patch")),
        P("frame", ("section", "patch"), None),
    )
    out_specs = (P("frame", ("section", "patch"), None, None), P(("section", "patch"), None, None))
    return jax.shard_map(local, mesh=mesh, in_specs=in_specs, out_specs=out_specs, check_vma=False)
```
